32 devices in a mesh: seq: 8 (over z, x), stream: 4 (over y, core).
Axes of the slice: x: 2, y: 2, z: 4, core: 2. Of those that a mesh axis runs over, the one named last changes fastest.
Arguments:
- inputs: bfloat16 [8, 1024, 2048], P('stream', 'seq'), may hold values from -6 to 6
- start_state: float32 [8, 2048], P('stream'), may hold values from -6 to 6
- lengths: int32 [8], P('stream'), may hold values from 512 to 1024, as said below
- weights: bfloat16 [2048, 6144], P('seq', 'stream'), may hold values from -0.125 to 0.125
- peep_forget: float32 [2048], replicated, may hold values from -1 to 1
- peep_reset: float32 [2048], replicated, may hold values from -1 to 1
- bias_forget: float32 [2048], replicated, may hold values from 2 to 7
- bias_reset: float32 [2048], replicated, may hold values from -1.5 to 1.5
- norm_gain: float32 [2048], replicated, may hold values from 0.5 to 1.5
- norm_bias: float32 [2048], replicated, may hold values from -3 to 3
- out_grad: bfloat16 [8, 1024, 2048], P('stream', 'seq'), may hold values from -6 to 6
Outputs:
- outputs: bfloat16 [8, 1024, 2048], P('stream', 'seq')
- final_state: float32 [8, 2048], P('stream', 'seq')
- input_grad: bfloat16 [8, 1024, 2048], P('stream', 'seq')
- weight_grad: float32 [2048, 6144], P('seq', 'stream')
- peep_forget_grad: float32 [2048], replicated
- peep_reset_grad: float32 [2048], replicated
- bias_forget_grad: float32 [2048], replicated
- bias_reset_grad: float32 [2048], replicated
- norm_gain_grad: float32 [2048], replicated
- norm_bias_grad: float32 [2048], replicated
The draws below stay inside these ranges and needn't reach their ends.
Inputs may be any that keep to these rules, and one draw needn't show every extreme that they name: `lengths`: among the 2 sequences of each index of stream, one drawn from the seed has length 1024.
All inputs are finite; a program needn't handle non-finite values.
Results may differ from the reference program's by a relative error of at most 0.0079.
Values may be sent and summed in bfloat16 or wider, within the bound.
No kernel may reach another device: no remote copies, remote signals or barrier semaphores. Data moves between devices by JAX's collectives and lax.ppermute only.
A program may use at most 128 MiB of HBM per device.

```python
import jax
import jax.numpy as jnp
from jax import lax

D = 2048
BATCH_DEV = 2
NS = 8
LEN = 1024


def draw_lengths(key, part):
    key = jax.random.fold_in(key, 11)
    key_lengths, key_pick = jax.random.split(key)
    groups = NS // BATCH_DEV
    drawn_lengths = jax.random.randint(key_lengths, (groups, BATCH_DEV), LEN // 2, LEN + 1)
    chosen = jax.random.randint(key_pick, (groups, 1), 0, BATCH_DEV)
    slot_index = jnp.arange(BATCH_DEV, dtype=jnp.int32)[None, :]
    filled = jnp.where(slot_index == chosen, LEN, drawn_lengths)
    return filled.reshape(NS).astype(jnp.int32)


def level_of(own_key, dims, pieces, smallest, largest):
    loudness = 1.0
    for position, shards_of in pieces:
        steps = jax.random.uniform(jax.random.fold_in(jax.random.fold_in(own_key, 6), position), (shards_of,), jnp.float32, smallest / len(pieces), largest / len(pieces))
        loudness = loudness * jnp.repeat(jnp.exp(steps), dims[position] // shards_of).reshape((-1,) + (1,) * (len(dims) - 1 - position))
    return loudness


def centred(rng, dims, width, limit, shards=(), held_as=jnp.bfloat16):
    values = width * jax.random.normal(rng, dims, jnp.float32)
    if shards:
        values = values * level_of(rng, dims, shards, -0.22, 0.18)
    return jnp.clip(values, -limit, limit).astype(held_as)


def setup_inputs(seed: int = 0) -> dict:
    seeds = jax.random.split(jax.random.key(seed), 12)
    return {
        "inputs": centred(seeds[0], (NS, LEN, D), 1.0, 6.0, ((0, 4), (1, 8))),
        "start_state": centred(seeds[1], (NS, D), 1.0, 6.0, ((0, 4),), jnp.float32),
        "lengths": draw_lengths(jax.random.fold_in(seeds[11], 71), 0),
        "weights": centred(seeds[3], (D, 3 * D), D ** -0.5, 0.125, ((0, 8), (1, 4))),
        "peep_forget": jnp.clip(jax.random.uniform(seeds[4], (D,), jnp.float32, -1.0, 1.0), -1.0, 1.0),
        "peep_reset": jnp.clip(jax.random.uniform(seeds[5], (D,), jnp.float32, -1.0, 1.0), -1.0, 1.0),
        "bias_forget": jnp.clip(jax.random.uniform(seeds[6], (D,), jnp.float32, 2.0, 7.0), 2.0, 7.0),
        "bias_reset": jnp.clip(jax.random.uniform(seeds[7], (D,), jnp.float32, -1.5, 1.5), -1.5, 1.5),
        "norm_gain": jnp.clip(1.0 + 0.1 * jax.random.normal(seeds[8], (D,), jnp.float32), 0.5, 1.5),
        "norm_bias": centred(seeds[9], (D,), 0.5, 3.0, (), jnp.float32),
        "out_grad": centred(seeds[10], (NS, LEN, D), 1.0, 6.0, ((0, 4), (1, 8))),
    }


epsilon = 1e-05

@jax.custom_vjp
def low(v):
    return lax.optimization_barrier(v.astype(jnp.bfloat16)).astype(jnp.float32)

@jax.custom_vjp
def low_back(v):
    return v

def low_keep(v):
    return (low(v), None)

def low_pass(kept, grad):
    return (grad,)

def back_keep(v):
    return (v, None)

def back_low(kept, grad):
    return (low(grad),)
low.defvjp(low_keep, low_pass)
low_back.defvjp(back_keep, back_low)

def advance(state, pair_item):
    fresh = pair_item[0] * state + pair_item[1]
    return (fresh, fresh)

def sequence_layer(source, start, length, weight_all, forget_peep, reset_peep, forget_bias, reset_bias, gain_all, shift_all):
    model_width = source.shape[1]
    steps_total = source.shape[0]
    centered = source - lax.optimization_barrier(jnp.mean(source, axis=1, keepdims=True))
    variance = lax.optimization_barrier(jnp.mean(centered * centered, axis=1, keepdims=True))
    scaled = centered * lax.rsqrt(variance + epsilon)
    normed = low(scaled * gain_all + shift_all)
    product = jnp.dot(normed, weight_all, precision=lax.Precision.HIGHEST, preferred_element_type=jnp.float32)
    projected = low(low_back(product))
    candidate = projected[:, :model_width]
    forget_pre = projected[:, model_width:2 * model_width]
    reset_pre = projected[:, 2 * model_width:]
    previous = jnp.concatenate([start[None, :], candidate[:-1]], axis=0)
    forget = jax.nn.sigmoid(forget_pre + forget_peep * previous + forget_bias)
    reset = jax.nn.sigmoid(reset_pre + reset_peep * previous + reset_bias)
    live = (jnp.arange(steps_total, dtype=jnp.int32) < length)[:, None]
    decay = jnp.where(live, forget, 1.0)
    inject = jnp.where(live, (1.0 - forget) * candidate, 0.0)
    final, states = lax.scan(advance, start, (decay, inject))
    result = jnp.where(live, reset * states + (1.0 - reset) * source, source)
    return (result, final)

def reference(inputs, start_state, lengths, weights, peep_forget, peep_reset, bias_forget, bias_reset, norm_gain, norm_bias, out_grad):

    def layer(source_all, weight_all, forget_peep, reset_peep, forget_bias, reset_bias, gain_all, shift_all):

        def single(item_tuple):
            return jax.checkpoint(sequence_layer)(item_tuple[0], item_tuple[1], item_tuple[2], weight_all, forget_peep, reset_peep, forget_bias, reset_bias, gain_all, shift_all)
        result, final = lax.map(single, (source_all, start_state, lengths))
        return (result, final)
    result, pullback, final = jax.vjp(layer, inputs.astype(jnp.float32), weights.astype(jnp.float32), peep_forget, peep_reset, bias_forget, bias_reset, norm_gain, norm_bias, has_aux=True)
    grads = pullback(out_grad.astype(jnp.float32))
    return (result.astype(jnp.bfloat16), final, grads[0].astype(jnp.bfloat16), grads[1], grads[2], grads[3], grads[4], grads[5], grads[6], grads[7])
```

```python
import functools

import jax
import jax.numpy as jnp
import numpy as np
from jax import lax
from jax.experimental import pallas as pl
from jax.experimental.pallas import tpu as pltpu
from jax.sharding import PartitionSpec as P

epsilon = 1e-05
f32 = jnp.float32
bf16 = jnp.bfloat16
GROUPS = 2
PAD = 8
VMEM_BYTES = 56 * 1024 * 1024


def vmem_spec():
    return pl.BlockSpec(memory_space=pltpu.VMEM)


def smem_spec():
    return pl.BlockSpec(memory_space=pltpu.SMEM)


def call(kernel, out_shape, operands, scratch=(), scalars=0, flops=0, touched=0):
    specs = [smem_spec()] * scalars + [vmem_spec()] * (len(operands) - scalars)
    return pl.pallas_call(
        kernel,
        out_shape=out_shape,
        in_specs=specs,
        out_specs=jax.tree.map(lambda _: vmem_spec(), out_shape),
        scratch_shapes=list(scratch),
        compiler_params=pltpu.CompilerParams(vmem_limit_bytes=VMEM_BYTES),
        cost_estimate=pl.CostEstimate(flops=flops, bytes_accessed=touched, transcendentals=0),
    )(*operands)


def ring_order(count):
    if count == 8:
        return [0, 2, 4, 6, 7, 5, 3, 1]
    return list(range(count))


def along_ring(value, steps):
    order = ring_order(lax.axis_size("seq"))
    count = len(order)
    return lax.ppermute(value, "seq", [(order[i], order[(i + steps) % count]) for i in range(count)])


def swapped(value, axis, bit):
    return lax.ppermute(value, axis, [(i, i ^ bit) for i in range(lax.axis_size(axis))])


def norm_kernel(count, rows, *refs):
    pieces = refs[:count]
    gain, bias, normed, means, scales = refs[count:]
    step = 32
    gain_row, bias_row = gain[...], bias[...]
    for k in range(count):

        def body(i, _, k=k):
            at = pl.multiple_of(i * step, step)
            x = pieces[k][pl.ds(at, step), :].astype(f32)
            mean = jnp.mean(x, axis=1, keepdims=True)
            centered = x - mean
            scale = lax.rsqrt(jnp.mean(centered * centered, axis=1, keepdims=True) + epsilon)
            out = (centered * scale * gain_row + bias_row).astype(bf16)
            to = pl.multiple_of(k * rows + i * step, step)
            normed[pl.ds(to, step), :] = out
            means[pl.ds(to, step), :] = jnp.broadcast_to(mean, (step, 128))
            scales[pl.ds(to, step), :] = jnp.broadcast_to(scale, (step, 128))
            return 0

        lax.fori_loop(0, rows // step, body, 0)


def strided(ref, row, seqs, stride):
    tiles = [ref[lane, pl.ds(row, seqs, stride=stride), :] for lane in range(ref.shape[0])]
    return jnp.concatenate(tiles, axis=1)


def put_strided(ref, row, seqs, stride, value):
    for lane in range(ref.shape[0]):
        ref[lane, pl.ds(row, seqs, stride=stride), :] = value[:, lane * 128 : (lane + 1) * 128]


def put_rows(ref, row, count, value):
    for lane in range(ref.shape[0]):
        ref[lane, pl.ds(row, count), :] = value[:, lane * 128 : (lane + 1) * 128]


def get_rows(ref, row, count):
    return jnp.concatenate([ref[lane, pl.ds(row, count), :] for lane in range(ref.shape[0])], axis=1)


def first_kernel(dims, part, sources, place, normed, halo, start, lens, vecs, *refs):
    seqs, span, width, slots, blocks, depth, split = dims
    stride = span + PAD
    w = refs[:blocks + (1 if split else 0)]
    g_in, x_in = refs[len(w) : len(w) + slots], refs[len(w) + slots : len(w) + 2 * slots]
    cand, forg, rese, maps, planes, gs, xs = refs[len(w) + 2 * slots :]
    per = seqs // slots
    lane0 = part * width
    for k in range(slots):
        for j in range(per):
            to = (k * per + j) * stride + PAD
            put_rows(gs, to, span, g_in[k][j, :, lane0 : lane0 + width].astype(f32))
            put_rows(xs, to, span, x_in[k][j, :, lane0 : lane0 + width].astype(f32))

    def block(b):
        if split and b == blocks - 1:
            return jnp.concatenate([w[b][...], w[b + 1][...]], axis=0)
        return w[b][...]

    rows = per * span
    for k in range(slots):
        total = None
        for b in range(blocks):
            at = pl.multiple_of(sources[b] * depth, depth)
            term = jnp.dot(
                normed[k * rows : (k + 1) * rows, pl.ds(at, depth)],
                block(b),
                preferred_element_type=f32,
            )
            total = term if total is None else total + term
        total = total.astype(bf16).astype(f32)
        for j in range(per):
            to = (k * per + j) * stride + PAD
            for ref, gate in ((cand, 0), (forg, 1), (rese, 2)):
                here = total[j * span : (j + 1) * span, gate * width : (gate + 1) * width]
                put_rows(ref, to, span, here)
    last = None
    for b in range(blocks):
        at = pl.multiple_of(sources[b] * depth, depth)
        term = jnp.dot(halo[:, pl.ds(at, depth)], block(b)[:, :width], preferred_element_type=f32)
        last = term if last is None else last + term
    last = last.astype(bf16).astype(f32)[:seqs]
    before = jnp.where(place[1] == 0, start[...], last)
    put_strided(cand, PAD - 1, seqs, stride, before)
    peep_f, peep_r, bias_f, bias_r = (vecs[i : i + 1, :] for i in range(4))
    ends = lens[...]
    base = place[0]

    def turn(t, carry):
        previous, decays, injects, handed = carry
        row = t + PAD
        c = strided(cand, row, seqs, stride)
        f = jax.nn.sigmoid(strided(forg, row, seqs, stride) + peep_f * previous + bias_f)
        r = jax.nn.sigmoid(strided(rese, row, seqs, stride) + peep_r * previous + bias_r)
        put_strided(forg, row, seqs, stride, f)
        put_strided(rese, row, seqs, stride, r)
        live = base + t < ends
        d = jnp.where(live, f, 1.0)
        inject = jnp.where(live, (1.0 - f) * c, 0.0)
        pulled = jnp.where(live, r * strided(gs, row, seqs, stride), 0.0)
        decays = decays * d
        return c, decays, d * injects + inject, handed + decays * pulled

    one, zero = jnp.ones((seqs, width), f32), jnp.zeros((seqs, width), f32)
    _, decays, injects, handed = lax.fori_loop(0, span, turn, (before, one, zero, zero), unroll=4)
    maps[0], maps[1], maps[2] = decays, injects, handed
    c, f, r, g, x = (strided(ref, PAD, seqs, stride) for ref in (cand, forg, rese, gs, xs))
    live = base < ends
    d = jnp.where(live, f, 1.0)
    inject = jnp.where(live, (1.0 - f) * c, 0.0)
    via_adjoint = jnp.where(live, (1.0 - f) * peep_f, 0.0)
    via_state = jnp.where(live, r * (1.0 - r) * g * peep_r, 0.0)
    planes[0], planes[1] = via_adjoint, via_adjoint * c
    planes[2], planes[3] = via_state * d, via_state * (inject - x)


def second_kernel(dims, part, place, lens, vecs, links, cand, forg, rese, *refs):
    seqs, span, width, slots = dims
    stride = span + PAD
    g_in, x_in = refs[:slots], refs[slots : 2 * slots]
    grads, moved = refs[2 * slots], refs[2 * slots + 1 : 3 * slots + 1]
    final, sums = refs[3 * slots + 1 : 3 * slots + 3]
    gs, xs, states, outs, gcs, fts, rts = refs[3 * slots + 3 :]
    per = seqs // slots
    lane0 = part * width
    for k in range(slots):
        for j in range(per):
            to = (k * per + j) * stride + PAD
            put_rows(gs, to, span, g_in[k][j, :, lane0 : lane0 + width].astype(f32))
            put_rows(xs, to, span, x_in[k][j, :, lane0 : lane0 + width].astype(f32))
    peep_f, peep_r = vecs[0:1, :], vecs[1:2, :]
    ends = lens[...]
    base = place[0]
    begin, after = links[0], links[1]
    put_strided(states, PAD - 1, seqs, stride, begin)

    def forward(t, state):
        row = t + PAD
        c, f, r, x = (strided(ref, row, seqs, stride) for ref in (cand, forg, rese, xs))
        live = base + t < ends
        state = jnp.where(live, f * state + (1.0 - f) * c, state)
        put_strided(states, row, seqs, stride, state)
        put_strided(outs, row, seqs, stride, jnp.where(live, r * state + (1.0 - r) * x, x))
        return state

    end = lax.fori_loop(0, span, forward, begin, unroll=4)
    final[...] = links[2] * end + links[3]
    upcoming = end * (links[4] * after + links[6]) - links[5] * after + links[7]

    def backward(i, carry):
        reached, upcoming, pf, pr, bf, br = carry
        row = span - 1 - i + PAD
        c, f, r, x, g = (strided(ref, row, seqs, stride) for ref in (cand, forg, rese, xs, gs))
        state = strided(states, row, seqs, stride)
        prior = strided(states, row - 1, seqs, stride)
        previous = strided(cand, row - 1, seqs, stride)
        live = base + (span - 1 - i) < ends
        zero = jnp.zeros_like(f)
        adjoint = jnp.where(live, r * g, 0.0) + reached
        kept = jnp.where(live, (1.0 - f) * adjoint, zero)
        ft = f * kept * (prior - c)
        rt = jnp.where(live, r * (1.0 - r) * g * (state - x), zero)
        put_strided(gcs, row, seqs, stride, kept + upcoming)
        put_strided(fts, row, seqs, stride, ft)
        put_strided(rts, row, seqs, stride, rt)
        put_strided(gs, row, seqs, stride, jnp.where(live, (1.0 - r) * g, g))
        reached = jnp.where(live, f * adjoint, adjoint)
        return (
            reached,
            ft * peep_f + rt * peep_r,
            pf + ft * previous,
            pr + rt * previous,
            bf + ft,
            br + rt,
        )

    zero = jnp.zeros((seqs, width), f32)
    done = lax.fori_loop(0, span, backward, (after, upcoming, zero, zero, zero, zero), unroll=4)
    sums[...] = jnp.zeros_like(sums)
    for i in range(4):
        sums[i : i + 1, :] = jnp.sum(done[2 + i], axis=0, keepdims=True)
    for n in range(seqs):
        at = n * stride + PAD
        for gate, ref in enumerate((gcs, fts, rts)):
            lanes = slice(gate * width, (gate + 1) * width)
            grads[n * span : (n + 1) * span, lanes] = get_rows(ref, at, span).astype(bf16)
        k, j = n // per, n % per
        moved[k][0, j] = get_rows(outs, at, span).astype(bf16)
        moved[k][1, j] = get_rows(gs, at, span).astype(bf16)


def token_kernel(dims, sources, *refs):
    slots, blocks, depth, rows, groups, split = dims
    n_w = blocks + (1 if split else 0)
    grads = refs[:groups]
    w = [refs[groups + a * n_w : groups + (a + 1) * n_w] for a in range(groups)]
    at0 = groups + groups * n_w
    pieces = refs[at0 : at0 + slots]
    means, scales = refs[at0 + slots : at0 + slots + 2]
    own = refs[at0 + slots + 2]
    others = refs[at0 + slots + 3 : at0 + 2 * slots + 2]
    sums = refs[at0 + 2 * slots + 2]

    def block(a, b):
        if split and b == blocks - 1:
            return jnp.concatenate([w[a][b][...], w[a][b + 1][...]], axis=0)
        return w[a][b][...]

    sums[...] = jnp.zeros_like(sums)
    for b in range(blocks):
        at = pl.multiple_of(sources[b] * depth, depth)
        lanes = pl.ds(at, depth)
        gain_sum, bias_sum = jnp.zeros((8, depth), f32), jnp.zeros((8, depth), f32)
        weights = [block(a, b) for a in range(groups)]
        for k in range(slots):
            here = pl.ds(k * rows, rows)
            total = None
            for a in range(groups):
                term = lax.dot_general(
                    grads[a][here, :],
                    weights[a],
                    (((1,), (1,)), ((), ())),
                    preferred_element_type=f32,
                )
                total = term if total is None else total + term
            copies = depth // 128
            mean = jnp.concatenate([means[here, :]] * copies, axis=1)
            scale = jnp.concatenate([scales[here, :]] * copies, axis=1)
            scaled = (pieces[k][:, lanes].astype(f32) - mean) * scale
            gain_sum += jnp.sum((total * scaled).reshape(rows // 8, 8, depth), axis=0)
            bias_sum += jnp.sum(total.reshape(rows // 8, 8, depth), axis=0)
            if k == 0:
                own[:, lanes] = total
            else:
                others[k - 1][:, lanes] = total.astype(bf16)
        sums[0:1, lanes] = jnp.sum(gain_sum, axis=0, keepdims=True)
        sums[1:2, lanes] = jnp.sum(bias_sum, axis=0, keepdims=True)


def pick(table, index):
    return jnp.take(jnp.asarray(np.asarray(table), jnp.int32), index, axis=0)


def chosen(options, index):
    result = options[0]
    for i in range(1, len(options)):
        result = jnp.where(index == i, options[i], result)
    return result


def gates_of_units(weights, width, lane0, lanes):
    count, here = lax.axis_size("stream"), lax.axis_index("stream")
    if count == 4:
        pieces = [weights[:, s * width + lane0 : s * width + lane0 + lanes] for s in range(3)]
        even = here % 2 == 0
        own = jnp.where(even, pieces[0], pieces[2])
        near = swapped(pieces[1], "stream", 1)
        far = swapped(jnp.where(even, pieces[2], pieces[0]), "stream", 2)
        got = [own, near, far]
        order = ((0, 1, 2), (1, 0, 2), (2, 0, 1), (2, 1, 0))
        return jnp.concatenate(
            [chosen([got[order[d][gate]] for d in range(4)], here) for gate in range(3)], axis=1
        )
    everything = lax.all_gather(weights, "stream", axis=1, tiled=True)
    model = count * width
    return jnp.concatenate(
        [
            lax.dynamic_slice_in_dim(everything, gate * model + here * width + lane0, lanes, 1)
            for gate in range(3)
        ],
        axis=1,
    )


def columns_as_stored(gates):
    count, here = lax.axis_size("stream"), lax.axis_index("stream")
    if count == 4:
        own = chosen([gates[0], gates[1], gates[1], gates[2]], here)
        near = swapped(
            chosen([gates[1], gates[0], gates[2], gates[1]], here).astype(bf16), "stream", 1
        ).astype(f32)
        far = swapped(
            chosen([gates[2], gates[2], gates[0], gates[0]], here).astype(bf16), "stream", 2
        ).astype(f32)
        even = here % 2 == 0
        return [jnp.where(even, own, far), near, jnp.where(even, far, own)]
    everything = lax.all_gather(jnp.stack(gates).astype(bf16), "stream", axis=1).astype(f32)
    flat = everything.reshape((3 * count,) + gates[0].shape)
    return [lax.dynamic_index_in_dim(flat, 3 * here + s, 0, keepdims=False) for s in range(3)]


def gathered_blocks(block):
    count = lax.axis_size("seq")
    half = block.shape[0] // 2
    up = down = block
    blocks = [block]
    for _ in range(count // 2 - 1):
        up, down = along_ring(up, 1), along_ring(down, -1)
        blocks += [up, down]
    blocks += [along_ring(up[:half], 1), along_ring(down[half:], -1)]
    return blocks


def exchanged_maps(maps):
    count, here = lax.axis_size("seq"), lax.axis_index("seq")
    decay, inject, handed = maps[0], maps[1], maps[2]
    one, zero = jnp.ones_like(decay), jnp.zeros_like(decay)
    before = (one, zero)
    after = (one, zero, zero)
    bit = 1
    while bit < count:
        other = swapped(jnp.stack([decay, inject, handed]), "seq", bit)
        theirs = (other[0], other[1], other[2])
        first = (here & bit) == 0
        before_new = (theirs[0] * before[0], before[0] * theirs[1] + before[1])
        after_new = (
            after[0] * theirs[0],
            theirs[0] * after[1] + theirs[1],
            after[2] + after[0] * theirs[2],
        )
        before = tuple(jnp.where(first, a, b) for a, b in zip(before, before_new))
        after = tuple(jnp.where(first, b, a) for a, b in zip(after, after_new))
        together = decay * theirs[0]
        inject_new = jnp.where(
            first, theirs[0] * inject + theirs[1], decay * theirs[1] + inject
        )
        handed_new = jnp.where(
            first, handed + decay * theirs[2], theirs[2] + theirs[0] * handed
        )
        decay, inject, handed = together, inject_new, handed_new
        bit *= 2
    return before, after


def local(
    inputs,
    start_state,
    lengths,
    weights,
    peep_forget,
    peep_reset,
    bias_forget,
    bias_reset,
    norm_gain,
    norm_bias,
    out_grad,
):
    per, span, model = inputs.shape
    n_seq, slots = lax.axis_size("seq"), lax.axis_size("stream")
    at_seq, at_stream = lax.axis_index("seq"), lax.axis_index("stream")
    seqs = per * slots
    units = model // slots
    width = units // GROUPS
    depth = model // n_seq
    rows = per * span
    tokens = seqs * span
    order = ring_order(n_seq)
    spot = pick(np.argsort(order), at_seq)
    far = n_seq // 2
    steps = [0]
    for k in range(1, far):
        steps += [-k, k]
    steps.append(far)
    sources = pick(order, (spot + jnp.asarray(steps, jnp.int32)) % n_seq)
    place = jnp.stack([at_seq * span, at_seq]).astype(jnp.int32)

    bits = []
    bit = slots // 2
    while bit:
        bits.append(bit)
        bit //= 2

    def everyone(own):
        pieces = {0: own}
        for bit in bits:
            for k in list(pieces):
                pieces[k ^ bit] = swapped(pieces[k], "stream", bit)
        return [pieces[k] for k in range(slots)]

    def owner_units(array, k, lanes=units, lane0=0):
        return lax.dynamic_slice_in_dim(
            array, (at_stream ^ k) * units + lane0, lanes, array.ndim - 1
        )

    ordered_weights = [
        gates_of_units(weights, units, a * width, width) for a in range(GROUPS)
    ]
    blocks = [gathered_blocks(block) for block in ordered_weights]

    held_depth, split = depth, True
    if depth % 128:
        places = jnp.stack([sources[b] for b in range(n_seq)] + [sources[n_seq - 1]]) * depth
        places = places.at[n_seq].add(depth // 2)
        held_depth, split = 2 * 128, False
        for a in range(GROUPS):
            whole = jnp.zeros((model, 3 * width), bf16)
            for b, block in enumerate(blocks[a]):
                whole = lax.dynamic_update_slice_in_dim(whole, block, places[b], 0)
            blocks[a] = [whole[i : i + held_depth] for i in range(0, model, held_depth)]
        sources = jnp.arange(model // held_depth, dtype=jnp.int32)
    n_blocks = model // held_depth

    pieces = everyone(inputs.reshape(rows, model))
    ahead = lax.ppermute(
        inputs[:, -1, :], "seq", [(i, i + 1) for i in range(n_seq - 1)]
    )
    halo = jnp.concatenate(everyone(ahead), axis=0)
    halo = jnp.concatenate([halo, jnp.zeros((-seqs % 16, model), bf16)], axis=0)
    small = []
    for k in range(slots):
        message = jnp.concatenate(
            [
                owner_units(start_state, k),
                jnp.broadcast_to(lengths.astype(f32)[:, None], (per, 128)),
            ],
            axis=1,
        )
        small.append(swapped(message, "stream", k) if k else message)
    small = jnp.concatenate(small, axis=0)
    start_units = small[:, :units]
    ends = small[:, units : units + 1].astype(jnp.int32)
    ends = jnp.broadcast_to(ends, (seqs, width))
    grads_in = []
    for k in range(slots):
        message = owner_units(out_grad, k)
        grads_in.append(swapped(message, "stream", k) if k else message)
    sources_in = [
        lax.dynamic_slice_in_dim(piece, at_stream * units, units, 1).reshape(per, span, units)
        for piece in pieces
    ]

    gain_row, bias_row = norm_gain.reshape(1, model), norm_bias.reshape(1, model)
    normed, means, scales = call(
        functools.partial(norm_kernel, slots, rows),
        [
            jax.ShapeDtypeStruct((tokens, model), bf16),
            jax.ShapeDtypeStruct((tokens, 128), f32),
            jax.ShapeDtypeStruct((tokens, 128), f32),
        ],
        [*pieces, gain_row, bias_row],
        flops=tokens * model * 10,
        touched=tokens * model * 4,
    )
    wide = halo.astype(f32)
    centered = wide - jnp.mean(wide, axis=1, keepdims=True)
    spread = lax.rsqrt(jnp.mean(centered * centered, axis=1, keepdims=True) + epsilon)
    halo = (centered * spread * gain_row + bias_row).astype(bf16)

    vectors = jnp.stack([peep_forget, peep_reset, bias_forget, bias_reset])
    vectors = lax.dynamic_slice_in_dim(vectors, at_stream * units, units, 1)
    vectors = jnp.concatenate([vectors, jnp.zeros_like(vectors)], axis=0)

    tall = seqs * (span + PAD)
    field = jax.ShapeDtypeStruct((width // 128, tall, 128), f32)
    space = pltpu.VMEM((width // 128, tall, 128), f32)
    grad_groups, sum_groups, final_groups, moved_groups, parts_groups = [], [], [], [], []
    for a in range(GROUPS):
        vecs = vectors[:, a * width : (a + 1) * width]
        start = start_units[:, a * width : (a + 1) * width]
        cand, forg, rese, maps, planes = call(
            functools.partial(
                first_kernel, (seqs, span, width, slots, n_blocks, held_depth, split), a
            ),
            [
                field,
                field,
                field,
                jax.ShapeDtypeStruct((3, seqs, width), f32),
                jax.ShapeDtypeStruct((4, seqs, width), f32),
            ],
            [sources, place, normed, halo, start, ends, vecs, *blocks[a], *grads_in, *sources_in],
            scratch=[space, space],
            scalars=2,
            flops=2 * tokens * model * 3 * width,
            touched=tokens * model * 2,
        )
        linked = lax.ppermute(planes, "seq", [(i + 1, i) for i in range(n_seq - 1)])
        before, after = exchanged_maps(maps)
        begin = before[0] * start + before[1]
        links = jnp.concatenate(
            [jnp.stack([begin, after[2], after[0], after[1]]), linked], axis=0
        )
        out = call(
            functools.partial(second_kernel, (seqs, span, width, slots), a),
            [
                jax.ShapeDtypeStruct((tokens, 3 * width), bf16),
                *[jax.ShapeDtypeStruct((2, per, span, width), bf16)] * slots,
                jax.ShapeDtypeStruct((seqs, width), f32),
                jax.ShapeDtypeStruct((8, width), f32),
            ],
            [place, ends, vecs, links, cand, forg, rese, *grads_in, *sources_in],
            scratch=[space] * 7,
            scalars=1,
            flops=tokens * width * 60,
            touched=tokens * width * 24,
        )
        grads = out[0]
        grad_groups.append(grads)
        final_groups.append(out[slots + 1])
        sum_groups.append(out[slots + 2][:4])
        moved = [
            swapped(out[1 + k], "stream", k) if k else out[1 + k] for k in range(slots)
        ]
        moved_groups.append(moved)

        def partial(dest, grads=grads):
            columns = lax.dynamic_slice_in_dim(normed, dest * depth, depth, 1)
            return lax.dot_general(
                columns, grads, (((0,), (0,)), ((), ())), preferred_element_type=f32
            )

        def owner(distance):
            return pick(order, (spot + distance) % n_seq)

        half = depth // 2
        farthest = partial(owner(far)).astype(bf16)
        up = along_ring(farthest[:half], 1)
        down = along_ring(farthest[half:], -1)
        for distance in range(far - 1, 0, -1):
            mine_up = partial(owner(distance))
            mine_down = partial(owner(-distance))
            if distance == far - 1:
                mine_up = jnp.concatenate(
                    [mine_up[:half] + up.astype(f32), mine_up[half:]], axis=0
                )
                mine_down = jnp.concatenate(
                    [mine_down[:half], mine_down[half:] + down.astype(f32)], axis=0
                )
            else:
                mine_up = mine_up + up.astype(f32)
                mine_down = mine_down + down.astype(f32)
            up = along_ring(mine_up.astype(bf16), 1)
            down = along_ring(mine_down.astype(bf16), -1)
        mine = partial(at_seq) + up.astype(f32) + down.astype(f32)
        parts_groups.append(
            columns_as_stored([mine[:, g * width : (g + 1) * width] for g in range(3)])
        )

    weight_grad = jnp.concatenate(
        [parts_groups[a][s] for s in range(3) for a in range(GROUPS)], axis=1
    )

    token_out = call(
        functools.partial(token_kernel, (slots, n_blocks, held_depth, rows, GROUPS, split)),
        [
            jax.ShapeDtypeStruct((rows, model), f32),
            *[jax.ShapeDtypeStruct((rows, model), bf16)] * (slots - 1),
            jax.ShapeDtypeStruct((8, model), f32),
        ],
        [
            sources,
            *grad_groups,
            *[block for group in blocks for block in group],
            *pieces,
            means,
            scales,
        ],
        scalars=1,
        flops=2 * tokens * model * 3 * units,
        touched=tokens * model * 4,
    )
    held = {k: token_out[k] for k in range(slots)}
    for bit in reversed(bits):
        for k in sorted(held):
            if k & bit:
                got = swapped(held.pop(k).astype(bf16), "stream", bit)
                held[k ^ bit] = held[k ^ bit].astype(f32) + got.astype(f32)
    grad_normed = held[0]

    outputs = jnp.zeros((per, span, model), bf16)
    direct = jnp.zeros((per, span, model), bf16)
    for a in range(GROUPS):
        for k in range(slots):
            at = (at_stream ^ k) * units + a * width
            outputs = lax.dynamic_update_slice_in_dim(outputs, moved_groups[a][k][0], at, 2)
            direct = lax.dynamic_update_slice_in_dim(direct, moved_groups[a][k][1], at, 2)

    source = inputs.astype(f32).reshape(rows, model)
    scale = scales[:rows, :1]
    scaled = (source - means[:rows, :1]) * scale
    grad_scaled = grad_normed * norm_gain
    grad_source = scale * (
        grad_scaled
        - jnp.mean(grad_scaled, axis=1, keepdims=True)
        - scaled * jnp.mean(grad_scaled * scaled, axis=1, keepdims=True)
    )
    input_grad = (grad_source.reshape(per, span, model) + direct.astype(f32)).astype(bf16)

    gate_sums = jnp.concatenate(sum_groups, axis=1)
    summed = jnp.concatenate(
        [
            lax.dynamic_update_slice_in_dim(
                jnp.zeros((4, model), f32), gate_sums, at_stream * units, 1
            ),
            token_out[slots][:2],
        ],
        axis=0,
    )
    for bit in reversed(bits):
        summed = summed + swapped(summed, "stream", bit)
    bit = 1
    while bit < n_seq:
        summed = summed + swapped(summed, "seq", bit)
        bit *= 2

    final_units = jnp.concatenate(final_groups, axis=1)
    share = model // n_seq
    holder = at_seq * share // units
    within = at_seq * share % units
    mine = lax.dynamic_slice_in_dim(final_units, within, share, 1)
    mine = jnp.where(at_stream == holder, mine, 0.0)
    ordered = jnp.zeros_like(mine)
    for k in range(slots):
        ordered = lax.dynamic_update_slice_in_dim(
            ordered, mine[k * per : (k + 1) * per], (at_stream ^ k) * per, 0
        )
    for bit in reversed(bits):
        ordered = ordered + swapped(ordered, "stream", bit)
    final_state = lax.dynamic_slice_in_dim(ordered, at_stream * per, per, 0)

    return (
        outputs,
        final_state,
        input_grad,
        weight_grad,
        summed[0],
        summed[1],
        summed[2],
        summed[3],
        summed[4],
        summed[5],
    )


def solution(mesh):
    return jax.shard_map(
        local,
        mesh=mesh,
        in_specs=(
            P("stream", "seq", None),
            P("stream", None),
            P("stream"),
            P("seq", "stream"),
            P(),
            P(),
            P(),
            P(),
            P(),
            P(),
            P("stream", "seq", None),
        ),
        out_specs=(
            P("stream", "seq", None),
            P("stream", "seq"),
            P("stream", "seq", None),
            P("seq", "stream"),
            P(),
            P(),
            P(),
            P(),
            P(),
            P(),
        ),
        check_vma=False,
    )
```

```python
import functools

import jax
import jax.numpy as jnp
from jax import lax
from jax.experimental import pallas as pl
from jax.experimental.pallas import tpu as pltpu
from jax.sharding import PartitionSpec as P

epsilon = 1e-05
f32 = jnp.float32
bf16 = jnp.bfloat16
GROUPS = 1
PAD = 8
PINNED = True
MIB = 1024 * 1024


def vmem_spec():
    return pl.BlockSpec(memory_space=pltpu.VMEM)


def smem_spec():
    return pl.BlockSpec(memory_space=pltpu.SMEM)


def call(kernel, out_shape, operands, scratch=(), scalars=0, room=6):
    specs = [smem_spec()] * scalars + [vmem_spec()] * (len(operands) - scalars)
    if PINNED:
        out_shape = jax.tree.map(lambda out: pltpu.VMEM(out.shape, out.dtype), out_shape)
        operands = operands[:scalars] + [
            pltpu.with_memory_space_constraint(x, pltpu.VMEM) for x in operands[scalars:]
        ]
    return pl.pallas_call(
        kernel,
        out_shape=out_shape,
        in_specs=specs,
        out_specs=jax.tree.map(lambda _: vmem_spec(), out_shape),
        scratch_shapes=list(scratch),
        compiler_params=pltpu.CompilerParams(vmem_limit_bytes=room * MIB),
        cost_estimate=pl.CostEstimate(flops=0, bytes_accessed=0, transcendentals=0),
    )(*operands)


def at_spot(spot, count):
    if count != 8:
        return spot
    return spot * 2 if isinstance(spot, int) and spot < 4 else (
        15 - spot * 2 if isinstance(spot, int) else jnp.where(spot < 4, spot * 2, 15 - spot * 2)
    )


def spot_of(index, count):
    if count != 8:
        return index
    return jnp.where(index % 2 == 0, index // 2, (15 - index) // 2)


def wrapped(value, count):
    value = jnp.where(value >= count, value - count, value)
    return jnp.where(value < 0, value + count, value)


def along_ring(value, steps):
    count = lax.axis_size("seq")
    order = [at_spot(i, count) for i in range(count)]
    return lax.ppermute(value, "seq", [(order[i], order[(i + steps) % count]) for i in range(count)])


def swapped(value, axis, bit):
    return lax.ppermute(value, axis, [(i, i ^ bit) for i in range(lax.axis_size(axis))])


def norm_kernel(parts, rows, tail, units, place, *refs):
    flat = sum(len(slot) for slot in parts)
    pieces = refs[:flat]
    gain, bias, normed, means, scales, picked = refs[flat:]
    gain_row, bias_row = gain[...], bias[...]
    lanes = pl.ds(pl.multiple_of(place[2], units), units)
    at = 0
    for k, slot in enumerate(parts):
        for low, high in slot:
            x = pieces[at][...].astype(f32)
            mean = jnp.mean(x, axis=1, keepdims=True)
            centered = x - mean
            scale = lax.rsqrt(jnp.mean(centered * centered, axis=1, keepdims=True) + epsilon)
            base = k * (rows + tail)
            normed[base + low : base + high, :] = (centered * scale * gain_row + bias_row).astype(bf16)
            count = min(high, rows) - low
            here = slice(k * rows + low, k * rows + low + count)
            means[here, :] = jnp.broadcast_to(mean[:count], (count, 128))
            scales[here, :] = jnp.broadcast_to(scale[:count], (count, 128))
            picked[here, :] = pieces[at][:count, lanes]
            at += 1


def strided(ref, row, seqs, stride):
    tiles = [ref[lane, pl.ds(row, seqs, stride=stride), :] for lane in range(ref.shape[0])]
    return jnp.concatenate(tiles, axis=1)


def put_strided(ref, row, seqs, stride, value):
    for lane in range(ref.shape[0]):
        ref[lane, pl.ds(row, seqs, stride=stride), :] = value[:, lane * 128 : (lane + 1) * 128]


def put_rows(ref, row, count, value):
    for lane in range(ref.shape[0]):
        ref[lane, pl.ds(row, count), :] = value[:, lane * 128 : (lane + 1) * 128]


def get_rows(ref, row, count):
    return jnp.concatenate([ref[lane, pl.ds(row, count), :] for lane in range(ref.shape[0])], axis=1)


def message_kernel(slots, units, tail, where, grads, start, lengths, *outs):
    rows, per = grads.shape[0], start.shape[0]
    for k in range(slots):
        lanes = pl.ds(pl.multiple_of(where[k], units), units)
        outs[k][:rows, :] = grads[:, lanes]
        left = start[:, lanes]
        extra = []
        for _ in range(3):
            part = left.astype(bf16).astype(f32)
            extra.append(part)
            left = left - part
        counts = lengths[...]
        high = counts // 256
        extra += [
            jnp.broadcast_to(n.astype(f32)[:, :1], (per, units)) for n in (high, counts - high * 256)
        ]
        extra.append(jnp.zeros((tail - 5 * per, units), f32))
        outs[k][rows:, :] = jnp.concatenate(extra, axis=0).astype(bf16)


def merge_kernel(mine_up, mine_down, up, down, out_up, out_down):
    count, total = up.shape[0], mine_up.shape[0]
    out_up[:count, :] = (mine_up[:count, :] + up[...].astype(f32)).astype(bf16)
    out_down[total - count :, :] = (mine_down[total - count :, :] + down[...].astype(f32)).astype(bf16)
    if count < total:
        out_up[count:, :] = mine_up[count:, :].astype(bf16)
        out_down[: total - count, :] = mine_down[: total - count, :].astype(bf16)


def spread_rows(dims, part, g_in, picked, gs, xs):
    seqs, span, width, slots = dims
    per, lanes = seqs // slots, slice(part * width, (part + 1) * width)
    for n in range(seqs):
        to = n * (span + PAD) + PAD
        put_rows(gs, to, span, g_in[n // per][n % per * span : n % per * span + span, lanes].astype(f32))
        put_rows(xs, to, span, picked[n * span : (n + 1) * span, lanes].astype(f32))


def begin_kernel(blocks, depth, rows, count, sources, normed, *refs):
    total = refs[blocks]
    for k in range(count):
        here = slice(k * rows, (k + 1) * rows)
        sum_ = None
        for b in range(blocks):
            at = pl.multiple_of(sources[b] * depth, depth)
            term = jnp.dot(
                normed[here, pl.ds(at, depth)], refs[b][...], preferred_element_type=f32
            )
            sum_ = term if sum_ is None else sum_ + term
        total[here, :] = sum_


def first_kernel(dims, part, sources, place, normed, start, lens, vecs, picked, *refs):
    seqs, span, width, slots, blocks, depth, split, tail = dims
    stride = span + PAD
    late = 2 if split else 1
    w, begun = refs[:late], refs[late]
    g_in = refs[late + 1 : late + 1 + slots]
    cand, forg, rese, maps, planes, gs, xs = refs[late + 1 + slots :]
    per = seqs // slots
    spread_rows((seqs, span, width, slots), part, g_in, picked, gs, xs)

    rows = per * span
    ext = rows + tail
    lead = w[len(w) - late][...] if late == 1 else jnp.concatenate([w[-2][...], w[-1][...]], axis=0)
    at = pl.multiple_of(sources[blocks - 1] * depth, depth)
    for k in range(slots):
        total = begun[k * ext : (k + 1) * ext, :] + jnp.dot(
            normed[k * ext : (k + 1) * ext, pl.ds(at, depth)], lead, preferred_element_type=f32
        )
        total = total.astype(bf16).astype(f32)
        for j in range(per):
            n = k * per + j
            put_rows(cand, n * stride + PAD - 8, 8, jnp.broadcast_to(total[rows + j : rows + j + 1, :width], (8, width)))
            for ref, gate in ((cand, 0), (forg, 1), (rese, 2)):
                here = total[j * span : (j + 1) * span, gate * width : (gate + 1) * width]
                put_rows(ref, n * stride + PAD, span, here)
    last = strided(cand, PAD - 1, seqs, stride)
    before = jnp.where(place[1] == 0, start[...], last)
    put_strided(cand, PAD - 1, seqs, stride, before)
    peep_f, peep_r, bias_f, bias_r = (vecs[i : i + 1, :] for i in range(4))
    ends = lens[...]
    base = place[0]

    def turn(t, carry):
        previous, decays, injects, handed = carry
        row = t + PAD
        c = strided(cand, row, seqs, stride)
        f = jax.nn.sigmoid(strided(forg, row, seqs, stride) + peep_f * previous + bias_f)
        r = jax.nn.sigmoid(strided(rese, row, seqs, stride) + peep_r * previous + bias_r)
        put_strided(forg, row, seqs, stride, f)
        put_strided(rese, row, seqs, stride, r)
        live = base + t < ends
        d = jnp.where(live, f, 1.0)
        inject = jnp.where(live, (1.0 - f) * c, 0.0)
        pulled = jnp.where(live, r * strided(gs, row, seqs, stride), 0.0)
        decays = decays * d
        return c, decays, d * injects + inject, handed + decays * pulled

    one, zero = jnp.ones((seqs, width), f32), jnp.zeros((seqs, width), f32)
    _, decays, injects, handed = lax.fori_loop(0, span, turn, (before, one, zero, zero), unroll=4)
    maps[0], maps[1], maps[2] = decays, injects, handed
    c, f, r, g, x = (strided(ref, PAD, seqs, stride) for ref in (cand, forg, rese, gs, xs))
    live = base < ends
    d = jnp.where(live, f, 1.0)
    inject = jnp.where(live, (1.0 - f) * c, 0.0)
    via_adjoint = jnp.where(live, (1.0 - f) * peep_f, 0.0)
    via_state = jnp.where(live, r * (1.0 - r) * g * peep_r, 0.0)
    planes[0], planes[1] = via_adjoint, via_adjoint * c
    planes[2], planes[3] = via_state * d, via_state * (inject - x)


def second_kernel(
    dims, part, place, lens, vecs, earlier, later, start, linked, cand, forg, rese, picked, *refs
):
    seqs, span, width, slots, tail = dims
    stride = span + PAD
    g_in = refs[:slots]
    grads, moved = refs[slots], refs[slots + 1 : 2 * slots + 1]
    final, sums = refs[2 * slots + 1 : 2 * slots + 3]
    gs, xs, states, outs, gcs, fts, rts = refs[2 * slots + 3 :]
    per = seqs // slots
    spread_rows((seqs, span, width, slots), part, g_in, picked, gs, xs)
    peep_f, peep_r = vecs[0:1, :], vecs[1:2, :]
    ends = lens[...]
    base = place[0]
    begin, after = earlier[0] * start[...] + earlier[1], later[2]
    put_strided(states, PAD - 1, seqs, stride, begin)

    def forward(t, state):
        row = t + PAD
        c, f, r, x = (strided(ref, row, seqs, stride) for ref in (cand, forg, rese, xs))
        live = base + t < ends
        state = jnp.where(live, f * state + (1.0 - f) * c, state)
        put_strided(states, row, seqs, stride, state)
        put_strided(outs, row, seqs, stride, jnp.where(live, r * state + (1.0 - r) * x, x))
        return state

    end = lax.fori_loop(0, span, forward, begin, unroll=4)
    final[...] = later[0] * end + later[1]
    upcoming = end * (linked[0] * after + linked[2]) - linked[1] * after + linked[3]

    def backward(i, carry):
        reached, upcoming, pf, pr, bf, br = carry
        row = span - 1 - i + PAD
        c, f, r, x, g = (strided(ref, row, seqs, stride) for ref in (cand, forg, rese, xs, gs))
        state = strided(states, row, seqs, stride)
        prior = strided(states, row - 1, seqs, stride)
        previous = strided(cand, row - 1, seqs, stride)
        live = base + (span - 1 - i) < ends
        zero = jnp.zeros_like(f)
        adjoint = jnp.where(live, r * g, 0.0) + reached
        kept = jnp.where(live, (1.0 - f) * adjoint, zero)
        ft = f * kept * (prior - c)
        rt = jnp.where(live, r * (1.0 - r) * g * (state - x), zero)
        put_strided(gcs, row, seqs, stride, kept + upcoming)
        put_strided(fts, row, seqs, stride, ft)
        put_strided(rts, row, seqs, stride, rt)
        put_strided(gs, row, seqs, stride, jnp.where(live, (1.0 - r) * g, g))
        reached = jnp.where(live, f * adjoint, adjoint)
        return (
            reached,
            ft * peep_f + rt * peep_r,
            pf + ft * previous,
            pr + rt * previous,
            bf + ft,
            br + rt,
        )

    zero = jnp.zeros((seqs, width), f32)
    done = lax.fori_loop(0, span, backward, (after, upcoming, zero, zero, zero, zero), unroll=4)
    sums[...] = jnp.zeros_like(sums)
    for i in range(4):
        sums[i : i + 1, :] = jnp.sum(done[2 + i], axis=0, keepdims=True)
    for n in range(seqs):
        at = n * stride + PAD
        k, j = n // per, n % per
        to = k * (per * span + tail) + j * span
        for gate, ref in enumerate((gcs, fts, rts)):
            lanes = slice(gate * width, (gate + 1) * width)
            grads[to : to + span, lanes] = get_rows(ref, at, span).astype(bf16)
        if j == per - 1:
            grads[to + span : to + span + tail, :] = jnp.zeros((tail, 3 * width), bf16)
        moved[k][0, j] = get_rows(outs, at, span).astype(bf16)
        moved[k][1, j] = get_rows(gs, at, span).astype(bf16)


def partial_kernel(count, depth, owners, normed, grads, *outs):
    for i in range(count):
        lanes = pl.ds(pl.multiple_of(owners[i] * depth, min(depth, 128)), depth)
        outs[i][...] = lax.dot_general(
            normed[:, lanes], grads[...], (((0,), (0,)), ((), ())), preferred_element_type=f32
        ).astype(outs[i].dtype)


def token_kernel(dims, parts, sources, *refs):
    slots, blocks, depth, rows, groups, split, tail = dims
    flat = sum(len(slot) for slot in parts)
    n_w = blocks + (1 if split else 0)
    grads = refs[:groups]
    w = [refs[groups + a * n_w : groups + (a + 1) * n_w] for a in range(groups)]
    at0 = groups + groups * n_w
    pieces = refs[at0 : at0 + flat]
    means, scales, own = refs[at0 + flat : at0 + flat + 3]
    others = refs[at0 + flat + 3 : at0 + flat + slots + 2]
    sums = refs[at0 + flat + slots + 2]
    first_of = [sum(len(slot) for slot in parts[:k]) for k in range(slots)]

    def raw(k, lanes):
        found = [
            pieces[first_of[k] + i][: min(high, rows) - low, lanes]
            for i, (low, high) in enumerate(parts[k])
        ]
        return found[0] if len(found) == 1 else jnp.concatenate(found, axis=0)

    def block(a, b):
        if split and b == blocks - 1:
            return jnp.concatenate([w[a][b][...], w[a][b + 1][...]], axis=0)
        return w[a][b][...]

    sums[...] = jnp.zeros_like(sums)
    for b in range(blocks):
        at = pl.multiple_of(sources[b] * depth, depth)
        lanes = pl.ds(at, depth)
        gain_sum, bias_sum = jnp.zeros((8, depth), f32), jnp.zeros((8, depth), f32)
        weights = [block(a, b) for a in range(groups)]
        for k in range(slots):
            here = pl.ds(k * rows, rows)
            total = None
            for a in range(groups):
                term = lax.dot_general(
                    grads[a][k * (rows + tail) : k * (rows + tail) + rows, :],
                    weights[a],
                    (((1,), (1,)), ((), ())),
                    preferred_element_type=f32,
                )
                total = term if total is None else total + term
            copies = depth // 128
            mean = jnp.concatenate([means[here, :]] * copies, axis=1)
            scale = jnp.concatenate([scales[here, :]] * copies, axis=1)
            scaled = (raw(k, lanes).astype(f32) - mean) * scale
            gain_sum += jnp.sum((total * scaled).reshape(rows // 8, 8, depth), axis=0)
            bias_sum += jnp.sum(total.reshape(rows // 8, 8, depth), axis=0)
            if k == 0:
                own[:, lanes] = total
            else:
                others[k - 1][:, lanes] = total.astype(bf16)
        sums[0:1, lanes] = jnp.sum(gain_sum, axis=0, keepdims=True)
        sums[1:2, lanes] = jnp.sum(bias_sum, axis=0, keepdims=True)


def chosen(options, index):
    result = options[0]
    for i in range(1, len(options)):
        result = jnp.where(index == i, options[i], result)
    return result


def gates_of_units(weights, width, lane0, lanes, take):
    count, here = lax.axis_size("stream"), lax.axis_index("stream")
    if count == 4:
        pieces = [weights[:, s * width + lane0 : s * width + lane0 + lanes] for s in range(3)]
        even = here % 2 == 0
        own = jnp.where(even, pieces[0], pieces[2])
        near = swapped(take(pieces[1]), "stream", 1)
        far = swapped(take(jnp.where(even, pieces[2], pieces[0])), "stream", 2)
        got = [own, near, far]
        order = ((0, 1, 2), (1, 0, 2), (2, 0, 1), (2, 1, 0))
        gates = [chosen([got[order[d][gate]] for d in range(4)], here) for gate in range(3)]
        return jnp.concatenate(gates, axis=1), (near, far)
    everything = lax.all_gather(weights, "stream", axis=1, tiled=True)
    model = count * width
    gates = [
        lax.dynamic_slice_in_dim(everything, gate * model + here * width + lane0, lanes, 1)
        for gate in range(3)
    ]
    return jnp.concatenate(gates, axis=1), ()


def columns_as_stored(gates):
    count, here = lax.axis_size("stream"), lax.axis_index("stream")
    if count == 4:
        own = chosen([gates[0], gates[1], gates[1], gates[2]], here)
        near = swapped(
            chosen([gates[1], gates[0], gates[2], gates[1]], here).astype(bf16), "stream", 1
        ).astype(f32)
        far = swapped(
            chosen([gates[2], gates[2], gates[0], gates[0]], here).astype(bf16), "stream", 2
        ).astype(f32)
        even = here % 2 == 0
        return [jnp.where(even, own, far), near, jnp.where(even, far, own)]
    everything = lax.all_gather(jnp.stack(gates).astype(bf16), "stream", axis=1).astype(f32)
    flat = everything.reshape((3 * count,) + gates[0].shape)
    return [lax.dynamic_index_in_dim(flat, 3 * here + s, 0, keepdims=False) for s in range(3)]


def first_maps(maps):
    one, zero = jnp.ones_like(maps[0]), jnp.zeros_like(maps[0])
    return (maps[0], maps[1], maps[2]), (one, zero), (one, zero, zero)


def joined_maps(known, other, bit):
    (decay, inject, handed), before, later = known
    theirs = (other[0], other[1], other[2])
    first = (lax.axis_index("seq") & bit) == 0
    before_new = (theirs[0] * before[0], before[0] * theirs[1] + before[1])
    later_new = (
        later[0] * theirs[0],
        theirs[0] * later[1] + theirs[1],
        later[2] + later[0] * theirs[2],
    )
    before = tuple(jnp.where(first, a, b) for a, b in zip(before, before_new))
    later = tuple(jnp.where(first, b, a) for a, b in zip(later, later_new))
    inject_new = jnp.where(first, theirs[0] * inject + theirs[1], decay * theirs[1] + inject)
    handed_new = jnp.where(first, handed + decay * theirs[2], theirs[2] + theirs[0] * handed)
    return (decay * theirs[0], inject_new, handed_new), before, later


class Rounds:
    def __init__(self):
        self.before, self.given = [], []

    def take(self, value):
        if not self.before:
            return value
        return lax.optimization_barrier((value, self.before))[0]

    def give(self, *values):
        self.given += values

    def turn(self):
        self.before, self.given = self.given, []


def local(
    inputs,
    start_state,
    lengths,
    weights,
    peep_forget,
    peep_reset,
    bias_forget,
    bias_reset,
    norm_gain,
    norm_bias,
    out_grad,
):
    per, span, model = inputs.shape
    n_seq, slots = lax.axis_size("seq"), lax.axis_size("stream")
    at_seq, at_stream = lax.axis_index("seq"), lax.axis_index("stream")
    seqs = per * slots
    units = model // slots
    width = units // GROUPS
    depth = model // n_seq
    rows = per * span
    tokens = seqs * span
    tail = 16
    half = depth // 2
    spot = spot_of(at_seq, n_seq)
    far = n_seq // 2
    steps = [0]
    for k in range(1, far):
        steps += [-k, k]
    steps.append(far)

    def owner(distance):
        return at_spot(wrapped(spot + distance, n_seq), n_seq)

    sources = jnp.stack([owner(distance) for distance in steps]).astype(jnp.int32)
    place = jnp.stack([at_seq * span, at_seq, at_stream * units]).astype(jnp.int32)
    bits = [1 << b for b in range(slots.bit_length() - 1)]

    def owner_units(array, k):
        return lax.dynamic_slice_in_dim(array, (at_stream ^ k) * units, units, array.ndim - 1)

    vectors = jnp.stack([peep_forget, peep_reset, bias_forget, bias_reset])
    vectors = lax.dynamic_slice_in_dim(vectors, at_stream * units, units, 1)
    vectors = jnp.concatenate([vectors, jnp.zeros_like(vectors)], axis=0)
    group_vectors = [vectors[:, a * width : (a + 1) * width] for a in range(GROUPS)]
    gain_row, bias_row = norm_gain.reshape(1, model), norm_bias.reshape(1, model)
    tall = seqs * (span + PAD)
    field = jax.ShapeDtypeStruct((width // 128, tall, 128), f32)
    space = pltpu.VMEM((width // 128, tall, 128), f32)

    rounds = Rounds()
    take, give = rounds.take, rounds.give
    box = {}

    up, down, blocks = [None] * GROUPS, [None] * GROUPS, [None] * GROUPS

    def gather(a, step):
        if step == 1:
            up[a] = down[a] = take(box["dealt", a])
            blocks[a] = [up[a]]
        if step == far:
            up[a], down[a] = up[a][:half], down[a][half:]
        up[a], down[a] = along_ring(take(up[a]), 1), along_ring(take(down[a]), -1)
        blocks[a] += [up[a], down[a]]
        give(up[a], down[a])

    def partials(a, distances, kind):
        places = [owner(distance) for distance in distances]
        grads = take(box["grads", a])
        if depth % 128:
            return [
                lax.dot_general(
                    lax.dynamic_slice_in_dim(box["normed"], place * depth, depth, 1),
                    grads,
                    (((0,), (0,)), ((), ())),
                    preferred_element_type=f32,
                ).astype(kind)
                for place in places
            ]
        return call(
            functools.partial(partial_kernel, len(places), depth),
            [jax.ShapeDtypeStruct((depth, 3 * width), kind)] * len(places),
            [jnp.stack(places).astype(jnp.int32), box["normed"], grads],
            scalars=1,
        )

    def scatter(a, step):
        if step == 1:
            farthest = take(box["farthest", a])
            to_up, to_down = farthest[:half], farthest[half:]
        else:
            to_up, to_down = call(
                merge_kernel,
                [jax.ShapeDtypeStruct((depth, 3 * width), bf16)] * 2,
                [*box["mine", a], up[a], down[a]],
            )
        up[a], down[a] = along_ring(take(to_up), 1), along_ring(take(to_down), -1)
        give(up[a], down[a])
        if step < far:
            box["mine", a] = partials(a, (far - step, step - far), f32)
            give(*box["mine", a])
        else:
            box["own", a] = partials(a, (0,), f32)[0]
            give(box["own", a])

    def deal(a):
        box["dealt", a], came = gates_of_units(weights, units, a * width, width, take)
        give(*came)

    in_parts = slots == 4
    whole_part = [(0, rows + tail)]
    cuts = [(0, rows // 2), (rows // 2, rows + tail)]
    parts = [whole_part, whole_part, cuts, cuts] if in_parts else [whole_part] * slots
    tokens_of = [[None] * len(slot) for slot in parts]
    flat_inputs = inputs.reshape(rows, model)

    def ahead_tokens():
        box["ahead"] = lax.ppermute(
            take(inputs[:, -1, :]), "seq", [(i, i + 1) for i in range(n_seq - 1)]
        )
        give(box["ahead"])

    def own_tokens():
        tokens_of[0][0] = jnp.concatenate(
            [flat_inputs, box["ahead"], jnp.zeros((tail - per, model), bf16)], axis=0
        )

    def everyones_tokens():
        ahead_tokens()
        own_tokens()
        for bit in reversed(bits):
            for k in range(slots):
                if tokens_of[k][0] is not None and tokens_of[k ^ bit][0] is None:
                    tokens_of[k ^ bit][0] = swapped(tokens_of[k][0], "stream", bit)

    def near_tokens():
        own_tokens()
        tokens_of[1][0] = swapped(take(tokens_of[0][0]), "stream", 1)
        give(tokens_of[1][0])

    def far_tokens(i):
        low, high = cuts[i]
        source = flat_inputs[low:high] if high <= rows else tokens_of[0][0][low:high]
        tokens_of[2][i] = swapped(take(source), "stream", 2)
        give(tokens_of[2][i])

    def passed_tokens(i):
        tokens_of[3][i] = swapped(take(tokens_of[2][i]), "stream", 1)
        give(tokens_of[3][i])

    def messages():
        where = jnp.stack([(at_stream ^ k) * units for k in range(slots)]).astype(jnp.int32)
        box["messages"] = call(
            functools.partial(message_kernel, slots, units, tail),
            [jax.ShapeDtypeStruct((rows + tail, units), bf16)] * slots,
            [
                where,
                take(out_grad.reshape(rows, model)),
                start_state,
                jnp.broadcast_to(lengths[:, None], (per, 128)),
            ],
            scalars=1,
        )

    def out_grads():
        for k in range(slots):
            box["g", k] = box["messages"][k]
            if k:
                box["g", k] = swapped(take(box["g", k]), "stream", k)
                give(box["g", k])

    def normalise():
        flat = [piece for slot in tokens_of for piece in slot]
        box["normed"], box["means"], box["scales"], box["picked"] = call(
            functools.partial(norm_kernel, parts, rows, tail, units),
            [
                jax.ShapeDtypeStruct((slots * (rows + tail), model), bf16),
                jax.ShapeDtypeStruct((tokens, 128), f32),
                jax.ShapeDtypeStruct((tokens, 128), f32),
                jax.ShapeDtypeStruct((tokens, units), bf16),
            ],
            [place, *flat, take(gain_row), bias_row],
            scalars=1,
        )
        give(box["normed"])

    def in_order(a):
        if depth % 128 == 0:
            return blocks[a], sources, n_seq, depth, True
        wide = 2 * 128
        if ("whole", a) not in box:
            whole = jnp.zeros((model, 3 * width), bf16)
            for b, block in enumerate(blocks[a]):
                at = owner(steps[min(b, n_seq - 1)]) * depth + (half if b == n_seq else 0)
                whole = lax.dynamic_update_slice_in_dim(whole, block, at, 0)
            box["whole", a] = [whole[i : i + wide] for i in range(0, model, wide)]
        return box["whole", a], jnp.arange(model // wide, dtype=jnp.int32), model // wide, wide, False

    def from_others():
        extra = [box["g", k][rows : rows + 5 * per].astype(f32) for k in range(slots)]
        extra = [x.reshape(5, per, units) for x in extra]
        box["start"] = jnp.concatenate([x[0] + x[1] + x[2] for x in extra], axis=0)
        ends = jnp.concatenate([x[3] * 256 + x[4] for x in extra], axis=0)
        box["ends"] = ends[:, :width].astype(jnp.int32)

    def begin(a):
        held, places, count, deep, _ = in_order(a)
        box["begun", a] = call(
            functools.partial(begin_kernel, count - 1, deep, rows + tail, slots),
            jax.ShapeDtypeStruct((slots * (rows + tail), 3 * width), f32),
            [places, take(box["normed"]), *held[: count - 1]],
            scalars=1,
        )
        give(box["begun", a])

    def first(a):
        start = box["start"][:, a * width : (a + 1) * width]
        held, places, count, deep, split = in_order(a)
        *fields, maps, planes = call(
            functools.partial(first_kernel, (seqs, span, width, slots, count, deep, split, tail), a),
            [
                field,
                field,
                field,
                jax.ShapeDtypeStruct((3, seqs, width), f32),
                jax.ShapeDtypeStruct((4, seqs, width), f32),
            ],
            [
                places,
                place,
                box["normed"],
                start,
                take(box["ends"]),
                group_vectors[a],
                box["picked"],
                *held[count - 1 :],
                box["begun", a],
                *[box["g", k] for k in range(slots)],
            ],
            scratch=[space, space],
            scalars=2,
            room=7,
        )
        box["fields", a] = fields
        box["linked", a] = lax.ppermute(planes, "seq", [(i + 1, i) for i in range(n_seq - 1)])
        box["known", a], box["maps", a] = first_maps(maps), maps
        join(a, 1)
        give(box["linked", a])

    def join(a, bit):
        mine = box["maps", a] if bit == 1 else take(jnp.stack(box["known", a][0]))
        other = swapped(mine, "seq", bit)
        give(other)
        box["known", a] = joined_maps(box["known", a], other, bit)

    def join_rest(a, low, high):
        for b in range(low, high):
            if 1 << b < n_seq:
                join(a, 1 << b)

    def second(a):
        _, earlier, later = box["known", a]
        start = box["start"][:, a * width : (a + 1) * width]
        out = call(
            functools.partial(second_kernel, (seqs, span, width, slots, tail), a),
            [
                jax.ShapeDtypeStruct((slots * (rows + tail), 3 * width), bf16),
                *[jax.ShapeDtypeStruct((2, per, span, width), bf16)] * slots,
                jax.ShapeDtypeStruct((seqs, width), f32),
                jax.ShapeDtypeStruct((8, width), f32),
            ],
            [
                place,
                take(box["ends"]),
                group_vectors[a],
                jnp.stack(earlier),
                jnp.stack(later),
                start,
                box["linked", a],
                *box["fields", a],
                box["picked"],
                *[box["g", k] for k in range(slots)],
            ],
            scratch=[space] * 7,
            scalars=1,
            room=17,
        )
        box["grads", a] = out[0]
        box["moving", a] = out[1 : slots + 1]
        box["final", a], box["sums", a] = out[slots + 1], out[slots + 2][:4]
        box["farthest", a] = partials(a, (far,), bf16)[0]
        box["grads", a] = lax.optimization_barrier((box["grads", a], box["farthest", a]))[0]

    def moved(a, among):
        for k in among:
            box["moved", a, k] = box["moving", a][k]
            if k:
                box["moved", a, k] = swapped(take(box["moving", a][k]), "stream", k)
                give(box["moved", a, k])

    def stored(a):
        total = box["own", a] + up[a].astype(f32) + down[a].astype(f32)
        total = take(total)
        box["stored", a] = columns_as_stored(
            [total[:, g * width : (g + 1) * width] for g in range(3)]
        )

    def token_grads():
        held = [in_order(a) for a in range(GROUPS)]
        _, places, count, deep, split = held[0]
        out = call(
            functools.partial(
                token_kernel, (slots, count, deep, rows, GROUPS, split, tail), parts
            ),
            [
                jax.ShapeDtypeStruct((rows, model), f32),
                *[jax.ShapeDtypeStruct((rows, model), bf16)] * (slots - 1),
                jax.ShapeDtypeStruct((8, model), f32),
            ],
            [
                places,
                *[take(box["grads", a]) for a in range(GROUPS)],
                *[block for group in held for block in group[0]],
                *[piece for slot in tokens_of for piece in slot],
                box["means"],
                box["scales"],
            ],
            scalars=1,
        )
        box["kept"] = {k: out[k] for k in range(slots)}
        box["token_sums"] = out[slots][:2]
        give(out[0])

    def token_sends(bit):
        kept = box["kept"]
        for k in sorted(kept, reverse=True):
            if k & bit:
                got = swapped(take(kept.pop(k).astype(bf16)), "stream", bit)
                kept[k ^ bit] = kept[k ^ bit].astype(f32) + got.astype(f32)
                give(got)

    def token_part(i, count):
        if i == 0:
            box["sending"] = box["kept"].pop(2).astype(bf16)
            box["arrived"] = []
        low, high = rows * i // count // 16 * 16, rows * (i + 1) // count // 16 * 16
        box["arrived"].append(swapped(take(box["sending"][low:high]), "stream", 2))
        give(box["arrived"][i])
        if i + 1 == count:
            box["kept"][0] = box["kept"][0] + jnp.concatenate(box["arrived"], axis=0).astype(f32)

    def sums():
        gate_sums = jnp.concatenate([box["sums", a] for a in range(GROUPS)], axis=1)
        box["summed"] = jnp.concatenate(
            [
                lax.dynamic_update_slice_in_dim(
                    jnp.zeros((4, model), f32), gate_sums, at_stream * units, 1
                ),
                box["token_sums"],
            ],
            axis=0,
        )

    def seq_sums(low, high):
        for b in range(low, high):
            if 1 << b < n_seq:
                box["summed"] = box["summed"] + swapped(take(box["summed"]), "seq", 1 << b)
                give(box["summed"])

    def stream_sums():
        share = model // n_seq
        final_units = jnp.concatenate([box["final", a] for a in range(GROUPS)], axis=1)
        mine = lax.dynamic_slice_in_dim(final_units, at_seq * share % units, share, 1)
        mine = jnp.where(at_stream == at_seq * share // units, mine, 0.0)
        ordered = jnp.zeros_like(mine)
        for k in range(slots):
            ordered = lax.dynamic_update_slice_in_dim(
                ordered, mine[k * per : (k + 1) * per], (at_stream ^ k) * per, 0
            )
        ordered = jnp.pad(ordered.reshape(-1), (0, -seqs * share % model)).reshape(-1, model)
        summed = jnp.concatenate([box["summed"], ordered], axis=0)
        for bit in bits:
            summed = summed + swapped(take(summed), "stream", bit)
        box["final_state"] = lax.dynamic_slice_in_dim(
            summed[6:].reshape(-1)[: seqs * share].reshape(seqs, share), at_stream * per, per, 0
        )
        box["summed"] = summed[:6]

    def assemble():
        for name, which in (("outputs", 0), ("direct", 1)):
            whole = take(jnp.zeros((per, span, model), bf16))
            for a in range(GROUPS):
                for k in range(slots):
                    at = (at_stream ^ k) * units + a * width
                    whole = lax.dynamic_update_slice_in_dim(whole, box["moved", a, k][which], at, 2)
            box[name] = whole

    group = functools.partial
    if in_parts:
        early = [
            [group(far_tokens, 0)],
            [near_tokens, group(far_tokens, 1), group(passed_tokens, 0), messages],
            [group(passed_tokens, 1), out_grads, normalise],
        ]
    else:
        early = [[everyones_tokens], [messages], [out_grads, normalise]]
    early.append([from_others] + ([group(begin, 0)] if depth % 128 == 0 else []))
    if in_parts:
        ahead_tokens()
    deal(0)
    rounds.turn()
    for step in range(1, far + 1):
        gather(0, step)
        for other in early[step - 1] if step <= len(early) else ():
            other()
        rounds.turn()
    if depth % 128:
        begin(0)
    first(0)
    rounds.turn()
    join_rest(0, 1, 9)
    rounds.turn()
    second(0)
    late = [
        [token_grads, group(moved, 0, range(slots)[:3])],
        [group(token_sends, 1), group(moved, 0, range(slots)[3:]), sums, group(seq_sums, 0, 1)],
        [group(seq_sums, 1, 2)],
        [group(seq_sums, 2, 9), assemble],
    ]
    if in_parts:
        late[2].append(group(token_part, 0, 2))
        late[3].append(group(token_part, 1, 2))
    else:
        late[2] += [group(token_sends, bit) for bit in bits[1:]]
    rounds.before = []
    for step in range(1, far + 1):
        scatter(0, step)
        for other in late[step - 1] if step <= len(late) else ():
            other()
        rounds.turn()
    stored(0)
    stream_sums()
    weight_grad = jnp.concatenate(
        [box["stored", a][s] for s in range(3) for a in range(GROUPS)], axis=1
    )

    grad_normed = box["kept"][0]
    source = inputs.astype(f32).reshape(rows, model)
    scale = box["scales"][:rows, :1]
    scaled = (source - box["means"][:rows, :1]) * scale
    grad_scaled = grad_normed * norm_gain
    grad_source = scale * (
        grad_scaled
        - jnp.mean(grad_scaled, axis=1, keepdims=True)
        - scaled * jnp.mean(grad_scaled * scaled, axis=1, keepdims=True)
    )
    input_grad = (grad_source.reshape(per, span, model) + box["direct"].astype(f32)).astype(bf16)
    outputs, final_state, summed = box["outputs"], box["final_state"], box["summed"]

    return (
        outputs,
        final_state,
        input_grad,
        weight_grad,
        summed[0],
        summed[1],
        summed[2],
        summed[3],
        summed[4],
        summed[5],
    )


def solution(mesh):
    return jax.shard_map(
        local,
        mesh=mesh,
        in_specs=(
            P("stream", "seq", None),
            P("stream", None),
            P("stream"),
            P("seq", "stream"),
            P(),
            P(),
            P(),
            P(),
            P(),
            P(),
            P("stream", "seq", None),
        ),
        out_specs=(
            P("stream", "seq", None),
            P("stream", "seq"),
            P("stream", "seq", None),
            P("seq", "stream"),
            P(),
            P(),
            P(),
            P(),
            P(),
            P(),
        ),
        check_vma=False,
    )
```

```python
import functools

import jax
import jax.numpy as jnp
from jax import lax
from jax.experimental import pallas as pl
from jax.experimental.pallas import tpu as pltpu
from jax.sharding import PartitionSpec as P

epsilon = 1e-05
f32 = jnp.float32
bf16 = jnp.bfloat16
PAD = 8
STEP = 256
ROOM = 5 * 512 * 1024


def vmem_spec():
    return pl.BlockSpec(memory_space=pltpu.VMEM)


def smem_spec():
    return pl.BlockSpec(memory_space=pltpu.SMEM)


def call(kernel, out_shape, operands, scratch=(), scalars=0, cost=0):
    return pl.pallas_call(
        kernel,
        out_shape=jax.tree.map(lambda out: pltpu.VMEM(out.shape, out.dtype), out_shape),
        in_specs=[smem_spec()] * scalars + [vmem_spec()] * (len(operands) - scalars),
        out_specs=jax.tree.map(lambda _: vmem_spec(), out_shape),
        scratch_shapes=list(scratch),
        compiler_params=pltpu.CompilerParams(vmem_limit_bytes=lax.axis_size("stream") * ROOM),
        cost_estimate=pl.CostEstimate(flops=int(cost * 1e9), bytes_accessed=0, transcendentals=0),
    )(
        *operands[:scalars],
        *[pltpu.with_memory_space_constraint(x, pltpu.VMEM) for x in operands[scalars:]],
    )


def at_spot(spot, count):
    if count != 8:
        return spot
    return spot * 2 if isinstance(spot, int) and spot < 4 else (
        15 - spot * 2 if isinstance(spot, int) else jnp.where(spot < 4, spot * 2, 15 - spot * 2)
    )


def spot_of(index, count):
    if count != 8:
        return index
    return jnp.where(index % 2 == 0, index // 2, (15 - index) // 2)


def wrapped(value, count):
    value = jnp.where(value >= count, value - count, value)
    return jnp.where(value < 0, value + count, value)


def along_ring(value, steps):
    count = lax.axis_size("seq")
    order = [at_spot(i, count) for i in range(count)]
    return lax.ppermute(value, "seq", [(order[i], order[(i + steps) % count]) for i in range(count)])


def cut(array, start, size, axis):
    starts = [jnp.int32(0)] * array.ndim
    sizes = list(array.shape)
    starts[axis], sizes[axis] = start, size
    return lax.dynamic_slice(array, starts, sizes, allow_negative_indices=False)


def pasted(array, piece, start, axis):
    starts = [jnp.int32(0)] * array.ndim
    starts[axis] = start
    return lax.dynamic_update_slice(array, piece, starts, allow_negative_indices=False)


def swapped(value, axis, bit):
    return lax.ppermute(value, axis, [(i, i ^ bit) for i in range(lax.axis_size(axis))])


def norm_kernel(parts, rows, tail, units, place, *refs):
    flat = sum(len(slot) for slot in parts)
    pieces = refs[:flat]
    gain, bias, normed, means, scales, picked = refs[flat:]
    gain_row, bias_row = gain[...], bias[...]
    lanes = pl.ds(pl.multiple_of(place[2], units), units)
    at = 0
    for k, slot in enumerate(parts):
        for low, high in slot:
            x = pieces[at][...].astype(f32)
            mean = jnp.mean(x, axis=1, keepdims=True)
            centered = x - mean
            scale = lax.rsqrt(jnp.mean(centered * centered, axis=1, keepdims=True) + epsilon)
            base = k * (rows + tail)
            normed[base + low : base + high, :] = (centered * scale * gain_row + bias_row).astype(bf16)
            count = min(high, rows) - low
            here = slice(k * rows + low, k * rows + low + count)
            means[here, :] = jnp.broadcast_to(mean[:count], (count, 128))
            scales[here, :] = jnp.broadcast_to(scale[:count], (count, 128))
            picked[here, :] = pieces[at][:count, lanes]
            at += 1


def strided(ref, row, seqs, stride, low=0, count=None):
    count = ref.shape[0] if count is None else count
    tiles = [ref[low + lane, pl.ds(row, seqs, stride=stride), :] for lane in range(count)]
    return jnp.concatenate(tiles, axis=1)


def put_strided(ref, row, seqs, stride, value, low=0):
    for lane in range(value.shape[1] // 128):
        ref[low + lane, pl.ds(row, seqs, stride=stride), :] = value[:, lane * 128 : (lane + 1) * 128]


def put_rows(ref, row, count, value):
    for lane in range(value.shape[1] // 128):
        ref[lane, pl.ds(row, count), :] = value[:, lane * 128 : (lane + 1) * 128]


def get_rows(ref, row, count):
    return jnp.concatenate([ref[lane, pl.ds(row, count), :] for lane in range(ref.shape[0])], axis=1)


def message_kernel(slots, units, tail, where, grads, start, lengths, *outs):
    rows, per = grads.shape[0], start.shape[0]
    for k in range(slots):
        lanes = pl.ds(pl.multiple_of(where[k], units), units)
        outs[k][:rows, :] = grads[:, lanes]
        left = start[:, lanes]
        extra = []
        for _ in range(3):
            part = left.astype(bf16).astype(f32)
            extra.append(part)
            left = left - part
        counts = lengths[...]
        high = counts // 256
        extra += [
            jnp.broadcast_to(n.astype(f32)[:, :1], (per, units)) for n in (high, counts - high * 256)
        ]
        extra.append(jnp.zeros((tail - 5 * per, units), f32))
        outs[k][rows:, :] = jnp.concatenate(extra, axis=0).astype(bf16)


def merge_kernel(cuts, mine_up, mine_down, up, down, *outs):
    count, total = up.shape[0], mine_up.shape[0]
    for n, (low, high) in enumerate(cuts):
        lanes = slice(low, high)
        out_up, out_down = outs[2 * n], outs[2 * n + 1]
        first, last = slice(0, count), slice(total - count, total)
        out_up[first, :] = (mine_up[first, lanes] + up[:, lanes].astype(f32)).astype(bf16)
        out_down[last, :] = (mine_down[last, lanes] + down[:, lanes].astype(f32)).astype(bf16)
        if count < total:
            out_up[count:, :] = mine_up[count:, lanes].astype(bf16)
            out_down[: total - count, :] = mine_down[: total - count, lanes].astype(bf16)


def assemble_kernel(slots, width, where, *refs):
    for k in range(slots):
        lanes = pl.ds(pl.multiple_of(where[k], width), width)
        for which in range(2):
            refs[slots + which][:, :, lanes] = refs[k][which]


def spread_rows(dims, low, width, g_in, picked, gs, xs):
    seqs, span, slots = dims
    per = seqs // slots
    for n in range(seqs):
        to, lanes = n * (span + PAD) + PAD, slice(low, low + width)
        at = n % per * span
        put_rows(gs, to, span, g_in[n // per][at : at + span, lanes].astype(f32))
        put_rows(xs, to, span, picked[n * span : (n + 1) * span, lanes].astype(f32))


def joined(refs):
    return refs[0][...] if len(refs) == 1 else jnp.concatenate([ref[...] for ref in refs], axis=0)


def begin_kernel(blocks, depth, rows, count, sources, normed, *refs):
    total = refs[blocks]
    for k in range(count):
        here = slice(k * rows, (k + 1) * rows)
        sum_ = None
        for b in range(blocks):
            at = pl.multiple_of(sources[b] * depth, depth)
            term = jnp.dot(normed[here, pl.ds(at, depth)], refs[b][...], preferred_element_type=f32)
            sum_ = term if sum_ is None else sum_ + term
        total[here, :] = sum_


def first_kernel(dims, sources, place, normed, start, lens, v0, v1, v2, v3, picked, begun, *refs):
    vecs = (v0, v1, v2, v3)
    seqs, span, width, slots, blocks, depth, late, tail = dims
    stride = span + PAD
    g_in = refs[late : late + slots]
    fields, maps, planes, gs, xs = refs[late + slots :]
    cand, forg, rese = fields.at[0], fields.at[1], fields.at[2]
    per = seqs // slots
    rows = per * span
    ext = rows + tail
    at = pl.multiple_of(sources[blocks - 1] * depth, depth)
    lead = joined(refs[:late])
    for k in range(slots):
        here = slice(k * ext, (k + 1) * ext)
        for piece in range(3):
            field = fields.at[place[3 + piece]]
            columns = slice(piece * width, (piece + 1) * width)
            total = begun[here, columns] + jnp.dot(
                normed[here, pl.ds(at, depth)], lead[:, columns], preferred_element_type=f32
            )
            total = total.astype(bf16).astype(f32)
            for j in range(per):
                to = (k * per + j) * stride + PAD
                before = jnp.broadcast_to(total[rows + j : rows + j + 1, :], (8, width))
                put_rows(field, to - 8, 8, before)
                put_rows(field, to, span, total[j * span : (j + 1) * span, :])
    before = jnp.where(place[1] == 0, start[...], strided(cand, PAD - 1, seqs, stride))
    put_strided(cand, PAD - 1, seqs, stride, before)
    ends = lens[...]
    base = place[0]
    step = min(width, STEP)
    ends = ends[:, :step]
    for low in range(0, width, step):
        units = slice(low, low + step)
        lane, lanes = low // 128, step // 128
        spread_rows((seqs, span, slots), low, step, g_in, picked, gs, xs)
        own = pl.ds(pl.multiple_of(place[2] + low, 128), step)
        peep_f, peep_r, bias_f, bias_r = (row[:, own] for row in vecs)

        def turn(t, carry):
            previous, decays, injects, handed = carry
            row = t + PAD
            c, f, r = (strided(ref, row, seqs, stride, lane, lanes) for ref in (cand, forg, rese))
            f = jax.nn.sigmoid(f + peep_f * previous + bias_f)
            r = jax.nn.sigmoid(r + peep_r * previous + bias_r)
            put_strided(forg, row, seqs, stride, f, lane)
            put_strided(rese, row, seqs, stride, r, lane)
            live = base + t < ends
            d = jnp.where(live, f, 1.0)
            inject = jnp.where(live, (1.0 - f) * c, 0.0)
            pulled = jnp.where(live, r * strided(gs, row, seqs, stride), 0.0)
            decays = decays * d
            return c, decays, d * injects + inject, handed + decays * pulled

        one, zero = jnp.ones((seqs, step), f32), jnp.zeros((seqs, step), f32)
        _, decays, injects, handed = lax.fori_loop(
            0, span, turn, (before[:, units], one, zero, zero), unroll=8
        )
        maps[0, :, units], maps[1, :, units], maps[2, :, units] = decays, injects, handed
        c, f, r = (strided(ref, PAD, seqs, stride, lane, lanes) for ref in (cand, forg, rese))
        g, x = (strided(ref, PAD, seqs, stride) for ref in (gs, xs))
        live = base < ends
        d = jnp.where(live, f, 1.0)
        inject = jnp.where(live, (1.0 - f) * c, 0.0)
        via_adjoint = jnp.where(live, (1.0 - f) * peep_f, 0.0)
        via_state = jnp.where(live, r * (1.0 - r) * g * peep_r, 0.0)
        planes[0, :, units], planes[1, :, units] = via_adjoint, via_adjoint * c
        planes[2, :, units], planes[3, :, units] = via_state * d, via_state * (inject - x)


def second_kernel(
    dims, place, lens, v0, v1, earlier, later, start, linked, fields, picked, *refs
):
    vecs = (v0, v1)
    seqs, span, width, slots, tail = dims
    stride = span + PAD
    g_in = refs[:slots]
    grads, moved = refs[slots], refs[slots + 1 : 2 * slots + 1]
    final, sums = refs[2 * slots + 1 : 2 * slots + 3]
    gs, xs, states, outs, gcs, fts, rts = refs[2 * slots + 3 :]
    cand, forg, rese = fields.at[0], fields.at[1], fields.at[2]
    per = seqs // slots
    base = place[0]
    step = min(width, STEP)
    ends = lens[:, :step]
    sums[...] = jnp.zeros_like(sums)
    for k in range(slots):
        to = k * (per * span + tail) + per * span
        grads[to : to + tail, :] = jnp.zeros((tail, 3 * width), bf16)
    for low in range(0, width, step):
        units = slice(low, low + step)
        lane, lanes = low // 128, step // 128
        spread_rows((seqs, span, slots), low, step, g_in, picked, gs, xs)
        own = pl.ds(pl.multiple_of(place[2] + low, 128), step)
        peep_f, peep_r = (row[:, own] for row in vecs[:2])
        begin = earlier[0, :, units] * start[:, units] + earlier[1, :, units]
        after = later[2, :, units]
        put_strided(states, PAD - 1, seqs, stride, begin)

        def forward(t, state):
            row = t + PAD
            c, f, r = (strided(ref, row, seqs, stride, lane, lanes) for ref in (cand, forg, rese))
            x = strided(xs, row, seqs, stride)
            live = base + t < ends
            state = jnp.where(live, f * state + (1.0 - f) * c, state)
            put_strided(states, row, seqs, stride, state)
            put_strided(outs, row, seqs, stride, jnp.where(live, r * state + (1.0 - r) * x, x))
            return state

        end = lax.fori_loop(0, span, forward, begin, unroll=8)
        final[:, units] = later[0, :, units] * end + later[1, :, units]
        link = [linked[i, :, units] for i in range(4)]
        upcoming = end * (link[0] * after + link[2]) - link[1] * after + link[3]

        def backward(i, carry):
            reached, upcoming, pf, pr, bf, br = carry
            row = span - 1 - i + PAD
            c, f, r = (strided(ref, row, seqs, stride, lane, lanes) for ref in (cand, forg, rese))
            x, g, state = (strided(ref, row, seqs, stride) for ref in (xs, gs, states))
            prior = strided(states, row - 1, seqs, stride)
            previous = strided(cand, row - 1, seqs, stride, lane, lanes)
            live = base + (span - 1 - i) < ends
            zero = jnp.zeros_like(f)
            adjoint = jnp.where(live, r * g, 0.0) + reached
            kept = jnp.where(live, (1.0 - f) * adjoint, zero)
            ft = f * kept * (prior - c)
            rt = jnp.where(live, r * (1.0 - r) * g * (state - x), zero)
            put_strided(gcs, row, seqs, stride, kept + upcoming)
            put_strided(fts, row, seqs, stride, ft)
            put_strided(rts, row, seqs, stride, rt)
            put_strided(gs, row, seqs, stride, jnp.where(live, (1.0 - r) * g, g))
            reached = jnp.where(live, f * adjoint, adjoint)
            return (
                reached,
                ft * peep_f + rt * peep_r,
                pf + ft * previous,
                pr + rt * previous,
                bf + ft,
                br + rt,
            )

        zero = jnp.zeros((seqs, step), f32)
        done = lax.fori_loop(
            0, span, backward, (after, upcoming, zero, zero, zero, zero), unroll=4
        )
        for i in range(4):
            sums[i : i + 1, units] = jnp.sum(done[2 + i], axis=0, keepdims=True)
        for n in range(seqs):
            at = n * stride + PAD
            k, j = n // per, n % per
            to = k * (per * span + tail) + j * span
            for gate, ref in enumerate((gcs, fts, rts)):
                here = slice(gate * width + low, gate * width + low + step)
                grads[to : to + span, here] = get_rows(ref, at, span).astype(bf16)
            moved[k][0, j, :, units] = get_rows(outs, at, span).astype(bf16)
            moved[k][1, j, :, units] = get_rows(gs, at, span).astype(bf16)


def partial_kernel(distances, depth, width, owners, place, normed, grads, *outs):
    for i, distance in enumerate(distances):
        lanes = pl.ds(pl.multiple_of(owners[distance] * depth, min(depth, 128)), depth)
        columns = normed[:, lanes]
        for piece in range(3):
            gate = pl.ds(pl.multiple_of(place[3 + piece] * width, width), width)
            sum_ = lax.dot_general(
                columns, grads[:, gate], (((0,), (0,)), ((), ())), preferred_element_type=f32
            )
            outs[i][:, piece * width : (piece + 1) * width] = sum_.astype(outs[i].dtype)


def token_kernel(dims, parts, sources, place, grads, gate_sums, *refs):
    slots, blocks, depth, rows, width, split, tail = dims
    flat = sum(len(slot) for slot in parts)
    n_w = blocks + (1 if split else 0)
    pieces = refs[n_w : n_w + flat]
    means, scales, own = refs[n_w + flat : n_w + flat + 3]
    others = refs[n_w + flat + 3 : n_w + flat + slots + 2]
    sums = refs[n_w + flat + slots + 2]
    first_of = [sum(len(slot) for slot in parts[:k]) for k in range(slots)]

    def raw(k, lanes):
        found = [
            pieces[first_of[k] + i][: min(high, rows) - low, lanes]
            for i, (low, high) in enumerate(parts[k])
        ]
        return found[0] if len(found) == 1 else jnp.concatenate(found, axis=0)

    def block(b):
        return joined(refs[b : b + 2] if split and b == blocks - 1 else refs[b : b + 1])

    sums[...] = jnp.zeros_like(sums)
    sums[:4, pl.ds(pl.multiple_of(place[2], width), width)] = gate_sums[:4, :]
    for b in range(blocks):
        at = pl.multiple_of(sources[b] * depth, depth)
        lanes = pl.ds(at, depth)
        gain_sum, bias_sum = jnp.zeros((8, depth), f32), jnp.zeros((8, depth), f32)
        weights = block(b)
        for k in range(slots):
            here = pl.ds(k * rows, rows)
            total = None
            for piece in range(3):
                gate = pl.ds(pl.multiple_of(place[3 + piece] * width, width), width)
                term = lax.dot_general(
                    grads[k * (rows + tail) : k * (rows + tail) + rows, gate],
                    weights[:, piece * width : (piece + 1) * width],
                    (((1,), (1,)), ((), ())),
                    preferred_element_type=f32,
                )
                total = term if total is None else total + term
            copies = depth // 128
            mean = jnp.concatenate([means[here, :]] * copies, axis=1)
            scale = jnp.concatenate([scales[here, :]] * copies, axis=1)
            scaled = (raw(k, lanes).astype(f32) - mean) * scale
            gain_sum += jnp.sum((total * scaled).reshape(rows // 8, 8, depth), axis=0)
            bias_sum += jnp.sum(total.reshape(rows // 8, 8, depth), axis=0)
            if k == 0:
                own[:, lanes] = total
            else:
                others[k - 1][:, lanes] = total.astype(bf16)
        sums[4:5, lanes] = jnp.sum(gain_sum, axis=0, keepdims=True)
        sums[5:6, lanes] = jnp.sum(bias_sum, axis=0, keepdims=True)


def first_maps(maps):
    one, zero = jnp.ones_like(maps[0]), jnp.zeros_like(maps[0])
    return (maps[0], maps[1], maps[2]), (one, zero), (one, zero, zero)


def joined_maps(known, other, first):
    (decay, inject, handed), before, later = known
    theirs = (other[0], other[1], other[2])
    before_new = (theirs[0] * before[0], before[0] * theirs[1] + before[1])
    later_new = (
        later[0] * theirs[0],
        theirs[0] * later[1] + theirs[1],
        later[2] + later[0] * theirs[2],
    )
    before = tuple(jnp.where(first, a, b) for a, b in zip(before, before_new))
    later = tuple(jnp.where(first, b, a) for a, b in zip(later, later_new))
    inject_new = jnp.where(first, theirs[0] * inject + theirs[1], decay * theirs[1] + inject)
    handed_new = jnp.where(first, handed + decay * theirs[2], theirs[2] + theirs[0] * handed)
    return (decay * theirs[0], inject_new, handed_new), before, later


class Rounds:
    def __init__(self):
        self.before, self.given = [], []

    def take(self, value):
        if not self.before:
            return value
        return lax.optimization_barrier((value, self.before))[0]

    def give(self, *values):
        self.given += values

    def turn(self):
        self.before, self.given = self.given, []


def local(
    inputs,
    start_state,
    lengths,
    weights,
    peep_forget,
    peep_reset,
    bias_forget,
    bias_reset,
    norm_gain,
    norm_bias,
    out_grad,
):
    per, span, model = inputs.shape
    n_seq, slots = lax.axis_size("seq"), lax.axis_size("stream")
    at_seq, at_stream = lax.axis_index("seq"), lax.axis_index("stream")
    seqs = per * slots
    width = model // slots
    depth = model // n_seq
    rows = per * span
    tokens = seqs * span
    tail = 16
    half = depth // 2
    spot = spot_of(at_seq, n_seq)
    far = n_seq // 2
    steps = [0]
    for k in range(1, far):
        steps += [-k, k]
    steps.append(far)
    dealing = slots == 4

    def owner(distance):
        return at_spot(wrapped(spot + distance, n_seq), n_seq)

    def per_stream(table):
        found = table[0]
        for d in range(1, len(table)):
            found = jnp.where(at_stream == d, table[d], found)
        return found

    gates = ((0, 1, 2), (1, 0, 2), (1, 2, 0), (2, 1, 0)) if dealing else ((0, 1, 2),)
    gate_of = [per_stream([table[piece] for table in gates]) for piece in range(3)]
    bits = [1 << b for b in range(slots.bit_length() - 1)]
    seq_bits = [1 << b for b in range(n_seq.bit_length() - 1)]
    share = model // n_seq
    index = {
        "sources": jnp.stack([owner(distance) for distance in steps]).astype(jnp.int32),
        "place": jnp.stack([at_seq * span, at_seq, at_stream * width, *gate_of]).astype(jnp.int32),
        "owners": jnp.stack([owner(distance) for distance in range(n_seq)]).astype(jnp.int32),
        "where": jnp.stack([(at_stream ^ k) * width for k in range(slots)]).astype(jnp.int32),
        "lanes": [(at_stream ^ k) * width for k in range(slots)],
        "rows": [(at_stream ^ k) * per for k in range(slots)],
        "first": [(at_seq & bit) == 0 for bit in seq_bits],
        "even": at_stream % 2 == 0,
        "share": at_seq * share % width,
        "holds": at_stream == at_seq * share // width,
    }
    index, inputs, weights, out_grad, start_state, lengths = lax.optimization_barrier(
        (index, inputs, weights, out_grad, start_state, lengths)
    )
    sources, place, even = index["sources"], index["place"], index["even"]

    vectors = [
        row.reshape(1, model) for row in (peep_forget, peep_reset, bias_forget, bias_reset)
    ]
    gain_row, bias_row = norm_gain.reshape(1, model), norm_bias.reshape(1, model)
    tall = seqs * (span + PAD)
    fields = jax.ShapeDtypeStruct((3, width // 128, tall, 128), f32)
    space = pltpu.VMEM((min(width, STEP) // 128, tall, 128), f32)

    rounds = Rounds()
    take, give = rounds.take, rounds.give
    box = {}

    def deal():
        if dealing:
            pieces = [weights[:, i * width : (i + 1) * width] for i in range(3)]
            own = jnp.where(even, pieces[0], pieces[2])
            near = swapped(pieces[1], "stream", 1)
            distant = swapped(jnp.where(even, pieces[2], pieces[0]), "stream", 2)
            box["dealt"] = jnp.concatenate([own, near, distant], axis=1)
            give(near, distant)
            return
        everything = lax.all_gather(weights, "stream", axis=1, tiled=True)
        found = [
            lax.dynamic_slice_in_dim(everything, gate * model + at_stream * width, width, 1)
            for gate in range(3)
        ]
        box["dealt"] = jnp.concatenate(found, axis=1)

    def stored():
        own, rest = box["total"]
        near, distant = rest[:, :width], rest[:, width:]
        if dealing:
            distant = swapped(distant.astype(bf16), "stream", 2).astype(f32)
            near = swapped(near.astype(bf16), "stream", 1).astype(f32)
            found = [jnp.where(even, own, distant), near, jnp.where(even, distant, own)]
        else:
            flat = lax.all_gather(
                jnp.concatenate(box["total"], axis=1).astype(bf16), "stream", axis=0
            ).astype(f32)
            flat = jnp.swapaxes(flat.reshape(slots, depth, 3, width), 0, 2)
            flat = jnp.swapaxes(flat, 1, 2).reshape(3 * slots, depth, width)
            found = [
                lax.dynamic_index_in_dim(flat, 3 * at_stream + i, 0, keepdims=False)
                for i in range(3)
            ]
        return jnp.concatenate(found, axis=1)

    def gather(step):
        if step == 1:
            box["up"] = box["down"] = take(box["dealt"])
            box["blocks"] = [box["dealt"]]
        if step == far:
            box["up"], box["down"] = box["up"][:half], box["down"][half:]
        box["up"] = along_ring(take(box["up"]), 1)
        box["down"] = along_ring(take(box["down"]), -1)
        box["blocks"] += [box["up"], box["down"]]
        give(box["up"], box["down"])

    def partials(distances, kind):
        grads = take(box["grads"])
        if depth % 128:
            found = []
            for distance in distances:
                at = owner(distance)
                sum_ = lax.dot_general(
                    lax.dynamic_slice_in_dim(box["normed"], at * depth, depth, 1),
                    grads,
                    (((0,), (0,)), ((), ())),
                    preferred_element_type=f32,
                ).astype(kind)
                found.append(sum_)
            return found
        return call(
            functools.partial(
                partial_kernel, [distance % n_seq for distance in distances], depth, width
            ),
            [jax.ShapeDtypeStruct((depth, 3 * width), kind)] * len(distances),
            [index["owners"], place, box["normed"], grads],
            scalars=2,
        )

    def scatter(step):
        cuts_of = [(0, 3 * width)]
        if step == 1:
            sent = [box["farthest"][:half], box["farthest"][half:]]
        else:
            sent = call(
                functools.partial(merge_kernel, cuts_of),
                [jax.ShapeDtypeStruct((depth, b - a), bf16) for a, b in cuts_of for _ in range(2)],
                [*box["mine"], box["up"], box["down"]],
            )
        came = [along_ring(take(value), 1 - 2 * (i % 2)) for i, value in enumerate(sent)]
        box["up"], box["down"] = came
        give(*came)
        box["mine"] = partials((far - step, step - far) if step < far else (0,), f32)
        give(*box["mine"])

    whole_part = [(0, rows + tail)]
    cuts = [(0, rows // 2), (rows // 2, rows + tail)]
    parts = [whole_part, whole_part, cuts, cuts] if dealing else [whole_part] * slots
    tokens_of = [[None] * len(slot) for slot in parts]
    flat_inputs = inputs.reshape(rows, model)

    def ahead_tokens():
        box["ahead"] = lax.ppermute(
            take(inputs[:, -1, :]), "seq", [(i, i + 1) for i in range(n_seq - 1)]
        )
        give(box["ahead"])

    def own_tokens():
        tokens_of[0][0] = jnp.concatenate(
            [flat_inputs, box["ahead"], jnp.zeros((tail - per, model), bf16)], axis=0
        )

    def everyones_tokens():
        ahead_tokens()
        own_tokens()
        for bit in reversed(bits):
            for k in range(slots):
                if tokens_of[k][0] is not None and tokens_of[k ^ bit][0] is None:
                    tokens_of[k ^ bit][0] = swapped(tokens_of[k][0], "stream", bit)

    def near_tokens():
        own_tokens()
        tokens_of[1][0] = swapped(take(tokens_of[0][0]), "stream", 1)
        give(tokens_of[1][0])

    def far_tokens(i):
        low, high = cuts[i]
        source = flat_inputs[low:high] if high <= rows else tokens_of[0][0][low:high]
        tokens_of[2][i] = swapped(take(source), "stream", 2)
        give(tokens_of[2][i])

    def passed_tokens(i):
        tokens_of[3][i] = swapped(take(tokens_of[2][i]), "stream", 1)
        give(tokens_of[3][i])

    def messages():
        box["messages"] = call(
            functools.partial(message_kernel, slots, width, tail),
            [jax.ShapeDtypeStruct((rows + tail, width), bf16)] * slots,
            [
                index["where"],
                take(out_grad.reshape(rows, model)),
                start_state,
                jnp.broadcast_to(lengths[:, None], (per, 128)),
            ],
            scalars=1,
        )

    def out_grads():
        for k in range(slots):
            box["g", k] = box["messages"][k]
            if k:
                box["g", k] = swapped(take(box["g", k]), "stream", k)
                give(box["g", k])

    def normalise():
        flat = [piece for slot in tokens_of for piece in slot]
        box["normed"], box["means"], box["scales"], box["picked"] = call(
            functools.partial(norm_kernel, parts, rows, tail, width),
            [
                jax.ShapeDtypeStruct((slots * (rows + tail), model), bf16),
                jax.ShapeDtypeStruct((tokens, 128), f32),
                jax.ShapeDtypeStruct((tokens, 128), f32),
                jax.ShapeDtypeStruct((tokens, width), bf16),
            ],
            [place, *flat, take(gain_row), bias_row],
            scalars=1,
        )
        give(box["normed"])

    def from_others():
        extra = [box["g", k][rows : rows + 5 * per].astype(f32) for k in range(slots)]
        extra = [x.reshape(5, per, width) for x in extra]
        box["start"] = jnp.concatenate([x[0] + x[1] + x[2] for x in extra], axis=0)
        ends = jnp.concatenate([x[3] * 256 + x[4] for x in extra], axis=0)
        box["ends"] = ends.astype(jnp.int32)

    def in_order():
        if depth % 128 == 0:
            return box["blocks"], sources, n_seq, depth, True
        deep = 2 * 128
        if "whole" not in box:
            whole = jnp.zeros((model, 3 * width), bf16)
            for b, block in enumerate(box["blocks"]):
                at = owner(steps[min(b, n_seq - 1)]) * depth + (half if b == n_seq else 0)
                whole = lax.dynamic_update_slice_in_dim(whole, block, at, 0)
            box["whole"] = [whole[i : i + deep] for i in range(0, model, deep)]
        count = model // deep
        return box["whole"], jnp.arange(count, dtype=jnp.int32), count, deep, False

    def begin():
        held, places, count, deep, _ = in_order()
        box["begun"] = call(
            functools.partial(begin_kernel, count - 1, deep, rows + tail, slots),
            jax.ShapeDtypeStruct((slots * (rows + tail), 3 * width), f32),
            [places, take(box["normed"]), *held[: count - 1]],
            scalars=1,
        )
        give(box["begun"])

    def first():
        held, places, count, deep, split = in_order()
        box["fields"], maps, planes = call(
            functools.partial(
                first_kernel, (seqs, span, width, slots, count, deep, 2 if split else 1, tail)
            ),
            [
                fields,
                jax.ShapeDtypeStruct((3, seqs, width), f32),
                jax.ShapeDtypeStruct((4, seqs, width), f32),
            ],
            [
                places,
                place,
                box["normed"],
                box["start"],
                take(box["ends"]),
                *vectors,
                box["picked"],
                box["begun"],
                *held[count - 1 :],
                *[box["g", k] for k in range(slots)],
            ],
            scratch=[space, space],
            scalars=2,
        )
        box["linked"] = lax.ppermute(planes, "seq", [(i + 1, i) for i in range(n_seq - 1)])
        box["known"], box["maps"] = first_maps(maps), maps
        join(1)

    def join(bit):
        mine = box["maps"] if bit == 1 else take(jnp.stack(box["known"][0]))
        other = swapped(mine, "seq", bit)
        give(other)
        box["known"] = joined_maps(box["known"], other, index["first"][seq_bits.index(bit)])

    def join_rest():
        bit = 2
        while bit < n_seq:
            join(bit)
            bit *= 2

    def second():
        _, earlier, later = box["known"]
        out = call(
            functools.partial(second_kernel, (seqs, span, width, slots, tail)),
            [
                jax.ShapeDtypeStruct((slots * (rows + tail), 3 * width), bf16),
                *[jax.ShapeDtypeStruct((2, per, span, width), bf16)] * slots,
                jax.ShapeDtypeStruct((seqs, width), f32),
                jax.ShapeDtypeStruct((8, width), f32),
            ],
            [
                place,
                take(box["ends"]),
                *vectors[:2],
                jnp.stack(earlier),
                jnp.stack(later),
                box["start"],
                box["linked"],
                box["fields"],
                box["picked"],
                *[box["g", k] for k in range(slots)],
            ],
            scratch=[space] * 7,
            scalars=1,
        )
        box["grads"], box["moving"] = out[0], out[1 : slots + 1]
        box["final"], box["sums"] = out[slots + 1], out[slots + 2]
        rounds.before = []
        box["farthest"] = partials((far,), bf16)[0]
        box["grads"] = lax.optimization_barrier((box["grads"], box["farthest"]))[0]

    def moved(among):
        for k in among:
            box["moved", k] = box["moving"][k]
            if k:
                box["moved", k] = swapped(take(box["moving"][k]), "stream", k)
                give(box["moved", k])

    def token_grads():
        held, places, count, deep, split = in_order()
        out = call(
            functools.partial(
                token_kernel, (slots, count, deep, rows, width, split, tail), parts
            ),
            [
                jax.ShapeDtypeStruct((rows, model), f32),
                *[jax.ShapeDtypeStruct((rows, model), bf16)] * (slots - 1),
                jax.ShapeDtypeStruct((8, model), f32),
            ],
            [
                places,
                place,
                take(box["grads"]),
                box["sums"],
                *held,
                *[piece for slot in tokens_of for piece in slot],
                box["means"],
                box["scales"],
            ],
            scalars=2,
        )
        box["kept"] = {k: out[k] for k in range(slots)}
        box["summed"] = out[slots]
        give(out[0])

    def token_sends(bit):
        kept = box["kept"]
        for k in sorted(kept, reverse=True):
            if k & bit:
                got = swapped(take(kept.pop(k).astype(bf16)), "stream", bit)
                kept[k ^ bit] = kept[k ^ bit].astype(f32) + got.astype(f32)
                give(got)

    def token_part(i, count):
        if i == 0:
            box["sending"] = box["kept"].pop(2).astype(bf16)
            box["arrived"] = []
        low, high = rows * i // count // 16 * 16, rows * (i + 1) // count // 16 * 16
        box["arrived"].append(swapped(take(box["sending"][low:high]), "stream", 2))
        give(box["arrived"][i])
        if i + 1 == count:
            box["kept"][0] = box["kept"][0] + jnp.concatenate(box["arrived"], axis=0).astype(f32)

    def sums(axis, bit):
        if "states" not in box:
            mine = jnp.where(index["holds"], cut(box["final"], index["share"], share, 1), 0.0)
            box["states"] = {k: mine[k * per : (k + 1) * per] for k in range(slots)}
        states, summed = box["states"], box["summed"][:6]
        going = [k for k in sorted(states) if k & bit] if axis == "stream" else []
        if going:
            row = jnp.concatenate([states[k] for k in going], axis=1)
            row = jnp.pad(row, ((0, 0), (0, model - row.shape[1])))
            summed = jnp.concatenate([summed, row], axis=0)
        got = swapped(take(summed), axis, bit)
        box["summed"] = box["summed"][:6] + got[:6]
        for i, k in enumerate(going):
            states.pop(k)
            states[k ^ bit] = states[k ^ bit] + got[6:, i * share : (i + 1) * share]

    def assemble():
        box["outputs"], box["direct"] = call(
            functools.partial(assemble_kernel, slots, width),
            [jax.ShapeDtypeStruct((per, span, model), bf16)] * 2,
            [index["where"], *[take(box["moved", k]) for k in range(slots)]],
            scalars=1,
        )

    part = functools.partial
    if dealing:
        early = [
            [part(far_tokens, 0)],
            [near_tokens, part(far_tokens, 1), part(passed_tokens, 0), messages],
            [part(passed_tokens, 1), out_grads, normalise],
        ]
    else:
        early = [[everyones_tokens], [messages], [out_grads, normalise]]
    early.append([from_others] + ([begin] if depth % 128 == 0 else []))
    deal()
    if dealing:
        ahead_tokens()
    rounds.turn()
    for step in range(1, far + 1):
        gather(step)
        for other in early[step - 1] if step <= len(early) else ():
            other()
        rounds.turn()
    if depth % 128:
        begin()
    first()
    rounds.turn()
    join_rest()
    rounds.turn()
    second()
    late = [
        [part(moved, range(slots)[:3])],
        [part(moved, range(slots)[3:]), token_grads],
        [part(token_sends, 1), part(sums, "stream", 1), part(sums, "seq", 1)],
        [part(sums, "seq", 2), assemble],
    ]
    if dealing:
        late[3] += [part(token_part, 0, 2), part(token_part, 1, 2)]
    else:
        late[3] += [part(token_sends, bit) for bit in bits[1:]]
    for step in range(1, far + 1):
        scatter(step)
        for other in late[step - 1] if step <= len(late) else ():
            other()
        rounds.turn()
    total = box["mine"][0] + box["up"].astype(f32) + box["down"].astype(f32)
    box["total"] = total[:, :width], total[:, width:]
    weight_grad = stored()
    for bit in seq_bits[2:]:
        sums("seq", bit)
    for bit in bits[1:]:
        sums("stream", bit)

    grad_normed = box["kept"][0]
    source = inputs.astype(f32).reshape(rows, model)
    scale = box["scales"][:rows, :1]
    scaled = (source - box["means"][:rows, :1]) * scale
    grad_scaled = grad_normed * norm_gain
    grad_source = scale * (
        grad_scaled
        - jnp.mean(grad_scaled, axis=1, keepdims=True)
        - scaled * jnp.mean(grad_scaled * scaled, axis=1, keepdims=True)
    )
    input_grad = (grad_source.reshape(per, span, model) + box["direct"].astype(f32)).astype(bf16)
    outputs, final_state, summed = box["outputs"], box["states"][0], box["summed"]

    return (
        outputs,
        final_state,
        input_grad,
        weight_grad,
        summed[0],
        summed[1],
        summed[2],
        summed[3],
        summed[4],
        summed[5],
    )


def solution(mesh):
    return jax.shard_map(
        local,
        mesh=mesh,
        in_specs=(
            P("stream", "seq", None),
            P("stream", None),
            P("stream"),
            P("seq", "stream"),
            P(),
            P(),
            P(),
            P(),
            P(),
            P(),
            P("stream", "seq", None),
        ),
        out_specs=(
            P("stream", "seq", None),
            P("stream", "seq"),
            P("stream", "seq", None),
            P("seq", "stream"),
            P(),
            P(),
            P(),
            P(),
            P(),
            P(),
        ),
        check_vma=False,
    )
```

```python
import functools

import jax
import jax.numpy as jnp
from jax import lax
from jax.experimental import pallas as pl
from jax.experimental.pallas import tpu as pltpu
from jax.sharding import PartitionSpec as P

epsilon = 1e-05
f32 = jnp.float32
bf16 = jnp.bfloat16
PAD = 8
STEP = 256
ROOM = 5 * 512 * 1024


def vmem_spec():
    return pl.BlockSpec(memory_space=pltpu.VMEM)


def smem_spec():
    return pl.BlockSpec(memory_space=pltpu.SMEM)


def call(kernel, out_shape, operands, scratch=(), scalars=0, pinned=True):
    held = jax.tree.map(lambda out: pltpu.VMEM(out.shape, out.dtype), out_shape)
    return pl.pallas_call(
        kernel,
        out_shape=held if pinned else out_shape,
        in_specs=[smem_spec()] * scalars + [vmem_spec()] * (len(operands) - scalars),
        out_specs=jax.tree.map(lambda _: vmem_spec(), out_shape),
        scratch_shapes=list(scratch),
        compiler_params=pltpu.CompilerParams(vmem_limit_bytes=lax.axis_size("stream") * ROOM),
        cost_estimate=pl.CostEstimate(flops=0, bytes_accessed=0, transcendentals=0),
    )(
        *operands[:scalars],
        *[pltpu.with_memory_space_constraint(x, pltpu.VMEM) for x in operands[scalars:]],
    )


def at_spot(spot, count):
    if count != 8:
        return spot
    return spot * 2 if isinstance(spot, int) and spot < 4 else (
        15 - spot * 2 if isinstance(spot, int) else jnp.where(spot < 4, spot * 2, 15 - spot * 2)
    )


def spot_of(index, count):
    if count != 8:
        return index
    return jnp.where(index % 2 == 0, index // 2, (15 - index) // 2)


def wrapped(value, count):
    value = jnp.where(value >= count, value - count, value)
    return jnp.where(value < 0, value + count, value)


def along_ring(value, steps):
    count = lax.axis_size("seq")
    order = [at_spot(i, count) for i in range(count)]
    return lax.ppermute(value, "seq", [(order[i], order[(i + steps) % count]) for i in range(count)])


def cut(array, start, size, axis):
    starts = [jnp.int32(0)] * array.ndim
    sizes = list(array.shape)
    starts[axis], sizes[axis] = start, size
    return lax.dynamic_slice(array, starts, sizes, allow_negative_indices=False)


def pasted(array, piece, start, axis):
    starts = [jnp.int32(0)] * array.ndim
    starts[axis] = start
    return lax.dynamic_update_slice(array, piece, starts, allow_negative_indices=False)


def swapped(value, axis, bit):
    return lax.ppermute(value, axis, [(i, i ^ bit) for i in range(lax.axis_size(axis))])


def norm_kernel(parts, rows, tail, units, place, *refs):
    flat = sum(len(slot) for slot in parts)
    pieces = refs[:flat]
    gain, bias, normed, means, scales, picked = refs[flat:]
    gain_row, bias_row = gain[...], bias[...]
    lanes = pl.ds(pl.multiple_of(place[2], units), units)
    at = 0
    for k, slot in enumerate(parts):
        for low, high in slot:
            x = pieces[at][...].astype(f32)
            mean = jnp.mean(x, axis=1, keepdims=True)
            centered = x - mean
            scale = lax.rsqrt(jnp.mean(centered * centered, axis=1, keepdims=True) + epsilon)
            base = k * (rows + tail)
            normed[base + low : base + high, :] = (centered * scale * gain_row + bias_row).astype(bf16)
            count = min(high, rows) - low
            here = slice(k * rows + low, k * rows + low + count)
            means[here, :] = jnp.broadcast_to(mean[:count], (count, 128))
            scales[here, :] = jnp.broadcast_to(scale[:count], (count, 128))
            picked[here, :] = pieces[at][:count, lanes]
            at += 1


def strided(ref, row, seqs, stride, low=0, count=None):
    count = ref.shape[0] if count is None else count
    tiles = [ref[low + lane, pl.ds(row, seqs, stride=stride), :] for lane in range(count)]
    return jnp.concatenate(tiles, axis=1)


def put_strided(ref, row, seqs, stride, value, low=0):
    for lane in range(value.shape[1] // 128):
        ref[low + lane, pl.ds(row, seqs, stride=stride), :] = value[:, lane * 128 : (lane + 1) * 128]


def put_rows(ref, row, count, value):
    for lane in range(value.shape[1] // 128):
        ref[lane, pl.ds(row, count), :] = value[:, lane * 128 : (lane + 1) * 128]


def get_rows(ref, row, count):
    return jnp.concatenate([ref[lane, pl.ds(row, count), :] for lane in range(ref.shape[0])], axis=1)


def message_kernel(slots, units, tail, where, grads, start, lengths, *outs):
    rows, per = grads.shape[0], start.shape[0]
    for k in range(slots):
        lanes = pl.ds(pl.multiple_of(where[k], units), units)
        outs[k][:rows, :] = grads[:, lanes]
        left = start[:, lanes]
        extra = []
        for _ in range(3):
            part = left.astype(bf16).astype(f32)
            extra.append(part)
            left = left - part
        counts = lengths[...]
        high = counts // 256
        extra += [
            jnp.broadcast_to(n.astype(f32)[:, :1], (per, units)) for n in (high, counts - high * 256)
        ]
        extra.append(jnp.zeros((tail - 5 * per, units), f32))
        outs[k][rows:, :] = jnp.concatenate(extra, axis=0).astype(bf16)


def merge_kernel(cuts, mine_up, mine_down, up, down, *outs):
    count, total = up.shape[0], mine_up.shape[0]
    for n, (low, high) in enumerate(cuts):
        lanes = slice(low, high)
        out_up, out_down = outs[2 * n], outs[2 * n + 1]
        first, last = slice(0, count), slice(total - count, total)
        out_up[first, :] = (mine_up[first, lanes] + up[:, lanes].astype(f32)).astype(bf16)
        out_down[last, :] = (mine_down[last, lanes] + down[:, lanes].astype(f32)).astype(bf16)
        if count < total:
            out_up[count:, :] = mine_up[count:, lanes].astype(bf16)
            out_down[: total - count, :] = mine_down[: total - count, lanes].astype(bf16)


def assemble_kernel(slots, width, where, *refs):
    for k in range(slots):
        lanes = pl.ds(pl.multiple_of(where[k], width), width)
        for which in range(2):
            refs[slots + which][:, :, lanes] = refs[k][which]


def spread_rows(dims, low, width, g_in, picked, gs, xs):
    seqs, span, slots = dims
    per = seqs // slots
    for n in range(seqs):
        to, lanes = n * (span + PAD) + PAD, slice(low, low + width)
        at = n % per * span
        put_rows(gs, to, span, g_in[n // per][at : at + span, lanes].astype(f32))
        put_rows(xs, to, span, picked[n * span : (n + 1) * span, lanes].astype(f32))


def joined(refs):
    return refs[0][...] if len(refs) == 1 else jnp.concatenate([ref[...] for ref in refs], axis=0)


def begin_kernel(blocks, depth, rows, count, sources, normed, *refs):
    total = refs[blocks]
    for k in range(count):
        here = slice(k * rows, (k + 1) * rows)
        sum_ = None
        for b in range(blocks):
            at = pl.multiple_of(sources[b] * depth, depth)
            term = jnp.dot(normed[here, pl.ds(at, depth)], refs[b][...], preferred_element_type=f32)
            sum_ = term if sum_ is None else sum_ + term
        total[here, :] = sum_


def first_kernel(dims, sources, place, normed, start, lens, v0, v1, v2, v3, picked, begun, *refs):
    vecs = (v0, v1, v2, v3)
    seqs, span, width, slots, blocks, depth, late, tail = dims
    stride = span + PAD
    g_in = refs[late : late + slots]
    fields, maps, planes, gs, xs = refs[late + slots :]
    cand, forg, rese = fields.at[0], fields.at[1], fields.at[2]
    per = seqs // slots
    rows = per * span
    ext = rows + tail
    at = pl.multiple_of(sources[blocks - 1] * depth, depth)
    lead = joined(refs[:late])
    for k in range(slots):
        here = slice(k * ext, (k + 1) * ext)
        for piece in range(3):
            field = fields.at[place[3 + piece]]
            columns = slice(piece * width, (piece + 1) * width)
            total = begun[here, columns] + jnp.dot(
                normed[here, pl.ds(at, depth)], lead[:, columns], preferred_element_type=f32
            )
            total = total.astype(bf16).astype(f32)
            for j in range(per):
                to = (k * per + j) * stride + PAD
                before = jnp.broadcast_to(total[rows + j : rows + j + 1, :], (8, width))
                put_rows(field, to - 8, 8, before)
                put_rows(field, to, span, total[j * span : (j + 1) * span, :])
    before = jnp.where(place[1] == 0, start[...], strided(cand, PAD - 1, seqs, stride))
    put_strided(cand, PAD - 1, seqs, stride, before)
    ends = lens[...]
    base = place[0]
    step = min(width, STEP)
    ends = ends[:, :step]
    for low in range(0, width, step):
        units = slice(low, low + step)
        lane, lanes = low // 128, step // 128
        spread_rows((seqs, span, slots), low, step, g_in, picked, gs, xs)
        own = pl.ds(pl.multiple_of(place[2] + low, 128), step)
        peep_f, peep_r, bias_f, bias_r = (row[:, own] for row in vecs)

        def turn(t, carry):
            previous, decays, injects, handed = carry
            row = t + PAD
            c, f, r = (strided(ref, row, seqs, stride, lane, lanes) for ref in (cand, forg, rese))
            f = jax.nn.sigmoid(f + peep_f * previous + bias_f)
            r = jax.nn.sigmoid(r + peep_r * previous + bias_r)
            put_strided(forg, row, seqs, stride, f, lane)
            put_strided(rese, row, seqs, stride, r, lane)
            live = base + t < ends
            d = jnp.where(live, f, 1.0)
            inject = jnp.where(live, (1.0 - f) * c, 0.0)
            pulled = jnp.where(live, r * strided(gs, row, seqs, stride), 0.0)
            decays = decays * d
            return c, decays, d * injects + inject, handed + decays * pulled

        one, zero = jnp.ones((seqs, step), f32), jnp.zeros((seqs, step), f32)
        _, decays, injects, handed = lax.fori_loop(
            0, span, turn, (before[:, units], one, zero, zero), unroll=8
        )
        maps[0, :, units], maps[1, :, units], maps[2, :, units] = decays, injects, handed
        c, f, r = (strided(ref, PAD, seqs, stride, lane, lanes) for ref in (cand, forg, rese))
        g, x = (strided(ref, PAD, seqs, stride) for ref in (gs, xs))
        live = base < ends
        d = jnp.where(live, f, 1.0)
        inject = jnp.where(live, (1.0 - f) * c, 0.0)
        via_adjoint = jnp.where(live, (1.0 - f) * peep_f, 0.0)
        via_state = jnp.where(live, r * (1.0 - r) * g * peep_r, 0.0)
        planes[0, :, units], planes[1, :, units] = via_adjoint, via_adjoint * c
        planes[2, :, units], planes[3, :, units] = via_state * d, via_state * (inject - x)


def second_kernel(
    dims, place, lens, v0, v1, earlier, later, start, linked, fields, picked, *refs
):
    vecs = (v0, v1)
    seqs, span, width, slots, tail = dims
    stride = span + PAD
    g_in = refs[:slots]
    grads, moved = refs[slots], refs[slots + 1 : 2 * slots + 1]
    final, sums = refs[2 * slots + 1 : 2 * slots + 3]
    gs, xs, states, outs, gcs, fts, rts = refs[2 * slots + 3 :]
    cand, forg, rese = fields.at[0], fields.at[1], fields.at[2]
    per = seqs // slots
    base = place[0]
    step = min(width, STEP)
    ends = lens[:, :step]
    sums[...] = jnp.zeros_like(sums)
    for k in range(slots):
        to = k * (per * span + tail) + per * span
        grads[to : to + tail, :] = jnp.zeros((tail, 3 * width), bf16)
    for low in range(0, width, step):
        units = slice(low, low + step)
        lane, lanes = low // 128, step // 128
        spread_rows((seqs, span, slots), low, step, g_in, picked, gs, xs)
        own = pl.ds(pl.multiple_of(place[2] + low, 128), step)
        peep_f, peep_r = (row[:, own] for row in vecs[:2])
        begin = earlier[0, :, units] * start[:, units] + earlier[1, :, units]
        after = later[2, :, units]
        put_strided(states, PAD - 1, seqs, stride, begin)

        def forward(t, state):
            row = t + PAD
            c, f, r = (strided(ref, row, seqs, stride, lane, lanes) for ref in (cand, forg, rese))
            x = strided(xs, row, seqs, stride)
            live = base + t < ends
            state = jnp.where(live, f * state + (1.0 - f) * c, state)
            put_strided(states, row, seqs, stride, state)
            put_strided(outs, row, seqs, stride, jnp.where(live, r * state + (1.0 - r) * x, x))
            return state

        end = lax.fori_loop(0, span, forward, begin, unroll=8)
        final[:, units] = later[0, :, units] * end + later[1, :, units]
        link = [linked[i, :, units] for i in range(4)]
        upcoming = end * (link[0] * after + link[2]) - link[1] * after + link[3]

        def backward(i, carry):
            reached, upcoming, pf, pr, bf, br = carry
            row = span - 1 - i + PAD
            c, f, r = (strided(ref, row, seqs, stride, lane, lanes) for ref in (cand, forg, rese))
            x, g, state = (strided(ref, row, seqs, stride) for ref in (xs, gs, states))
            prior = strided(states, row - 1, seqs, stride)
            previous = strided(cand, row - 1, seqs, stride, lane, lanes)
            live = base + (span - 1 - i) < ends
            zero = jnp.zeros_like(f)
            adjoint = jnp.where(live, r * g, 0.0) + reached
            kept = jnp.where(live, (1.0 - f) * adjoint, zero)
            ft = f * kept * (prior - c)
            rt = jnp.where(live, r * (1.0 - r) * g * (state - x), zero)
            put_strided(gcs, row, seqs, stride, kept + upcoming)
            put_strided(fts, row, seqs, stride, ft)
            put_strided(rts, row, seqs, stride, rt)
            put_strided(gs, row, seqs, stride, jnp.where(live, (1.0 - r) * g, g))
            reached = jnp.where(live, f * adjoint, adjoint)
            return (
                reached,
                ft * peep_f + rt * peep_r,
                pf + ft * previous,
                pr + rt * previous,
                bf + ft,
                br + rt,
            )

        zero = jnp.zeros((seqs, step), f32)
        done = lax.fori_loop(
            0, span, backward, (after, upcoming, zero, zero, zero, zero), unroll=4
        )
        for i in range(4):
            sums[i : i + 1, units] = jnp.sum(done[2 + i], axis=0, keepdims=True)
        for n in range(seqs):
            at = n * stride + PAD
            k, j = n // per, n % per
            to = k * (per * span + tail) + j * span
            for gate, ref in enumerate((gcs, fts, rts)):
                here = slice(gate * width + low, gate * width + low + step)
                grads[to : to + span, here] = get_rows(ref, at, span).astype(bf16)
            moved[k][0, j, :, units] = get_rows(outs, at, span).astype(bf16)
            moved[k][1, j, :, units] = get_rows(gs, at, span).astype(bf16)


def partial_kernel(distances, depth, width, owners, place, normed, grads, *outs):
    for i, distance in enumerate(distances):
        lanes = pl.ds(pl.multiple_of(owners[distance] * depth, min(depth, 128)), depth)
        columns = normed[:, lanes]
        for piece in range(3):
            gate = pl.ds(pl.multiple_of(place[3 + piece] * width, width), width)
            sum_ = lax.dot_general(
                columns, grads[:, gate], (((0,), (0,)), ((), ())), preferred_element_type=f32
            )
            outs[i][:, piece * width : (piece + 1) * width] = sum_.astype(outs[i].dtype)


def token_kernel(dims, parts, sources, place, grads, gate_sums, *refs):
    slots, blocks, depth, rows, width, split, tail = dims
    flat = sum(len(slot) for slot in parts)
    n_w = blocks + (1 if split else 0)
    pieces = refs[n_w : n_w + flat]
    means, scales, own = refs[n_w + flat : n_w + flat + 3]
    others = refs[n_w + flat + 3 : n_w + flat + slots + 2]
    sums = refs[n_w + flat + slots + 2]
    first_of = [sum(len(slot) for slot in parts[:k]) for k in range(slots)]

    def raw(k, lanes):
        found = [
            pieces[first_of[k] + i][: min(high, rows) - low, lanes]
            for i, (low, high) in enumerate(parts[k])
        ]
        return found[0] if len(found) == 1 else jnp.concatenate(found, axis=0)

    def block(b):
        return joined(refs[b : b + 2] if split and b == blocks - 1 else refs[b : b + 1])

    sums[...] = jnp.zeros_like(sums)
    sums[:4, pl.ds(pl.multiple_of(place[2], width), width)] = gate_sums[:4, :]
    for b in range(blocks):
        at = pl.multiple_of(sources[b] * depth, depth)
        lanes = pl.ds(at, depth)
        gain_sum, bias_sum = jnp.zeros((8, depth), f32), jnp.zeros((8, depth), f32)
        weights = block(b)
        for k in range(slots):
            here = pl.ds(k * rows, rows)
            total = None
            for piece in range(3):
                gate = pl.ds(pl.multiple_of(place[3 + piece] * width, width), width)
                term = lax.dot_general(
                    grads[k * (rows + tail) : k * (rows + tail) + rows, gate],
                    weights[:, piece * width : (piece + 1) * width],
                    (((1,), (1,)), ((), ())),
                    preferred_element_type=f32,
                )
                total = term if total is None else total + term
            copies = depth // 128
            mean = jnp.concatenate([means[here, :]] * copies, axis=1)
            scale = jnp.concatenate([scales[here, :]] * copies, axis=1)
            scaled = (raw(k, lanes).astype(f32) - mean) * scale
            gain_sum += jnp.sum((total * scaled).reshape(rows // 8, 8, depth), axis=0)
            bias_sum += jnp.sum(total.reshape(rows // 8, 8, depth), axis=0)
            if k == 0:
                own[:, lanes] = total
            else:
                others[k - 1][:, lanes] = total.astype(bf16)
        sums[4:5, lanes] = jnp.sum(gain_sum, axis=0, keepdims=True)
        sums[5:6, lanes] = jnp.sum(bias_sum, axis=0, keepdims=True)


def first_maps(maps):
    one, zero = jnp.ones_like(maps[0]), jnp.zeros_like(maps[0])
    return (maps[0], maps[1], maps[2]), (one, zero), (one, zero, zero)


def joined_maps(known, other, first):
    (decay, inject, handed), before, later = known
    theirs = (other[0], other[1], other[2])
    before_new = (theirs[0] * before[0], before[0] * theirs[1] + before[1])
    later_new = (
        later[0] * theirs[0],
        theirs[0] * later[1] + theirs[1],
        later[2] + later[0] * theirs[2],
    )
    before = tuple(jnp.where(first, a, b) for a, b in zip(before, before_new))
    later = tuple(jnp.where(first, b, a) for a, b in zip(later, later_new))
    inject_new = jnp.where(first, theirs[0] * inject + theirs[1], decay * theirs[1] + inject)
    handed_new = jnp.where(first, handed + decay * theirs[2], theirs[2] + theirs[0] * handed)
    return (decay * theirs[0], inject_new, handed_new), before, later


class Rounds:
    def __init__(self):
        self.before, self.given = [], []

    def take(self, value):
        if not self.before:
            return value
        return lax.optimization_barrier((value, self.before))[0]

    def give(self, *values):
        self.given += values

    def turn(self):
        self.before, self.given = self.given, []


def local(
    inputs,
    start_state,
    lengths,
    weights,
    peep_forget,
    peep_reset,
    bias_forget,
    bias_reset,
    norm_gain,
    norm_bias,
    out_grad,
):
    per, span, model = inputs.shape
    n_seq, slots = lax.axis_size("seq"), lax.axis_size("stream")
    at_seq, at_stream = lax.axis_index("seq"), lax.axis_index("stream")
    seqs = per * slots
    width = model // slots
    depth = model // n_seq
    rows = per * span
    tokens = seqs * span
    tail = 16
    half = depth // 2
    spot = spot_of(at_seq, n_seq)
    far = n_seq // 2
    steps = [0]
    for k in range(1, far):
        steps += [-k, k]
    steps.append(far)
    dealing = slots == 4

    def owner(distance):
        return at_spot(wrapped(spot + distance, n_seq), n_seq)

    def per_stream(table):
        found = table[0]
        for d in range(1, len(table)):
            found = jnp.where(at_stream == d, table[d], found)
        return found

    gates = ((0, 1, 2), (1, 0, 2), (1, 2, 0), (2, 1, 0)) if dealing else ((0, 1, 2),)
    gate_of = [per_stream([table[piece] for table in gates]) for piece in range(3)]
    bits = [1 << b for b in range(slots.bit_length() - 1)]
    seq_bits = [1 << b for b in range(n_seq.bit_length() - 1)]
    share = model // n_seq
    index = {
        "sources": jnp.stack([owner(distance) for distance in steps]).astype(jnp.int32),
        "place": jnp.stack([at_seq * span, at_seq, at_stream * width, *gate_of]).astype(jnp.int32),
        "owners": jnp.stack([owner(distance) for distance in range(n_seq)]).astype(jnp.int32),
        "where": jnp.stack([(at_stream ^ k) * width for k in range(slots)]).astype(jnp.int32),
        "lanes": [(at_stream ^ k) * width for k in range(slots)],
        "rows": [(at_stream ^ k) * per for k in range(slots)],
        "first": [(at_seq & bit) == 0 for bit in seq_bits],
        "even": at_stream % 2 == 0,
        "share": at_seq * share % width,
        "holds": at_stream == at_seq * share // width,
    }
    index, inputs, weights, out_grad, start_state, lengths = lax.optimization_barrier(
        (index, inputs, weights, out_grad, start_state, lengths)
    )
    sources, place, even = index["sources"], index["place"], index["even"]

    vectors = [
        row.reshape(1, model) for row in (peep_forget, peep_reset, bias_forget, bias_reset)
    ]
    gain_row, bias_row = norm_gain.reshape(1, model), norm_bias.reshape(1, model)
    tall = seqs * (span + PAD)
    fields = jax.ShapeDtypeStruct((3, width // 128, tall, 128), f32)
    space = pltpu.VMEM((min(width, STEP) // 128, tall, 128), f32)

    rounds = Rounds()
    take, give = rounds.take, rounds.give
    box = {}

    def deal():
        if dealing:
            pieces = [weights[:, i * width : (i + 1) * width] for i in range(3)]
            own = jnp.where(even, pieces[0], pieces[2])
            near = swapped(pieces[1], "stream", 1)
            distant = swapped(jnp.where(even, pieces[2], pieces[0]), "stream", 2)
            box["dealt"] = jnp.concatenate([own, near, distant], axis=1)
            give(near, distant)
            return
        everything = lax.all_gather(weights, "stream", axis=1, tiled=True)
        found = [
            lax.dynamic_slice_in_dim(everything, gate * model + at_stream * width, width, 1)
            for gate in range(3)
        ]
        box["dealt"] = jnp.concatenate(found, axis=1)

    def stored():
        own, rest = box["total"]
        near, distant = rest[:, :width], rest[:, width:]
        if dealing:
            distant, near = distant.astype(bf16), near.astype(bf16)
            rounds.before = [*rounds.before, distant, near]
            distant = swapped(distant, "stream", 2).astype(f32)
            near = swapped(near, "stream", 1).astype(f32)
            found = [jnp.where(even, own, distant), near, jnp.where(even, distant, own)]
        else:
            flat = lax.all_gather(
                jnp.concatenate(box["total"], axis=1).astype(bf16), "stream", axis=0
            ).astype(f32)
            flat = jnp.swapaxes(flat.reshape(slots, depth, 3, width), 0, 2)
            flat = jnp.swapaxes(flat, 1, 2).reshape(3 * slots, depth, width)
            found = [
                lax.dynamic_index_in_dim(flat, 3 * at_stream + i, 0, keepdims=False)
                for i in range(3)
            ]
        return jnp.concatenate(found, axis=1)

    def gather(step):
        if step == 1:
            box["up"] = box["down"] = take(box["dealt"])
            box["blocks"] = [box["dealt"]]
        if step == far:
            box["up"], box["down"] = box["up"][:half], box["down"][half:]
        box["up"] = along_ring(take(box["up"]), 1)
        box["down"] = along_ring(take(box["down"]), -1)
        box["blocks"] += [box["up"], box["down"]]
        give(box["up"], box["down"])

    def partials(distances, kind):
        grads = take(box["grads"])
        if depth % 128:
            found = []
            for distance in distances:
                at = owner(distance)
                sum_ = lax.dot_general(
                    lax.dynamic_slice_in_dim(box["normed"], at * depth, depth, 1),
                    grads,
                    (((0,), (0,)), ((), ())),
                    preferred_element_type=f32,
                ).astype(kind)
                found.append(sum_)
            return found
        return call(
            functools.partial(
                partial_kernel, [distance % n_seq for distance in distances], depth, width
            ),
            [jax.ShapeDtypeStruct((depth, 3 * width), kind)] * len(distances),
            [index["owners"], place, box["normed"], grads],
            scalars=2,
        )

    def scatter(step):
        cuts_of = [(0, 3 * width)]
        if step == 1:
            sent = [box["farthest"][:half], box["farthest"][half:]]
        else:
            sent = call(
                functools.partial(merge_kernel, cuts_of),
                [jax.ShapeDtypeStruct((depth, b - a), bf16) for a, b in cuts_of for _ in range(2)],
                [*box["mine", step], box["up"], box["down"]],
            )
        came = [along_ring(take(value), 1 - 2 * (i % 2)) for i, value in enumerate(sent)]
        rounds.before = [*rounds.before, *sent]
        box["up"], box["down"] = came
        give(*came)

    def sums_of(step):
        distance = far + 1 - step
        box["mine", step] = partials((distance, -distance) if distance else (0,), f32)
        give(*box["mine", step])

    whole_part = [(0, rows + tail)]
    cuts = [(0, rows // 2), (rows // 2, rows + tail)]
    parts = [whole_part, whole_part, cuts, cuts] if dealing else [whole_part] * slots
    tokens_of = [[None] * len(slot) for slot in parts]
    flat_inputs = inputs.reshape(rows, model)

    def ahead_tokens():
        box["ahead"] = lax.ppermute(
            take(inputs[:, -1, :]), "seq", [(i, i + 1) for i in range(n_seq - 1)]
        )
        give(box["ahead"])

    def own_tokens():
        tokens_of[0][0] = jnp.concatenate(
            [flat_inputs, box["ahead"], jnp.zeros((tail - per, model), bf16)], axis=0
        )

    def everyones_tokens():
        ahead_tokens()
        own_tokens()
        for bit in reversed(bits):
            for k in range(slots):
                if tokens_of[k][0] is not None and tokens_of[k ^ bit][0] is None:
                    tokens_of[k ^ bit][0] = swapped(tokens_of[k][0], "stream", bit)

    def near_tokens():
        own_tokens()
        tokens_of[1][0] = swapped(take(tokens_of[0][0]), "stream", 1)
        give(tokens_of[1][0])

    def far_tokens(i):
        low, high = cuts[i]
        source = flat_inputs[low:high] if high <= rows else tokens_of[0][0][low:high]
        tokens_of[2][i] = swapped(take(source), "stream", 2)
        give(tokens_of[2][i])

    def passed_tokens(i):
        tokens_of[3][i] = swapped(take(tokens_of[2][i]), "stream", 1)
        give(tokens_of[3][i])

    def messages():
        box["messages"] = call(
            functools.partial(message_kernel, slots, width, tail),
            [jax.ShapeDtypeStruct((rows + tail, width), bf16)] * slots,
            [
                index["where"],
                take(out_grad.reshape(rows, model)),
                start_state,
                jnp.broadcast_to(lengths[:, None], (per, 128)),
            ],
            scalars=1,
        )

    def out_grads():
        for k in range(slots):
            box["g", k] = box["messages"][k]
            if k:
                box["g", k] = swapped(take(box["g", k]), "stream", k)
                give(box["g", k])

    def normalise():
        flat = [piece for slot in tokens_of for piece in slot]
        box["normed"], box["means"], box["scales"], box["picked"] = call(
            functools.partial(norm_kernel, parts, rows, tail, width),
            [
                jax.ShapeDtypeStruct((slots * (rows + tail), model), bf16),
                jax.ShapeDtypeStruct((tokens, 128), f32),
                jax.ShapeDtypeStruct((tokens, 128), f32),
                jax.ShapeDtypeStruct((tokens, width), bf16),
            ],
            [place, *flat, take(gain_row), bias_row],
            scalars=1,
        )
        give(box["normed"])

    def from_others():
        extra = [box["g", k][rows : rows + 5 * per].astype(f32) for k in range(slots)]
        extra = [x.reshape(5, per, width) for x in extra]
        box["start"] = jnp.concatenate([x[0] + x[1] + x[2] for x in extra], axis=0)
        ends = jnp.concatenate([x[3] * 256 + x[4] for x in extra], axis=0)
        box["ends"] = ends.astype(jnp.int32)

    def in_order():
        if depth % 128 == 0:
            return box["blocks"], sources, n_seq, depth, True
        deep = 2 * 128
        if "whole" not in box:
            whole = jnp.zeros((model, 3 * width), bf16)
            for b, block in enumerate(box["blocks"]):
                at = owner(steps[min(b, n_seq - 1)]) * depth + (half if b == n_seq else 0)
                whole = lax.dynamic_update_slice_in_dim(whole, block, at, 0)
            box["whole"] = [whole[i : i + deep] for i in range(0, model, deep)]
        count = model // deep
        return box["whole"], jnp.arange(count, dtype=jnp.int32), count, deep, False

    def begin():
        held, places, count, deep, _ = in_order()
        box["begun"] = call(
            functools.partial(begin_kernel, count - 1, deep, rows + tail, slots),
            jax.ShapeDtypeStruct((slots * (rows + tail), 3 * width), f32),
            [places, take(box["normed"]), *held[: count - 1]],
            scalars=1,
        )
        give(box["begun"])

    def first():
        held, places, count, deep, split = in_order()
        box["fields"], maps, planes = call(
            functools.partial(
                first_kernel, (seqs, span, width, slots, count, deep, 2 if split else 1, tail)
            ),
            [
                fields,
                jax.ShapeDtypeStruct((3, seqs, width), f32),
                jax.ShapeDtypeStruct((4, seqs, width), f32),
            ],
            [
                places,
                place,
                box["normed"],
                box["start"],
                take(box["ends"]),
                *vectors,
                box["picked"],
                box["begun"],
                *held[count - 1 :],
                *[box["g", k] for k in range(slots)],
            ],
            scratch=[space, space],
            scalars=2,
        )
        box["linked"] = lax.ppermute(planes, "seq", [(i + 1, i) for i in range(n_seq - 1)])
        box["known"], box["maps"] = first_maps(maps), maps
        join(1)

    def join(bit):
        mine = box["maps"] if bit == 1 else take(jnp.stack(box["known"][0]))
        other = swapped(mine, "seq", bit)
        give(other)
        box["known"] = joined_maps(box["known"], other, index["first"][seq_bits.index(bit)])

    def join_rest():
        bit = 2
        while bit < n_seq:
            join(bit)
            bit *= 2

    def second():
        _, earlier, later = box["known"]
        out = call(
            functools.partial(second_kernel, (seqs, span, width, slots, tail)),
            [
                jax.ShapeDtypeStruct((slots * (rows + tail), 3 * width), bf16),
                *[jax.ShapeDtypeStruct((2, per, span, width), bf16)] * slots,
                jax.ShapeDtypeStruct((seqs, width), f32),
                jax.ShapeDtypeStruct((8, width), f32),
            ],
            [
                place,
                take(box["ends"]),
                *vectors[:2],
                jnp.stack(earlier),
                jnp.stack(later),
                box["start"],
                box["linked"],
                box["fields"],
                box["picked"],
                *[box["g", k] for k in range(slots)],
            ],
            scratch=[space] * 7,
            scalars=1,
        )
        box["grads"], box["moving"] = out[0], out[1 : slots + 1]
        box["final"], box["sums"] = out[slots + 1], out[slots + 2]
        rounds.before = []
        box["farthest"] = partials((far,), bf16)[0]
        box["grads"] = lax.optimization_barrier((box["grads"], box["farthest"]))[0]

    def moved(among):
        for k in among:
            box["moved", k] = box["moving"][k]
            if k:
                box["moved", k] = swapped(take(box["moving"][k]), "stream", k)
                give(box["moved", k])

    def token_grads():
        held, places, count, deep, split = in_order()
        out = call(
            functools.partial(
                token_kernel, (slots, count, deep, rows, width, split, tail), parts
            ),
            [
                jax.ShapeDtypeStruct((rows, model), f32),
                *[jax.ShapeDtypeStruct((rows, model), bf16)] * (slots - 1),
                jax.ShapeDtypeStruct((8, model), f32),
            ],
            [
                places,
                place,
                take(box["grads"]),
                box["sums"],
                *held,
                *[piece for slot in tokens_of for piece in slot],
                box["means"],
                box["scales"],
            ],
            scalars=2,
        )
        box["kept"] = {k: out[k] for k in range(slots)}
        box["summed"] = out[slots]
        give(out[0])

    def token_sends(bit):
        kept = box["kept"]
        for k in sorted(kept, reverse=True):
            if k & bit:
                got = swapped(take(kept.pop(k).astype(bf16)), "stream", bit)
                kept[k ^ bit] = kept[k ^ bit].astype(f32) + got.astype(f32)
                give(got)

    def token_part(i, count):
        if i == 0:
            box["sending"] = box["kept"].pop(2).astype(bf16)
            box["arrived"] = []
        low, high = rows * i // count // 16 * 16, rows * (i + 1) // count // 16 * 16
        box["arrived"].append(swapped(take(box["sending"][low:high]), "stream", 2))
        give(box["arrived"][i])
        if i + 1 == count:
            box["kept"][0] = box["kept"][0] + jnp.concatenate(box["arrived"], axis=0).astype(f32)

    def sums(axis, bit):
        if "states" not in box:
            mine = jnp.where(index["holds"], cut(box["final"], index["share"], share, 1), 0.0)
            box["states"] = {k: mine[k * per : (k + 1) * per] for k in range(slots)}
        states, summed = box["states"], box["summed"][:6]
        going = [k for k in sorted(states) if k & bit] if axis == "stream" else []
        if going:
            row = jnp.concatenate([states[k] for k in going], axis=1)
            row = jnp.pad(row, ((0, 0), (0, model - row.shape[1])))
            summed = jnp.concatenate([summed, row], axis=0)
        got = swapped(take(summed), axis, bit)
        give(got)
        box["summed"] = box["summed"][:6] + got[:6]
        for i, k in enumerate(going):
            states.pop(k)
            states[k ^ bit] = states[k ^ bit] + got[6:, i * share : (i + 1) * share]

    def assemble():
        box["outputs"], box["direct"] = found = call(
            functools.partial(assemble_kernel, slots, width),
            [jax.ShapeDtypeStruct((per, span, model), bf16)] * 2,
            [index["where"], *[take(box["moved", k]) for k in range(slots)]],
            scalars=1,
            pinned=False,
        )
        give(*found)
        give(*found)

    def finish():
        grad_normed = box["kept"][0]
        source = inputs.astype(f32).reshape(rows, model)
        scale = box["scales"][:rows, :1]
        scaled = (source - box["means"][:rows, :1]) * scale
        grad_scaled = grad_normed * norm_gain
        grad_source = scale * (
            grad_scaled
            - jnp.mean(grad_scaled, axis=1, keepdims=True)
            - scaled * jnp.mean(grad_scaled * scaled, axis=1, keepdims=True)
        )
        box["input_grad"] = (grad_source.reshape(per, span, model) + box["direct"].astype(f32)).astype(bf16)
        give(box["input_grad"])

    part = functools.partial
    if dealing:
        early = [
            [part(far_tokens, 0)],
            [near_tokens, part(far_tokens, 1), part(passed_tokens, 0), messages],
            [part(passed_tokens, 1), out_grads, normalise],
        ]
    else:
        early = [[everyones_tokens], [messages], [out_grads, normalise]]
    early.append([from_others] + ([begin] if depth % 128 == 0 else []))
    deal()
    if dealing:
        ahead_tokens()
    rounds.turn()
    for step in range(1, far + 1):
        gather(step)
        for other in early[step - 1] if step <= len(early) else ():
            other()
        rounds.turn()
    if depth % 128:
        begin()
    first()
    rounds.turn()
    join_rest()
    rounds.turn()
    second()
    late = [
        [part(moved, range(slots)[:3])],
        [part(moved, range(slots)[3:]), token_grads],
        [part(token_sends, 1)]
        + [part(sums, "stream", bit) for bit in bits]
        + [part(sums, "seq", 1)],
        [part(sums, "seq", 2)],
    ]
    for step in range(2, far + 2):
        late_at = step - 2 if far > 4 or step < 3 else min(step - 3, 1)
        while len(late) <= late_at:
            late.append([])
        late[late_at].insert(0, part(sums_of, step))
    if dealing:
        late[2].append(part(token_part, 0, 2))
        late[3] += [part(token_part, 1, 2)]
    else:
        late[3] += [part(token_sends, bit) for bit in bits[1:]]
    late[2].append(assemble)
    late[3].append(finish)
    for step in range(1, far + 1):
        scatter(step)
        for other in late[step - 1] if step <= len(late) else ():
            other()
        rounds.turn()
    total = box["mine", far + 1][0] + box["up"].astype(f32) + box["down"].astype(f32)
    box["total"] = total[:, :width], total[:, width:]
    weight_grad = stored()
    for bit in seq_bits[2:]:
        sums("seq", bit)

    input_grad = box["input_grad"]
    outputs, final_state, summed = box["outputs"], box["states"][0], box["summed"]

    return (
        outputs,
        final_state,
        input_grad,
        weight_grad,
        summed[0],
        summed[1],
        summed[2],
        summed[3],
        summed[4],
        summed[5],
    )


def solution(mesh):
    return jax.shard_map(
        local,
        mesh=mesh,
        in_specs=(
            P("stream", "seq", None),
            P("stream", None),
            P("stream"),
            P("seq", "stream"),
            P(),
            P(),
            P(),
            P(),
            P(),
            P(),
            P("stream", "seq", None),
        ),
        out_specs=(
            P("stream", "seq", None),
            P("stream", "seq"),
            P("stream", "seq", None),
            P("seq", "stream"),
            P(),
            P(),
            P(),
            P(),
            P(),
            P(),
        ),
        check_vma=False,
    )
```

```python
import functools

import jax
import jax.numpy as jnp
from jax import lax
from jax.experimental import pallas as pl
from jax.experimental.pallas import tpu as pltpu
from jax.sharding import PartitionSpec as P

epsilon = 1e-05
f32 = jnp.float32
bf16 = jnp.bfloat16
PAD = 8
STEP = 256
ROOM = 5 * 512 * 1024


def vmem_spec():
    return pl.BlockSpec(memory_space=pltpu.VMEM)


def smem_spec():
    return pl.BlockSpec(memory_space=pltpu.SMEM)


def call(kernel, out_shape, operands, scratch=(), scalars=0, pinned=True):
    held = jax.tree.map(lambda out: pltpu.VMEM(out.shape, out.dtype), out_shape)
    return pl.pallas_call(
        kernel,
        out_shape=held if pinned else out_shape,
        in_specs=[smem_spec()] * scalars + [vmem_spec()] * (len(operands) - scalars),
        out_specs=jax.tree.map(lambda _: vmem_spec(), out_shape),
        scratch_shapes=list(scratch),
        compiler_params=pltpu.CompilerParams(vmem_limit_bytes=lax.axis_size("stream") * ROOM),
        cost_estimate=pl.CostEstimate(flops=0, bytes_accessed=0, transcendentals=0),
    )(
        *operands[:scalars],
        *[pltpu.with_memory_space_constraint(x, pltpu.VMEM) for x in operands[scalars:]],
    )


def at_spot(spot, count):
    if count != 8:
        return spot
    return spot * 2 if isinstance(spot, int) and spot < 4 else (
        15 - spot * 2 if isinstance(spot, int) else jnp.where(spot < 4, spot * 2, 15 - spot * 2)
    )


def spot_of(index, count):
    if count != 8:
        return index
    return jnp.where(index % 2 == 0, index // 2, (15 - index) // 2)


def wrapped(value, count):
    value = jnp.where(value >= count, value - count, value)
    return jnp.where(value < 0, value + count, value)


def along_ring(value, steps):
    count = lax.axis_size("seq")
    order = [at_spot(i, count) for i in range(count)]
    return lax.ppermute(value, "seq", [(order[i], order[(i + steps) % count]) for i in range(count)])


def cut(array, start, size, axis):
    starts = [jnp.int32(0)] * array.ndim
    sizes = list(array.shape)
    starts[axis], sizes[axis] = start, size
    return lax.dynamic_slice(array, starts, sizes, allow_negative_indices=False)


def pasted(array, piece, start, axis):
    starts = [jnp.int32(0)] * array.ndim
    starts[axis] = start
    return lax.dynamic_update_slice(array, piece, starts, allow_negative_indices=False)


def swapped(value, axis, bit):
    return lax.ppermute(value, axis, [(i, i ^ bit) for i in range(lax.axis_size(axis))])


def norm_kernel(parts, rows, tail, units, place, *refs):
    flat = sum(len(slot) for slot in parts)
    pieces = refs[:flat]
    gain, bias, normed, means, scales, picked = refs[flat:]
    gain_row, bias_row = gain[...], bias[...]
    lanes = pl.ds(pl.multiple_of(place[2], units), units)
    at = 0
    for k, slot in enumerate(parts):
        for low, high in slot:
            x = pieces[at][...].astype(f32)
            mean = jnp.mean(x, axis=1, keepdims=True)
            centered = x - mean
            scale = lax.rsqrt(jnp.mean(centered * centered, axis=1, keepdims=True) + epsilon)
            base = k * (rows + tail)
            normed[base + low : base + high, :] = (centered * scale * gain_row + bias_row).astype(bf16)
            count = min(high, rows) - low
            here = slice(k * rows + low, k * rows + low + count)
            means[here, :] = jnp.broadcast_to(mean[:count], (count, 128))
            scales[here, :] = jnp.broadcast_to(scale[:count], (count, 128))
            picked[here, :] = pieces[at][:count, lanes]
            at += 1


def strided(ref, row, seqs, stride, low=0, count=None):
    count = ref.shape[0] if count is None else count
    tiles = [ref[low + lane, pl.ds(row, seqs, stride=stride), :] for lane in range(count)]
    return jnp.concatenate(tiles, axis=1)


def put_strided(ref, row, seqs, stride, value, low=0):
    for lane in range(value.shape[1] // 128):
        ref[low + lane, pl.ds(row, seqs, stride=stride), :] = value[:, lane * 128 : (lane + 1) * 128]


def put_rows(ref, row, count, value, low=0):
    for lane in range(value.shape[1] // 128):
        ref[low + lane, pl.ds(row, count), :] = value[:, lane * 128 : (lane + 1) * 128]


def get_rows(ref, row, count):
    return jnp.concatenate([ref[lane, pl.ds(row, count), :] for lane in range(ref.shape[0])], axis=1)


def message_kernel(slots, units, tail, where, grads, start, lengths, *outs):
    rows, per = grads.shape[0], start.shape[0]
    for k in range(slots):
        lanes = pl.ds(pl.multiple_of(where[k], units), units)
        outs[k][:rows, :] = grads[:, lanes]
        left = start[:, lanes]
        extra = []
        for _ in range(3):
            part = left.astype(bf16).astype(f32)
            extra.append(part)
            left = left - part
        counts = lengths[...]
        high = counts // 256
        extra += [
            jnp.broadcast_to(n.astype(f32)[:, :1], (per, units)) for n in (high, counts - high * 256)
        ]
        extra.append(jnp.zeros((tail - 5 * per, units), f32))
        outs[k][rows:, :] = jnp.concatenate(extra, axis=0).astype(bf16)


def merge_kernel(cuts, mine_up, mine_down, up, down, *outs):
    count, total = up.shape[0], mine_up.shape[0]
    first, last = slice(0, count), slice(total - count, total)
    for n, (low, high) in enumerate(cuts):
        lanes = slice(low, high)
        out_up, out_down = outs[2 * n], outs[2 * n + 1]
        out_up[first, :] = (mine_up[first, lanes] + up[:, lanes].astype(f32)).astype(bf16)
        out_down[last, :] = (mine_down[last, lanes] + down[:, lanes].astype(f32)).astype(bf16)
        if count < total:
            out_up[count:, :] = mine_up[count:, lanes].astype(bf16)
            out_down[: total - count, :] = mine_down[: total - count, lanes].astype(bf16)


def assemble_kernel(slots, width, where, *refs):
    for k in range(slots):
        lanes = pl.ds(pl.multiple_of(where[k], width), width)
        for which in range(2):
            refs[slots + which][:, :, lanes] = refs[k][which]


def spread_rows(dims, low, width, g_in, picked, gs, xs):
    seqs, span, slots = dims
    per, lane = seqs // slots, low // 128
    for n in range(seqs):
        to, lanes = n * (span + PAD) + PAD, slice(low, low + width)
        at = n % per * span
        put_rows(gs, to, span, g_in[n // per][at : at + span, lanes].astype(f32), lane)
        put_rows(xs, to, span, picked[n * span : (n + 1) * span, lanes].astype(f32), lane)


def joined(refs):
    return refs[0][...] if len(refs) == 1 else jnp.concatenate([ref[...] for ref in refs], axis=0)


def begin_kernel(blocks, depth, rows, count, sources, normed, *refs):
    total = refs[blocks]
    for k in range(count):
        here = slice(k * rows, (k + 1) * rows)
        sum_ = None
        for b in range(blocks):
            at = pl.multiple_of(sources[b] * depth, depth)
            term = jnp.dot(normed[here, pl.ds(at, depth)], refs[b][...], preferred_element_type=f32)
            sum_ = term if sum_ is None else sum_ + term
        total[here, :] = sum_


def first_kernel(dims, sources, place, normed, start, lens, v0, v1, v2, v3, picked, begun, *refs):
    vecs = (v0, v1, v2, v3)
    seqs, span, width, slots, blocks, depth, late, tail = dims
    stride = span + PAD
    g_in = refs[late : late + slots]
    fields, known, scans, maps, planes = refs[late + slots :]
    cand, forg, rese = (fields.at[i] for i in range(3))
    gs, xs, products, sums = known.at[0], known.at[1], scans.at[0], scans.at[1]
    per = seqs // slots
    rows = per * span
    ext = rows + tail
    at = pl.multiple_of(sources[blocks - 1] * depth, depth)
    lead = joined(refs[:late])
    for k in range(slots):
        here = slice(k * ext, (k + 1) * ext)
        for piece in range(3):
            field = fields.at[place[3 + piece]]
            columns = slice(piece * width, (piece + 1) * width)
            total = begun[here, columns] + jnp.dot(
                normed[here, pl.ds(at, depth)], lead[:, columns], preferred_element_type=f32
            )
            total = total.astype(bf16).astype(f32)
            for j in range(per):
                to = (k * per + j) * stride + PAD
                before = jnp.broadcast_to(total[rows + j : rows + j + 1, :], (8, width))
                put_rows(field, to - 8, 8, before)
                put_rows(field, to, span, total[j * span : (j + 1) * span, :])
    before = jnp.where(place[1] == 0, start[...], strided(cand, PAD - 1, seqs, stride))
    put_strided(cand, PAD - 1, seqs, stride, before)
    ends = lens[...]
    base = place[0]
    step = min(width, STEP)
    ends = ends[:, :step]
    for low in range(0, width, step):
        units = slice(low, low + step)
        lane, lanes = low // 128, step // 128
        spread_rows((seqs, span, slots), low, step, g_in, picked, gs, xs)
        own = pl.ds(pl.multiple_of(place[2] + low, 128), step)
        peep_f, peep_r, bias_f, bias_r = (row[:, own] for row in vecs)

        def turn(t, carry):
            previous, decays, injects, handed = carry
            row = t + PAD
            c, f, r = (strided(ref, row, seqs, stride, lane, lanes) for ref in (cand, forg, rese))
            f = jax.nn.sigmoid(f + peep_f * previous + bias_f)
            r = jax.nn.sigmoid(r + peep_r * previous + bias_r)
            put_strided(forg, row, seqs, stride, f, lane)
            put_strided(rese, row, seqs, stride, r, lane)
            live = base + t < ends
            d = jnp.where(live, f, 1.0)
            inject = jnp.where(live, (1.0 - f) * c, 0.0)
            pulled = jnp.where(live, r * strided(gs, row, seqs, stride, lane, lanes), 0.0)
            decays, injects = decays * d, d * injects + inject
            put_strided(products, row, seqs, stride, decays, lane)
            put_strided(sums, row, seqs, stride, injects, lane)
            return c, decays, injects, handed + decays * pulled

        one, zero = jnp.ones((seqs, step), f32), jnp.zeros((seqs, step), f32)
        put_strided(products, PAD - 1, seqs, stride, one, lane)
        put_strided(sums, PAD - 1, seqs, stride, zero, lane)
        _, decays, injects, handed = lax.fori_loop(
            0, span, turn, (before[:, units], one, zero, zero), unroll=8
        )
        maps[0, :, units], maps[1, :, units], maps[2, :, units] = decays, injects, handed
        c, f, r, g, x = (
            strided(ref, PAD, seqs, stride, lane, lanes) for ref in (cand, forg, rese, gs, xs)
        )
        live = base < ends
        d = jnp.where(live, f, 1.0)
        inject = jnp.where(live, (1.0 - f) * c, 0.0)
        via_adjoint = jnp.where(live, (1.0 - f) * peep_f, 0.0)
        via_state = jnp.where(live, r * (1.0 - r) * g * peep_r, 0.0)
        planes[0, :, units], planes[1, :, units] = via_adjoint, via_adjoint * c
        planes[2, :, units], planes[3, :, units] = via_state * d, via_state * (inject - x)


def second_kernel(
    dims, place, lens, v0, v1, earlier, later, start, linked, fields, known, scans, *refs
):
    vecs = (v0, v1)
    seqs, span, width, slots, tail = dims
    stride = span + PAD
    grads, moved = refs[0], refs[1 : slots + 1]
    final, sums, outs, directs, gcs, fts, rts = refs[slots + 1 :]
    cand, forg, rese = (fields.at[i] for i in range(3))
    gs, xs, products, injected = known.at[0], known.at[1], scans.at[0], scans.at[1]
    per = seqs // slots
    base = place[0]
    step = min(width, STEP)
    ends = lens[:, :step]
    sums[...] = jnp.zeros_like(sums)
    for k in range(slots):
        to = k * (per * span + tail) + per * span
        grads[to : to + tail, :] = jnp.zeros((tail, 3 * width), bf16)
    for low in range(0, width, step):
        units = slice(low, low + step)
        lane, lanes = low // 128, step // 128
        own = pl.ds(pl.multiple_of(place[2] + low, 128), step)
        peep_f, peep_r = (row[:, own] for row in vecs)
        begin = earlier[0, :, units] * start[:, units] + earlier[1, :, units]
        after = later[2, :, units]

        def token(ref, row):
            return strided(ref, row, seqs, stride, lane, lanes)

        def state_at(row):
            return token(products, row) * begin + token(injected, row)

        end = state_at(span - 1 + PAD)
        final[:, units] = later[0, :, units] * end + later[1, :, units]
        link = [linked[i, :, units] for i in range(4)]
        upcoming = end * (link[0] * after + link[2]) - link[1] * after + link[3]

        def backward(i, carry):
            reached, upcoming, state, c, pf, pr, bf, br = carry
            row = span - 1 - i + PAD
            f, r, x, g = (token(ref, row) for ref in (forg, rese, xs, gs))
            prior, previous = state_at(row - 1), token(cand, row - 1)
            live = base + (span - 1 - i) < ends
            zero = jnp.zeros_like(f)
            pulled = r * g
            adjoint = jnp.where(live, pulled, zero) + reached
            kept = jnp.where(live, (1.0 - f) * adjoint, zero)
            ft = f * kept * (prior - c)
            change = r * (state - x)
            rt = jnp.where(live, (1.0 - r) * g * change, zero)
            put_strided(gcs, row, seqs, stride, kept + upcoming)
            put_strided(fts, row, seqs, stride, ft)
            put_strided(rts, row, seqs, stride, rt)
            put_strided(outs, row, seqs, stride, jnp.where(live, r * state + (1.0 - r) * x, x))
            put_strided(directs, row, seqs, stride, jnp.where(live, (1.0 - r) * g, g))
            reached = jnp.where(live, f * adjoint, adjoint)
            return (
                reached,
                ft * peep_f + rt * peep_r,
                prior,
                previous,
                pf + ft * previous,
                pr + rt * previous,
                bf + ft,
                br + rt,
            )

        zero = jnp.zeros((seqs, step), f32)
        last = token(cand, span - 1 + PAD)
        done = lax.fori_loop(
            0, span, backward, (after, upcoming, end, last, zero, zero, zero, zero), unroll=4
        )
        for i in range(4):
            sums[i : i + 1, units] = jnp.sum(done[4 + i], axis=0, keepdims=True)
        for n in range(seqs):
            at = n * stride + PAD
            k, j = n // per, n % per
            to = k * (per * span + tail) + j * span
            for gate, ref in enumerate((gcs, fts, rts)):
                here = slice(gate * width + low, gate * width + low + step)
                grads[to : to + span, here] = get_rows(ref, at, span).astype(bf16)
            moved[k][0, j, :, units] = get_rows(outs, at, span).astype(bf16)
            moved[k][1, j, :, units] = get_rows(directs, at, span).astype(bf16)


def partial_kernel(distances, depth, width, owners, place, normed, grads, *outs):
    for i, distance in enumerate(distances):
        lanes = pl.ds(pl.multiple_of(owners[distance] * depth, min(depth, 128)), depth)
        columns = normed[:, lanes]
        for piece in range(3):
            gate = pl.ds(pl.multiple_of(place[3 + piece] * width, width), width)
            sum_ = lax.dot_general(
                columns, grads[:, gate], (((0,), (0,)), ((), ())), preferred_element_type=f32
            )
            here = slice(piece * width, (piece + 1) * width)
            split = len(outs) // len(distances)
            count = depth // split
            for n in range(split):
                outs[split * i + n][:, here] = sum_[n * count : (n + 1) * count].astype(outs[0].dtype)


def token_kernel(dims, parts, sources, place, grads, gate_sums, *refs):
    slots, blocks, depth, rows, width, split, tail = dims
    flat = sum(len(slot) for slot in parts)
    n_w = blocks + (1 if split else 0)
    pieces = refs[n_w : n_w + flat]
    means, scales, own = refs[n_w + flat : n_w + flat + 3]
    others = refs[n_w + flat + 3 : n_w + flat + slots + 2]
    sums = refs[n_w + flat + slots + 2]
    first_of = [sum(len(slot) for slot in parts[:k]) for k in range(slots)]

    def raw(k, lanes):
        found = [
            pieces[first_of[k] + i][: min(high, rows) - low, lanes]
            for i, (low, high) in enumerate(parts[k])
        ]
        return found[0] if len(found) == 1 else jnp.concatenate(found, axis=0)

    def block(b):
        return joined(refs[b : b + 2] if split and b == blocks - 1 else refs[b : b + 1])

    sums[...] = jnp.zeros_like(sums)
    sums[:4, pl.ds(pl.multiple_of(place[2], width), width)] = gate_sums[:4, :]
    for b in range(blocks):
        at = pl.multiple_of(sources[b] * depth, depth)
        lanes = pl.ds(at, depth)
        gain_sum, bias_sum = jnp.zeros((8, depth), f32), jnp.zeros((8, depth), f32)
        weights = block(b)
        for k in range(slots):
            here = pl.ds(k * rows, rows)
            total = None
            for piece in range(3):
                gate = pl.ds(pl.multiple_of(place[3 + piece] * width, width), width)
                term = lax.dot_general(
                    grads[k * (rows + tail) : k * (rows + tail) + rows, gate],
                    weights[:, piece * width : (piece + 1) * width],
                    (((1,), (1,)), ((), ())),
                    preferred_element_type=f32,
                )
                total = term if total is None else total + term
            copies = depth // 128
            mean = jnp.concatenate([means[here, :]] * copies, axis=1)
            scale = jnp.concatenate([scales[here, :]] * copies, axis=1)
            scaled = (raw(k, lanes).astype(f32) - mean) * scale
            gain_sum += jnp.sum((total * scaled).reshape(rows // 8, 8, depth), axis=0)
            bias_sum += jnp.sum(total.reshape(rows // 8, 8, depth), axis=0)
            if k == 0:
                own[:, lanes] = total
            else:
                others[k - 1][:, lanes] = total.astype(bf16)
        sums[4:5, lanes] = jnp.sum(gain_sum, axis=0, keepdims=True)
        sums[5:6, lanes] = jnp.sum(bias_sum, axis=0, keepdims=True)


def first_maps(maps):
    one, zero = jnp.ones_like(maps[0]), jnp.zeros_like(maps[0])
    return (maps[0], maps[1], maps[2]), (one, zero), (one, zero, zero)


def joined_maps(known, other, first):
    (decay, inject, handed), before, later = known
    theirs = (other[0], other[1], other[2])
    before_new = (theirs[0] * before[0], before[0] * theirs[1] + before[1])
    later_new = (
        later[0] * theirs[0],
        theirs[0] * later[1] + theirs[1],
        later[2] + later[0] * theirs[2],
    )
    before = tuple(jnp.where(first, a, b) for a, b in zip(before, before_new))
    later = tuple(jnp.where(first, b, a) for a, b in zip(later, later_new))
    inject_new = jnp.where(first, theirs[0] * inject + theirs[1], decay * theirs[1] + inject)
    handed_new = jnp.where(first, handed + decay * theirs[2], theirs[2] + theirs[0] * handed)
    return (decay * theirs[0], inject_new, handed_new), before, later


class Rounds:
    def __init__(self):
        self.before, self.given = [], []

    def take(self, value):
        if not self.before:
            return value
        return lax.optimization_barrier((value, self.before))[0]

    def give(self, *values):
        self.given += values

    def turn(self):
        self.before, self.given = self.given, []


def local(
    inputs,
    start_state,
    lengths,
    weights,
    peep_forget,
    peep_reset,
    bias_forget,
    bias_reset,
    norm_gain,
    norm_bias,
    out_grad,
):
    per, span, model = inputs.shape
    n_seq, slots = lax.axis_size("seq"), lax.axis_size("stream")
    at_seq, at_stream = lax.axis_index("seq"), lax.axis_index("stream")
    seqs = per * slots
    width = model // slots
    depth = model // n_seq
    rows = per * span
    tokens = seqs * span
    tail = 16
    half = depth // 2
    spot = spot_of(at_seq, n_seq)
    far = n_seq // 2
    steps = [0]
    for k in range(1, far):
        steps += [-k, k]
    steps.append(far)
    dealing = slots == 4

    def owner(distance):
        return at_spot(wrapped(spot + distance, n_seq), n_seq)

    def per_stream(table):
        found = table[0]
        for d in range(1, len(table)):
            found = jnp.where(at_stream == d, table[d], found)
        return found

    gates = ((0, 1, 2), (1, 0, 2), (1, 2, 0), (2, 1, 0)) if dealing else ((0, 1, 2),)
    gate_of = [per_stream([table[piece] for table in gates]) for piece in range(3)]
    bits = [1 << b for b in range(slots.bit_length() - 1)]
    seq_bits = [1 << b for b in range(n_seq.bit_length() - 1)]
    share = model // n_seq
    index = {
        "sources": jnp.stack([owner(distance) for distance in steps]).astype(jnp.int32),
        "place": jnp.stack([at_seq * span, at_seq, at_stream * width, *gate_of]).astype(jnp.int32),
        "owners": jnp.stack([owner(distance) for distance in range(n_seq)]).astype(jnp.int32),
        "where": jnp.stack([(at_stream ^ k) * width for k in range(slots)]).astype(jnp.int32),
        "lanes": [(at_stream ^ k) * width for k in range(slots)],
        "rows": [(at_stream ^ k) * per for k in range(slots)],
        "first": [(at_seq & bit) == 0 for bit in seq_bits],
        "even": at_stream % 2 == 0,
        "share": at_seq * share % width,
        "holds": at_stream == at_seq * share // width,
    }
    index, inputs, weights, out_grad, start_state, lengths = lax.optimization_barrier(
        (index, inputs, weights, out_grad, start_state, lengths)
    )
    sources, place, even = index["sources"], index["place"], index["even"]

    vectors = [
        row.reshape(1, model) for row in (peep_forget, peep_reset, bias_forget, bias_reset)
    ]
    gain_row, bias_row = norm_gain.reshape(1, model), norm_bias.reshape(1, model)
    tall = seqs * (span + PAD)
    fields, two = (jax.ShapeDtypeStruct((n, width // 128, tall, 128), f32) for n in (3, 2))
    space = pltpu.VMEM((min(width, STEP) // 128, tall, 128), f32)

    rounds = Rounds()
    take, give = rounds.take, rounds.give
    box = {}

    def deal():
        if dealing:
            pieces = [weights[:, i * width : (i + 1) * width] for i in range(3)]
            own = jnp.where(even, pieces[0], pieces[2])
            near = swapped(pieces[1], "stream", 1)
            distant = swapped(jnp.where(even, pieces[2], pieces[0]), "stream", 2)
            box["dealt"] = jnp.concatenate([own, near, distant], axis=1)
            give(near, distant)
            return
        everything = lax.all_gather(weights, "stream", axis=1, tiled=True)
        found = [
            lax.dynamic_slice_in_dim(everything, gate * model + at_stream * width, width, 1)
            for gate in range(3)
        ]
        box["dealt"] = jnp.concatenate(found, axis=1)

    def last_columns():
        came = box["came"]
        rest = box["mine", far + 1][0][:, width:] + came[0].astype(f32) + came[1].astype(f32)
        box["rest"] = rest[:, :width], rest[:, width:]
        if dealing:
            near, distant = (part_of.astype(bf16) for part_of in box["rest"])
            box["distant"] = swapped(distant, "stream", 2)
            box["near"] = swapped(near, "stream", 1)
            rounds.before = [*rounds.before, distant, near]

    def stored():
        came = box["came"]
        own = box["mine", far + 1][0][:, :width] + came[2].astype(f32) + came[3].astype(f32)
        if dealing:
            distant, near = box["distant"].astype(f32), box["near"].astype(f32)
            found = [jnp.where(even, own, distant), near, jnp.where(even, distant, own)]
        else:
            flat = lax.all_gather(
                jnp.concatenate([own, *box["rest"]], axis=1).astype(bf16), "stream", axis=0
            ).astype(f32)
            flat = jnp.swapaxes(flat.reshape(slots, depth, 3, width), 0, 2)
            flat = jnp.swapaxes(flat, 1, 2).reshape(3 * slots, depth, width)
            found = [
                lax.dynamic_index_in_dim(flat, 3 * at_stream + i, 0, keepdims=False)
                for i in range(3)
            ]
        return jnp.concatenate(found, axis=1)

    def gather(step):
        if step == 1:
            box["up"] = box["down"] = take(box["dealt"])
            box["blocks"] = [box["dealt"]]
        if step == far:
            box["up"], box["down"] = box["up"][:half], box["down"][half:]
        box["up"] = along_ring(take(box["up"]), 1)
        box["down"] = along_ring(take(box["down"]), -1)
        box["blocks"] += [box["up"], box["down"]]
        give(box["up"], box["down"])

    def partials(distances, kind, split=1):
        grads = take(box["grads"])
        if depth % 128:
            found = []
            for distance in distances:
                at = owner(distance)
                sum_ = lax.dot_general(
                    lax.dynamic_slice_in_dim(box["normed"], at * depth, depth, 1),
                    grads,
                    (((0,), (0,)), ((), ())),
                    preferred_element_type=f32,
                ).astype(kind)
                found += [sum_[n * depth // split :][: depth // split] for n in range(split)]
            return found
        return call(
            functools.partial(
                partial_kernel, [distance % n_seq for distance in distances], depth, width
            ),
            [jax.ShapeDtypeStruct((depth // split, 3 * width), kind)] * (split * len(distances)),
            [index["owners"], place, box["normed"], grads],
            scalars=2,
        )

    def scatter(step):
        cuts_of = [(width, 3 * width), (0, width)] if step == far else [(0, 3 * width)]
        if step == 1:
            sent = box["farthest"]
        else:
            sent = call(
                functools.partial(merge_kernel, cuts_of),
                [jax.ShapeDtypeStruct((depth, b - a), bf16) for a, b in cuts_of for _ in range(2)],
                [*box["mine", step], box["up"], box["down"]],
            )
        came = [along_ring(take(value), 1 - 2 * (i % 2)) for i, value in enumerate(sent)]
        rounds.before = [*rounds.before, *sent]
        box["up"], box["down"] = came[:2]
        box["came"] = came
        give(*came)

    def sums_of(step):
        distance = far + 1 - step
        box["mine", step] = partials((distance, -distance) if distance else (0,), f32)
        give(*box["mine", step])

    whole_part = [(0, rows + tail)]
    cuts = [(0, rows // 2), (rows // 2, rows + tail)]
    parts = [whole_part, whole_part, cuts, cuts] if dealing else [whole_part] * slots
    tokens_of = [[None] * len(slot) for slot in parts]
    flat_inputs = inputs.reshape(rows, model)

    def ahead_tokens():
        box["ahead"] = lax.ppermute(
            take(inputs[:, -1, :]), "seq", [(i, i + 1) for i in range(n_seq - 1)]
        )
        give(box["ahead"])

    def own_tokens():
        tokens_of[0][0] = jnp.concatenate(
            [flat_inputs, box["ahead"], jnp.zeros((tail - per, model), bf16)], axis=0
        )

    def everyones_tokens():
        ahead_tokens()
        own_tokens()
        for bit in reversed(bits):
            for k in range(slots):
                if tokens_of[k][0] is not None and tokens_of[k ^ bit][0] is None:
                    tokens_of[k ^ bit][0] = swapped(tokens_of[k][0], "stream", bit)

    def near_tokens():
        own_tokens()
        tokens_of[1][0] = swapped(take(tokens_of[0][0]), "stream", 1)
        give(tokens_of[1][0])

    def far_tokens(i):
        low, high = cuts[i]
        source = flat_inputs[low:high] if high <= rows else tokens_of[0][0][low:high]
        tokens_of[2][i] = swapped(take(source), "stream", 2)
        give(tokens_of[2][i])

    def passed_tokens(i):
        tokens_of[3][i] = swapped(take(tokens_of[2][i]), "stream", 1)
        give(tokens_of[3][i])

    def messages():
        box["messages"] = call(
            functools.partial(message_kernel, slots, width, tail),
            [jax.ShapeDtypeStruct((rows + tail, width), bf16)] * slots,
            [
                index["where"],
                take(out_grad.reshape(rows, model)),
                start_state,
                jnp.broadcast_to(lengths[:, None], (per, 128)),
            ],
            scalars=1,
        )

    def out_grads():
        for k in range(slots):
            box["g", k] = box["messages"][k]
            if k:
                box["g", k] = swapped(take(box["g", k]), "stream", k)
                give(box["g", k])

    def normalise():
        flat = [piece for slot in tokens_of for piece in slot]
        box["normed"], box["means"], box["scales"], box["picked"] = call(
            functools.partial(norm_kernel, parts, rows, tail, width),
            [
                jax.ShapeDtypeStruct((slots * (rows + tail), model), bf16),
                jax.ShapeDtypeStruct((tokens, 128), f32),
                jax.ShapeDtypeStruct((tokens, 128), f32),
                jax.ShapeDtypeStruct((tokens, width), bf16),
            ],
            [place, *flat, take(gain_row), bias_row],
            scalars=1,
        )
        give(box["normed"])

    def from_others():
        extra = [box["g", k][rows : rows + 5 * per].astype(f32) for k in range(slots)]
        extra = [x.reshape(5, per, width) for x in extra]
        box["start"] = jnp.concatenate([x[0] + x[1] + x[2] for x in extra], axis=0)
        ends = jnp.concatenate([x[3] * 256 + x[4] for x in extra], axis=0)
        box["ends"] = ends.astype(jnp.int32)

    def in_order():
        if depth % 128 == 0:
            return box["blocks"], sources, n_seq, depth, True
        deep = 2 * 128
        if "whole" not in box:
            whole = jnp.zeros((model, 3 * width), bf16)
            for b, block in enumerate(box["blocks"]):
                at = owner(steps[min(b, n_seq - 1)]) * depth + (half if b == n_seq else 0)
                whole = lax.dynamic_update_slice_in_dim(whole, block, at, 0)
            box["whole"] = [whole[i : i + deep] for i in range(0, model, deep)]
        count = model // deep
        return box["whole"], jnp.arange(count, dtype=jnp.int32), count, deep, False

    def begin():
        held, places, count, deep, _ = in_order()
        box["begun"] = call(
            functools.partial(begin_kernel, count - 1, deep, rows + tail, slots),
            jax.ShapeDtypeStruct((slots * (rows + tail), 3 * width), f32),
            [places, take(box["normed"]), *held[: count - 1]],
            scalars=1,
        )
        give(box["begun"])

    def first():
        held, places, count, deep, split = in_order()
        *box["fields"], maps, planes = call(
            functools.partial(
                first_kernel, (seqs, span, width, slots, count, deep, 2 if split else 1, tail)
            ),
            [
                fields,
                two,
                two,
                jax.ShapeDtypeStruct((3, seqs, width), f32),
                jax.ShapeDtypeStruct((4, seqs, width), f32),
            ],
            [
                places,
                place,
                box["normed"],
                box["start"],
                take(box["ends"]),
                *vectors,
                box["picked"],
                box["begun"],
                *held[count - 1 :],
                *[box["g", k] for k in range(slots)],
            ],
            scalars=2,
        )
        box["linked"] = lax.ppermute(planes, "seq", [(i + 1, i) for i in range(n_seq - 1)])
        box["known"], box["maps"] = first_maps(maps), maps
        join(1)

    def join(bit):
        mine = box["maps"] if bit == 1 else take(jnp.stack(box["known"][0]))
        other = swapped(mine, "seq", bit)
        give(other)
        box["known"] = joined_maps(box["known"], other, index["first"][seq_bits.index(bit)])

    def join_rest():
        bit = 2
        while bit < n_seq:
            join(bit)
            bit *= 2

    def second():
        _, earlier, later = box["known"]
        out = call(
            functools.partial(second_kernel, (seqs, span, width, slots, tail)),
            [
                jax.ShapeDtypeStruct((slots * (rows + tail), 3 * width), bf16),
                *[jax.ShapeDtypeStruct((2, per, span, width), bf16)] * slots,
                jax.ShapeDtypeStruct((seqs, width), f32),
                jax.ShapeDtypeStruct((8, width), f32),
            ],
            [
                place,
                take(box["ends"]),
                *vectors[:2],
                jnp.stack(earlier),
                jnp.stack(later),
                box["start"],
                box["linked"],
                *box["fields"],
            ],
            scratch=[space] * 5,
            scalars=1,
        )
        box["grads"], box["moving"] = out[0], out[1 : slots + 1]
        box["final"], box["sums"] = out[slots + 1], out[slots + 2]
        rounds.before = []
        box["farthest"] = partials((far,), bf16, 2)
        box["grads"] = lax.optimization_barrier((box["grads"], box["farthest"]))[0]

    def moved(among):
        for k in among:
            box["moved", k] = box["moving"][k]
            if k:
                box["moved", k] = swapped(take(box["moving"][k]), "stream", k)
                give(box["moved", k])

    def token_grads():
        held, places, count, deep, split = in_order()
        out = call(
            functools.partial(
                token_kernel, (slots, count, deep, rows, width, split, tail), parts
            ),
            [
                jax.ShapeDtypeStruct((rows, model), f32),
                *[jax.ShapeDtypeStruct((rows, model), bf16)] * (slots - 1),
                jax.ShapeDtypeStruct((8, model), f32),
            ],
            [
                places,
                place,
                take(box["grads"]),
                box["sums"],
                *held,
                *[piece for slot in tokens_of for piece in slot],
                box["means"],
                box["scales"],
            ],
            scalars=2,
        )
        box["kept"] = {k: out[k] for k in range(slots)}
        box["summed"] = out[slots]
        give(out[0])

    def token_sends(bit):
        kept = box["kept"]
        for k in sorted(kept, reverse=True):
            if k & bit:
                got = swapped(take(kept.pop(k).astype(bf16)), "stream", bit)
                kept[k ^ bit] = kept[k ^ bit].astype(f32) + got.astype(f32)
                give(got)

    def token_part(i, count):
        if i == 0:
            box["sending"] = box["kept"].pop(2).astype(bf16)
            box["arrived"] = []
        low, high = rows * i // count // 16 * 16, rows * (i + 1) // count // 16 * 16
        box["arrived"].append(swapped(take(box["sending"][low:high]), "stream", 2))
        give(box["arrived"][i])
        if i + 1 == count:
            box["kept"][0] = box["kept"][0] + jnp.concatenate(box["arrived"], axis=0).astype(f32)

    def sums(axis, bit):
        if "states" not in box:
            mine = jnp.where(index["holds"], cut(box["final"], index["share"], share, 1), 0.0)
            box["states"] = {k: mine[k * per : (k + 1) * per] for k in range(slots)}
        states, summed = box["states"], box["summed"][:6]
        going = [k for k in sorted(states) if k & bit] if axis == "stream" else []
        if going:
            row = jnp.concatenate([states[k] for k in going], axis=1)
            row = jnp.pad(row, ((0, 0), (0, model - row.shape[1])))
            summed = jnp.concatenate([summed, row], axis=0)
        got = swapped(take(summed), axis, bit)
        give(got)
        box["summed"] = box["summed"][:6] + got[:6]
        for i, k in enumerate(going):
            states.pop(k)
            states[k ^ bit] = states[k ^ bit] + got[6:, i * share : (i + 1) * share]

    def assemble():
        box["outputs"], box["direct"] = found = call(
            functools.partial(assemble_kernel, slots, width),
            [jax.ShapeDtypeStruct((per, span, model), bf16)] * 2,
            [index["where"], *[take(box["moved", k]) for k in range(slots)]],
            scalars=1,
            pinned=False,
        )
        give(*found)
        give(*found)

    def finish():
        grad_normed = box["kept"][0]
        source = inputs.astype(f32).reshape(rows, model)
        scale = take(box["scales"])[:rows, :1]
        scaled = (source - box["means"][:rows, :1]) * scale
        grad_scaled = grad_normed * norm_gain
        grad_source = scale * (
            grad_scaled
            - jnp.mean(grad_scaled, axis=1, keepdims=True)
            - scaled * jnp.mean(grad_scaled * scaled, axis=1, keepdims=True)
        )
        box["input_grad"] = (grad_source.reshape(per, span, model) + box["direct"].astype(f32)).astype(bf16)
        give(box["input_grad"])

    part = functools.partial
    if dealing:
        early = [
            [part(far_tokens, 0)],
            [near_tokens, part(far_tokens, 1), part(passed_tokens, 0), messages],
            [part(passed_tokens, 1), out_grads, normalise],
        ]
    else:
        early = [[everyones_tokens], [messages], [out_grads, normalise]]
    early.append([from_others] + ([begin] if depth % 128 == 0 else []))
    deal()
    if dealing:
        ahead_tokens()
    rounds.turn()
    for step in range(1, far + 1):
        gather(step)
        for other in early[step - 1] if step <= len(early) else ():
            other()
        rounds.turn()
    if depth % 128:
        begin()
    first()
    rounds.turn()
    join_rest()
    rounds.turn()
    second()
    late = [
        [part(moved, range(slots)[:3])],
        [part(moved, range(slots)[3:]), token_grads],
        [part(token_sends, 1)]
        + [part(sums, "stream", bit) for bit in bits]
        + [part(sums, "seq", 1)],
        [part(sums, "seq", 2)],
    ]
    for step in range(2, far + 2):
        late_at = step - 2 if far > 4 or step < 3 else min(step - 3, 1)
        while len(late) <= late_at:
            late.append([])
        late[late_at].insert(0, part(sums_of, step))
    if dealing:
        late[2].append(part(token_part, 0, 2))
        late[3].insert(0, part(token_part, 1, 2))
    else:
        late[3] += [part(token_sends, bit) for bit in bits[1:]]
    late[2].append(assemble)
    late += [[] for _ in range(far - len(late))]
    late[far - 1].insert(1, last_columns)
    for step in range(1, far + 1):
        scatter(step)
        for other in late[step - 1] if step <= len(late) else ():
            other()
        rounds.turn()
    weight_grad = stored()
    finish()
    for bit in seq_bits[2:]:
        sums("seq", bit)

    input_grad = box["input_grad"]
    outputs, final_state, summed = box["outputs"], box["states"][0], box["summed"]

    return (
        outputs,
        final_state,
        input_grad,
        weight_grad,
        summed[0],
        summed[1],
        summed[2],
        summed[3],
        summed[4],
        summed[5],
    )


def solution(mesh):
    return jax.shard_map(
        local,
        mesh=mesh,
        in_specs=(
            P("stream", "seq", None),
            P("stream", None),
            P("stream"),
            P("seq", "stream"),
            P(),
            P(),
            P(),
            P(),
            P(),
            P(),
            P("stream", "seq", None),
        ),
        out_specs=(
            P("stream", "seq", None),
            P("stream", "seq"),
            P("stream", "seq", None),
            P("seq", "stream"),
            P(),
            P(),
            P(),
            P(),
            P(),
            P(),
        ),
        check_vma=False,
    )
```

```python
import functools

import jax
import jax.numpy as jnp
from jax import lax
from jax.experimental import pallas as pl
from jax.experimental.pallas import tpu as pltpu
from jax.sharding import PartitionSpec as P

epsilon = 1e-05
f32 = jnp.float32
bf16 = jnp.bfloat16
PAD = 8
STEP = 256
ROOM = 5 * 512 * 1024


def vmem_spec():
    return pl.BlockSpec(memory_space=pltpu.VMEM)


def smem_spec():
    return pl.BlockSpec(memory_space=pltpu.SMEM)


def call(kernel, out_shape, operands, scratch=(), scalars=0, pinned=True, aliases=None):
    held = jax.tree.map(lambda out: pltpu.VMEM(out.shape, out.dtype), out_shape)
    return pl.pallas_call(
        kernel,
        out_shape=held if pinned else out_shape,
        in_specs=[smem_spec()] * scalars + [vmem_spec()] * (len(operands) - scalars),
        out_specs=jax.tree.map(lambda _: vmem_spec(), out_shape),
        scratch_shapes=list(scratch),
        input_output_aliases=aliases or {},
        compiler_params=pltpu.CompilerParams(vmem_limit_bytes=lax.axis_size("stream") * ROOM),
        cost_estimate=pl.CostEstimate(flops=0, bytes_accessed=0, transcendentals=0),
    )(
        *operands[:scalars],
        *[pltpu.with_memory_space_constraint(x, pltpu.VMEM) for x in operands[scalars:]],
    )


def at_spot(spot, count):
    if count != 8:
        return spot
    return spot * 2 if isinstance(spot, int) and spot < 4 else (
        15 - spot * 2 if isinstance(spot, int) else jnp.where(spot < 4, spot * 2, 15 - spot * 2)
    )


def spot_of(index, count):
    if count != 8:
        return index
    return jnp.where(index % 2 == 0, index // 2, (15 - index) // 2)


def wrapped(value, count):
    value = jnp.where(value >= count, value - count, value)
    return jnp.where(value < 0, value + count, value)


def along_ring(value, steps):
    count = lax.axis_size("seq")
    order = [at_spot(i, count) for i in range(count)]
    return lax.ppermute(value, "seq", [(order[i], order[(i + steps) % count]) for i in range(count)])


def cut(array, start, size, axis):
    starts = [jnp.int32(0)] * array.ndim
    sizes = list(array.shape)
    starts[axis], sizes[axis] = start, size
    return lax.dynamic_slice(array, starts, sizes, allow_negative_indices=False)


def pasted(array, piece, start, axis):
    starts = [jnp.int32(0)] * array.ndim
    starts[axis] = start
    return lax.dynamic_update_slice(array, piece, starts, allow_negative_indices=False)


def swapped(value, axis, bit):
    return lax.ppermute(value, axis, [(i, i ^ bit) for i in range(lax.axis_size(axis))])


def norm_kernel(parts, rows, tail, units, place, *refs):
    flat = sum(len(slot) for slot in parts)
    pieces = refs[:flat]
    gain, bias, normed, means, scales, picked = refs[flat:]
    gain_row, bias_row = gain[...], bias[...]
    lanes = pl.ds(pl.multiple_of(place[2], units), units)
    at = 0
    for k, slot in enumerate(parts):
        for low, high in slot:
            x = pieces[at][...].astype(f32)
            mean = jnp.mean(x, axis=1, keepdims=True)
            centered = x - mean
            scale = lax.rsqrt(jnp.mean(centered * centered, axis=1, keepdims=True) + epsilon)
            base = k * (rows + tail)
            normed[base + low : base + high, :] = (centered * scale * gain_row + bias_row).astype(bf16)
            count = min(high, rows) - low
            here = slice(k * rows + low, k * rows + low + count)
            means[here, :] = jnp.broadcast_to(mean[:count], (count, 128))
            scales[here, :] = jnp.broadcast_to(scale[:count], (count, 128))
            picked[here, :] = pieces[at][:count, lanes]
            at += 1


def strided(ref, row, seqs, stride, low=0, count=None):
    count = ref.shape[0] if count is None else count
    tiles = [ref[low + lane, pl.ds(row, seqs, stride=stride), :] for lane in range(count)]
    return jnp.concatenate(tiles, axis=1)


def put_strided(ref, row, seqs, stride, value, low=0):
    for lane in range(value.shape[1] // 128):
        ref[low + lane, pl.ds(row, seqs, stride=stride), :] = value[:, lane * 128 : (lane + 1) * 128]


def put_rows(ref, row, count, value, low=0):
    for lane in range(value.shape[1] // 128):
        ref[low + lane, pl.ds(row, count), :] = value[:, lane * 128 : (lane + 1) * 128]


def get_rows(ref, row, count):
    return jnp.concatenate([ref[lane, pl.ds(row, count), :] for lane in range(ref.shape[0])], axis=1)


def message_kernel(slots, units, tail, where, grads, start, lengths, *outs):
    rows, per = grads.shape[0], start.shape[0]
    for k in range(slots):
        lanes = pl.ds(pl.multiple_of(where[k], units), units)
        outs[k][:rows, :] = grads[:, lanes]
        left = start[:, lanes]
        extra = []
        for _ in range(3):
            part = left.astype(bf16).astype(f32)
            extra.append(part)
            left = left - part
        counts = lengths[...]
        high = counts // 256
        extra += [
            jnp.broadcast_to(n.astype(f32)[:, :1], (per, units)) for n in (high, counts - high * 256)
        ]
        extra.append(jnp.zeros((tail - 5 * per, units), f32))
        outs[k][rows:, :] = jnp.concatenate(extra, axis=0).astype(bf16)


def merge_kernel(cuts, mine_up, mine_down, up, down, *outs):
    count, total = up.shape[0], mine_up.shape[0]
    first, last = slice(0, count), slice(total - count, total)
    for n, (low, high) in enumerate(cuts):
        lanes = slice(low, high)
        out_up, out_down = outs[2 * n], outs[2 * n + 1]
        out_up[first, :] = (mine_up[first, lanes] + up[:, lanes].astype(f32)).astype(bf16)
        out_down[last, :] = (mine_down[last, lanes] + down[:, lanes].astype(f32)).astype(bf16)
        if count < total:
            out_up[count:, :] = mine_up[count:, lanes].astype(bf16)
            out_down[: total - count, :] = mine_down[: total - count, lanes].astype(bf16)


def assemble_kernel(slots, width, where, *refs):
    for k in range(slots):
        lanes = pl.ds(pl.multiple_of(where[k], width), width)
        for which in range(2):
            refs[slots + which][:, :, lanes] = refs[k][which]


def spread_rows(dims, low, width, g_in, picked, gs, xs):
    seqs, span, slots = dims
    per, lane = seqs // slots, low // 128
    for n in range(seqs):
        to, lanes = n * (span + PAD) + PAD, slice(low, low + width)
        at = n % per * span
        put_rows(gs, to, span, g_in[n // per][at : at + span, lanes].astype(f32), lane)
        put_rows(xs, to, span, picked[n * span : (n + 1) * span, lanes].astype(f32), lane)


def joined(refs):
    return refs[0][...] if len(refs) == 1 else jnp.concatenate([ref[...] for ref in refs], axis=0)


def begin_kernel(blocks, depth, rows, count, sources, normed, *refs):
    total = refs[blocks]
    for k in range(count):
        here = slice(k * rows, (k + 1) * rows)
        sum_ = None
        for b in range(blocks):
            at = pl.multiple_of(sources[b] * depth, depth)
            term = jnp.dot(normed[here, pl.ds(at, depth)], refs[b][...], preferred_element_type=f32)
            sum_ = term if sum_ is None else sum_ + term
        total[here, :] = sum_


def first_kernel(dims, sources, place, normed, start, lens, v0, v1, v2, v3, picked, begun, *refs):
    vecs = (v0, v1, v2, v3)
    seqs, span, width, slots, blocks, depth, late, tail = dims
    stride = span + PAD
    g_in = refs[late : late + slots]
    fields, known, scans, maps, planes = refs[late + slots :]
    cand, forg, rese = (fields.at[i] for i in range(3))
    gs, xs, products, sums = known.at[0], known.at[1], scans.at[0], scans.at[1]
    per = seqs // slots
    rows = per * span
    ext = rows + tail
    at = pl.multiple_of(sources[blocks - 1] * depth, depth)
    lead = joined(refs[:late])
    for k in range(slots):
        here = slice(k * ext, (k + 1) * ext)
        for piece in range(3):
            field = fields.at[place[3 + piece]]
            columns = slice(piece * width, (piece + 1) * width)
            total = begun[here, columns] + jnp.dot(
                normed[here, pl.ds(at, depth)], lead[:, columns], preferred_element_type=f32
            )
            total = total.astype(bf16).astype(f32)
            for j in range(per):
                to = (k * per + j) * stride + PAD
                before = jnp.broadcast_to(total[rows + j : rows + j + 1, :], (8, width))
                put_rows(field, to - 8, 8, before)
                put_rows(field, to, span, total[j * span : (j + 1) * span, :])
    before = jnp.where(place[1] == 0, start[...], strided(cand, PAD - 1, seqs, stride))
    put_strided(cand, PAD - 1, seqs, stride, before)
    ends = lens[...]
    base = place[0]
    step = min(width, STEP)
    ends = ends[:, :step]
    for low in range(0, width, step):
        units = slice(low, low + step)
        lane, lanes = low // 128, step // 128
        spread_rows((seqs, span, slots), low, step, g_in, picked, gs, xs)
        own = pl.ds(pl.multiple_of(place[2] + low, 128), step)
        peep_f, peep_r, bias_f, bias_r = (row[:, own] for row in vecs)

        def turn(t, carry):
            previous, decays, injects, handed = carry
            row = t + PAD
            c, f, r = (strided(ref, row, seqs, stride, lane, lanes) for ref in (cand, forg, rese))
            f = jax.nn.sigmoid(f + peep_f * previous + bias_f)
            r = jax.nn.sigmoid(r + peep_r * previous + bias_r)
            put_strided(forg, row, seqs, stride, f, lane)
            put_strided(rese, row, seqs, stride, r, lane)
            live = base + t < ends
            d = jnp.where(live, f, 1.0)
            inject = jnp.where(live, (1.0 - f) * c, 0.0)
            pulled = jnp.where(live, r * strided(gs, row, seqs, stride, lane, lanes), 0.0)
            decays, injects = decays * d, d * injects + inject
            put_strided(products, row, seqs, stride, decays, lane)
            put_strided(sums, row, seqs, stride, injects, lane)
            return c, decays, injects, handed + decays * pulled

        one, zero = jnp.ones((seqs, step), f32), jnp.zeros((seqs, step), f32)
        put_strided(products, PAD - 1, seqs, stride, one, lane)
        put_strided(sums, PAD - 1, seqs, stride, zero, lane)
        _, decays, injects, handed = lax.fori_loop(
            0, span, turn, (before[:, units], one, zero, zero), unroll=8
        )
        maps[0, :, units], maps[1, :, units], maps[2, :, units] = decays, injects, handed
        c, f, r, g, x = (
            strided(ref, PAD, seqs, stride, lane, lanes) for ref in (cand, forg, rese, gs, xs)
        )
        live = base < ends
        d = jnp.where(live, f, 1.0)
        inject = jnp.where(live, (1.0 - f) * c, 0.0)
        via_adjoint = jnp.where(live, (1.0 - f) * peep_f, 0.0)
        via_state = jnp.where(live, r * (1.0 - r) * g * peep_r, 0.0)
        planes[0, :, units], planes[1, :, units] = via_adjoint, via_adjoint * c
        planes[2, :, units], planes[3, :, units] = via_state * d, via_state * (inject - x)


def second_kernel(
    dims, place, lens, v0, v1, earlier, later, start, fields, known, scans, *refs
):
    vecs = (v0, v1)
    seqs, span, width, slots, tail = dims
    stride = span + PAD
    grads, moved = refs[0], refs[1 : slots + 1]
    final, sums, ending, ends_kept, outs, directs, gcs, fts, rts = refs[slots + 1 :]
    cand, forg, rese = (fields.at[i] for i in range(3))
    gs, xs, products, injected = known.at[0], known.at[1], scans.at[0], scans.at[1]
    per = seqs // slots
    base = place[0]
    step = min(width, STEP)
    ends = lens[:, :step]
    sums[...] = jnp.zeros_like(sums)
    for k in range(slots):
        to = k * (per * span + tail) + per * span
        grads[to : to + tail, :] = jnp.zeros((tail, 3 * width), bf16)
    for low in range(0, width, step):
        units = slice(low, low + step)
        lane, lanes = low // 128, step // 128
        own = pl.ds(pl.multiple_of(place[2] + low, 128), step)
        peep_f, peep_r = (row[:, own] for row in vecs)
        begin = earlier[0, :, units] * start[:, units] + earlier[1, :, units]
        after = later[2, :, units]

        def token(ref, row):
            return strided(ref, row, seqs, stride, lane, lanes)

        def token_of(ref, row):
            return strided(ref, row, seqs, stride)

        def state_at(row):
            return token(products, row) * begin + token(injected, row)

        end = state_at(span - 1 + PAD)
        final[:, units] = later[0, :, units] * end + later[1, :, units]
        ending[:, units] = end

        def backward(i, carry):
            reached, upcoming, state, c, pf, pr, bf, br = carry
            row = span - 1 - i + PAD
            f, r, x, g = (token(ref, row) for ref in (forg, rese, xs, gs))
            prior, previous = state_at(row - 1), token(cand, row - 1)
            live = base + (span - 1 - i) < ends
            zero = jnp.zeros_like(f)
            pulled = r * g
            adjoint = jnp.where(live, pulled, zero) + reached
            kept = jnp.where(live, (1.0 - f) * adjoint, zero)
            ft = f * kept * (prior - c)
            change = r * (state - x)
            rt = jnp.where(live, (1.0 - r) * g * change, zero)
            put_strided(gcs, row, seqs, stride, kept + upcoming)
            put_strided(fts, row, seqs, stride, ft)
            put_strided(rts, row, seqs, stride, rt)
            put_strided(outs, row, seqs, stride, jnp.where(live, r * state + (1.0 - r) * x, x))
            put_strided(directs, row, seqs, stride, jnp.where(live, (1.0 - r) * g, g))
            reached = jnp.where(live, f * adjoint, adjoint)
            return (
                reached,
                ft * peep_f + rt * peep_r,
                prior,
                previous,
                pf + ft * previous,
                pr + rt * previous,
                bf + ft,
                br + rt,
            )

        zero = jnp.zeros((seqs, step), f32)
        last = token(cand, span - 1 + PAD)
        done = lax.fori_loop(
            0, span, backward, (after, zero, end, last, zero, zero, zero, zero), unroll=4
        )
        ends_kept[:, units] = token_of(gcs, span - 1 + PAD)
        for i in range(4):
            sums[i : i + 1, units] = jnp.sum(done[4 + i], axis=0, keepdims=True)
        for n in range(seqs):
            at = n * stride + PAD
            k, j = n // per, n % per
            to = k * (per * span + tail) + j * span
            for gate, ref in enumerate((gcs, fts, rts)):
                here = slice(gate * width + low, gate * width + low + step)
                grads[to : to + span, here] = get_rows(ref, at, span).astype(bf16)
            moved[k][0, j, :, units] = get_rows(outs, at, span).astype(bf16)
            moved[k][1, j, :, units] = get_rows(directs, at, span).astype(bf16)


def mend_kernel(dims, grads, ending, kept, later, linked, out):
    per, span, width, ext = dims
    after = later[2]
    upcoming = ending[...] * (linked[0] * after + linked[2]) - linked[1] * after + linked[3]
    value = (kept[...] + upcoming).astype(bf16)
    last = lax.broadcasted_iota(jnp.int32, (16, width), 0) == 15
    for n in range(ending.shape[0]):
        at = n // per * ext + n % per * span + span - 16
        rows = slice(at, at + 16)
        row = jnp.broadcast_to(value[n : n + 1, :].astype(f32), (16, width))
        out[rows, :width] = jnp.where(last, row, grads[rows, :width].astype(f32)).astype(bf16)


def partial_kernel(distances, depth, width, owners, place, normed, grads, *outs):
    for i, distance in enumerate(distances):
        lanes = pl.ds(pl.multiple_of(owners[distance] * depth, min(depth, 128)), depth)
        columns = normed[:, lanes]
        for piece in range(3):
            gate = pl.ds(pl.multiple_of(place[3 + piece] * width, width), width)
            sum_ = lax.dot_general(
                columns, grads[:, gate], (((0,), (0,)), ((), ())), preferred_element_type=f32
            )
            here = slice(piece * width, (piece + 1) * width)
            split = len(outs) // len(distances)
            count = depth // split
            for n in range(split):
                outs[split * i + n][:, here] = sum_[n * count : (n + 1) * count].astype(outs[0].dtype)


def token_kernel(dims, parts, sources, place, grads, gate_sums, *refs):
    slots, blocks, depth, rows, width, split, tail = dims
    flat = sum(len(slot) for slot in parts)
    n_w = blocks + (1 if split else 0)
    pieces = refs[n_w : n_w + flat]
    means, scales, own = refs[n_w + flat : n_w + flat + 3]
    others = refs[n_w + flat + 3 : n_w + flat + slots + 2]
    sums = refs[n_w + flat + slots + 2]
    first_of = [sum(len(slot) for slot in parts[:k]) for k in range(slots)]

    def raw(k, lanes):
        found = [
            pieces[first_of[k] + i][: min(high, rows) - low, lanes]
            for i, (low, high) in enumerate(parts[k])
        ]
        return found[0] if len(found) == 1 else jnp.concatenate(found, axis=0)

    def block(b):
        return joined(refs[b : b + 2] if split and b == blocks - 1 else refs[b : b + 1])

    sums[...] = jnp.zeros_like(sums)
    sums[:4, pl.ds(pl.multiple_of(place[2], width), width)] = gate_sums[:4, :]
    for b in range(blocks):
        at = pl.multiple_of(sources[b] * depth, depth)
        lanes = pl.ds(at, depth)
        gain_sum, bias_sum = jnp.zeros((8, depth), f32), jnp.zeros((8, depth), f32)
        weights = block(b)
        for k in range(slots):
            here = pl.ds(k * rows, rows)
            total = None
            for piece in range(3):
                gate = pl.ds(pl.multiple_of(place[3 + piece] * width, width), width)
                term = lax.dot_general(
                    grads[k * (rows + tail) : k * (rows + tail) + rows, gate],
                    weights[:, piece * width : (piece + 1) * width],
                    (((1,), (1,)), ((), ())),
                    preferred_element_type=f32,
                )
                total = term if total is None else total + term
            copies = depth // 128
            mean = jnp.concatenate([means[here, :]] * copies, axis=1)
            scale = jnp.concatenate([scales[here, :]] * copies, axis=1)
            scaled = (raw(k, lanes).astype(f32) - mean) * scale
            gain_sum += jnp.sum((total * scaled).reshape(rows // 8, 8, depth), axis=0)
            bias_sum += jnp.sum(total.reshape(rows // 8, 8, depth), axis=0)
            if k == 0:
                own[:, lanes] = total
            else:
                others[k - 1][:, lanes] = total.astype(bf16)
        sums[4:5, lanes] = jnp.sum(gain_sum, axis=0, keepdims=True)
        sums[5:6, lanes] = jnp.sum(bias_sum, axis=0, keepdims=True)


def first_maps(maps):
    one, zero = jnp.ones_like(maps[0]), jnp.zeros_like(maps[0])
    return (maps[0], maps[1], maps[2]), (one, zero), (one, zero, zero)


def joined_maps(known, other, first):
    (decay, inject, handed), before, later = known
    theirs = (other[0], other[1], other[2])
    before_new = (theirs[0] * before[0], before[0] * theirs[1] + before[1])
    later_new = (
        later[0] * theirs[0],
        theirs[0] * later[1] + theirs[1],
        later[2] + later[0] * theirs[2],
    )
    before = tuple(jnp.where(first, a, b) for a, b in zip(before, before_new))
    later = tuple(jnp.where(first, b, a) for a, b in zip(later, later_new))
    inject_new = jnp.where(first, theirs[0] * inject + theirs[1], decay * theirs[1] + inject)
    handed_new = jnp.where(first, handed + decay * theirs[2], theirs[2] + theirs[0] * handed)
    return (decay * theirs[0], inject_new, handed_new), before, later


class Rounds:
    def __init__(self):
        self.before, self.given = [], []

    def take(self, value):
        if not self.before:
            return value
        return lax.optimization_barrier((value, self.before))[0]

    def give(self, *values):
        self.given += values

    def turn(self):
        self.before, self.given = self.given, []


def local(
    inputs,
    start_state,
    lengths,
    weights,
    peep_forget,
    peep_reset,
    bias_forget,
    bias_reset,
    norm_gain,
    norm_bias,
    out_grad,
):
    per, span, model = inputs.shape
    n_seq, slots = lax.axis_size("seq"), lax.axis_size("stream")
    at_seq, at_stream = lax.axis_index("seq"), lax.axis_index("stream")
    seqs = per * slots
    width = model // slots
    depth = model // n_seq
    rows = per * span
    tokens = seqs * span
    tail = 16
    half = depth // 2
    spot = spot_of(at_seq, n_seq)
    far = n_seq // 2
    steps = [0]
    for k in range(1, far):
        steps += [-k, k]
    steps.append(far)
    dealing = slots == 4

    def owner(distance):
        return at_spot(wrapped(spot + distance, n_seq), n_seq)

    def per_stream(table):
        found = table[0]
        for d in range(1, len(table)):
            found = jnp.where(at_stream == d, table[d], found)
        return found

    gates = ((0, 1, 2), (1, 0, 2), (1, 2, 0), (2, 1, 0)) if dealing else ((0, 1, 2),)
    gate_of = [per_stream([table[piece] for table in gates]) for piece in range(3)]
    bits = [1 << b for b in range(slots.bit_length() - 1)]
    seq_bits = [1 << b for b in range(n_seq.bit_length() - 1)]
    share = model // n_seq
    index = {
        "sources": jnp.stack([owner(distance) for distance in steps]).astype(jnp.int32),
        "place": jnp.stack([at_seq * span, at_seq, at_stream * width, *gate_of]).astype(jnp.int32),
        "owners": jnp.stack([owner(distance) for distance in range(n_seq)]).astype(jnp.int32),
        "where": jnp.stack([(at_stream ^ k) * width for k in range(slots)]).astype(jnp.int32),
        "lanes": [(at_stream ^ k) * width for k in range(slots)],
        "rows": [(at_stream ^ k) * per for k in range(slots)],
        "first": [(at_seq & bit) == 0 for bit in seq_bits],
        "even": at_stream % 2 == 0,
        "share": at_seq * share % width,
        "holds": at_stream == at_seq * share // width,
    }
    index, inputs, weights, out_grad, start_state, lengths = lax.optimization_barrier(
        (index, inputs, weights, out_grad, start_state, lengths)
    )
    sources, place, even = index["sources"], index["place"], index["even"]

    vectors = [
        row.reshape(1, model) for row in (peep_forget, peep_reset, bias_forget, bias_reset)
    ]
    gain_row, bias_row = norm_gain.reshape(1, model), norm_bias.reshape(1, model)
    tall = seqs * (span + PAD)
    fields, two = (jax.ShapeDtypeStruct((n, width // 128, tall, 128), f32) for n in (3, 2))
    space = pltpu.VMEM((min(width, STEP) // 128, tall, 128), f32)

    rounds = Rounds()
    take, give = rounds.take, rounds.give
    box = {}

    def deal():
        if dealing:
            pieces = [weights[:, i * width : (i + 1) * width] for i in range(3)]
            own = jnp.where(even, pieces[0], pieces[2])
            near = swapped(pieces[1], "stream", 1)
            distant = swapped(jnp.where(even, pieces[2], pieces[0]), "stream", 2)
            box["dealt"] = jnp.concatenate([own, near, distant], axis=1)
            give(near, distant)
            return
        everything = lax.all_gather(weights, "stream", axis=1, tiled=True)
        found = [
            lax.dynamic_slice_in_dim(everything, gate * model + at_stream * width, width, 1)
            for gate in range(3)
        ]
        box["dealt"] = jnp.concatenate(found, axis=1)

    def last_columns():
        came = box["came"]
        rest = box["mine", far + 1][0][:, width:] + came[0].astype(f32) + came[1].astype(f32)
        box["rest"] = rest[:, :width], rest[:, width:]
        if dealing:
            near, distant = (part_of.astype(bf16) for part_of in box["rest"])
            box["distant"] = swapped(distant, "stream", 2)
            box["near"] = swapped(near, "stream", 1)
            rounds.before = [*rounds.before, distant, near]

    def stored():
        came = box["came"]
        own = box["mine", far + 1][0][:, :width] + came[2].astype(f32) + came[3].astype(f32)
        if dealing:
            distant, near = box["distant"].astype(f32), box["near"].astype(f32)
            found = [jnp.where(even, own, distant), near, jnp.where(even, distant, own)]
        else:
            flat = lax.all_gather(
                jnp.concatenate([own, *box["rest"]], axis=1).astype(bf16), "stream", axis=0
            ).astype(f32)
            flat = jnp.swapaxes(flat.reshape(slots, depth, 3, width), 0, 2)
            flat = jnp.swapaxes(flat, 1, 2).reshape(3 * slots, depth, width)
            found = [
                lax.dynamic_index_in_dim(flat, 3 * at_stream + i, 0, keepdims=False)
                for i in range(3)
            ]
        return jnp.concatenate(found, axis=1)

    def gather(step):
        if step == 1:
            box["up"] = box["down"] = take(box["dealt"])
            box["blocks"] = [box["dealt"]]
        if step == far:
            box["up"], box["down"] = box["up"][:half], box["down"][half:]
        box["up"] = along_ring(take(box["up"]), 1)
        box["down"] = along_ring(take(box["down"]), -1)
        box["blocks"] += [box["up"], box["down"]]
        give(box["up"], box["down"])

    def partials(distances, kind, split=1):
        grads = take(box["grads"])
        if depth % 128:
            found = []
            for distance in distances:
                at = owner(distance)
                sum_ = lax.dot_general(
                    lax.dynamic_slice_in_dim(box["normed"], at * depth, depth, 1),
                    grads,
                    (((0,), (0,)), ((), ())),
                    preferred_element_type=f32,
                ).astype(kind)
                found += [sum_[n * depth // split :][: depth // split] for n in range(split)]
            return found
        return call(
            functools.partial(
                partial_kernel, [distance % n_seq for distance in distances], depth, width
            ),
            [jax.ShapeDtypeStruct((depth // split, 3 * width), kind)] * (split * len(distances)),
            [index["owners"], place, box["normed"], grads],
            scalars=2,
        )

    def scatter(step):
        cuts_of = [(width, 3 * width), (0, width)] if step == far else [(0, 3 * width)]
        if step == 1:
            sent = box["farthest"]
        else:
            sent = call(
                functools.partial(merge_kernel, cuts_of),
                [jax.ShapeDtypeStruct((depth, b - a), bf16) for a, b in cuts_of for _ in range(2)],
                [*box["mine", step], box["up"], box["down"]],
            )
        came = [along_ring(take(value), 1 - 2 * (i % 2)) for i, value in enumerate(sent)]
        rounds.before = [*rounds.before, *sent]
        box["up"], box["down"] = came[:2]
        box["came"] = came
        give(*came)

    def sums_of(step):
        distance = far + 1 - step
        box["mine", step] = partials((distance, -distance) if distance else (0,), f32)
        give(*box["mine", step])

    whole_part = [(0, rows + tail)]
    cuts = [(0, rows // 2), (rows // 2, rows + tail)]
    parts = [whole_part, whole_part, cuts, cuts] if dealing else [whole_part] * slots
    tokens_of = [[None] * len(slot) for slot in parts]
    flat_inputs = inputs.reshape(rows, model)

    def ahead_tokens():
        box["ahead"] = lax.ppermute(
            take(inputs[:, -1, :]), "seq", [(i, i + 1) for i in range(n_seq - 1)]
        )
        give(box["ahead"])

    def own_tokens():
        tokens_of[0][0] = jnp.concatenate(
            [flat_inputs, box["ahead"], jnp.zeros((tail - per, model), bf16)], axis=0
        )

    def everyones_tokens():
        ahead_tokens()
        own_tokens()
        for bit in reversed(bits):
            for k in range(slots):
                if tokens_of[k][0] is not None and tokens_of[k ^ bit][0] is None:
                    tokens_of[k ^ bit][0] = swapped(tokens_of[k][0], "stream", bit)

    def near_tokens():
        own_tokens()
        tokens_of[1][0] = swapped(take(tokens_of[0][0]), "stream", 1)
        give(tokens_of[1][0])

    def far_tokens(i):
        low, high = cuts[i]
        source = flat_inputs[low:high] if high <= rows else tokens_of[0][0][low:high]
        tokens_of[2][i] = swapped(take(source), "stream", 2)
        give(tokens_of[2][i])

    def passed_tokens(i):
        tokens_of[3][i] = swapped(take(tokens_of[2][i]), "stream", 1)
        give(tokens_of[3][i])

    def messages():
        box["messages"] = call(
            functools.partial(message_kernel, slots, width, tail),
            [jax.ShapeDtypeStruct((rows + tail, width), bf16)] * slots,
            [
                index["where"],
                take(out_grad.reshape(rows, model)),
                start_state,
                jnp.broadcast_to(lengths[:, None], (per, 128)),
            ],
            scalars=1,
        )

    def out_grads():
        for k in range(slots):
            box["g", k] = box["messages"][k]
            if k:
                box["g", k] = swapped(take(box["g", k]), "stream", k)
                give(box["g", k])

    def normalise():
        flat = [piece for slot in tokens_of for piece in slot]
        box["normed"], box["means"], box["scales"], box["picked"] = call(
            functools.partial(norm_kernel, parts, rows, tail, width),
            [
                jax.ShapeDtypeStruct((slots * (rows + tail), model), bf16),
                jax.ShapeDtypeStruct((tokens, 128), f32),
                jax.ShapeDtypeStruct((tokens, 128), f32),
                jax.ShapeDtypeStruct((tokens, width), bf16),
            ],
            [place, *flat, take(gain_row), bias_row],
            scalars=1,
        )
        give(box["normed"])

    def from_others():
        extra = [box["g", k][rows : rows + 5 * per].astype(f32) for k in range(slots)]
        extra = [x.reshape(5, per, width) for x in extra]
        box["start"] = jnp.concatenate([x[0] + x[1] + x[2] for x in extra], axis=0)
        ends = jnp.concatenate([x[3] * 256 + x[4] for x in extra], axis=0)
        box["ends"] = ends.astype(jnp.int32)

    def in_order():
        if depth % 128 == 0:
            return box["blocks"], sources, n_seq, depth, True
        deep = 2 * 128
        if "whole" not in box:
            whole = jnp.zeros((model, 3 * width), bf16)
            for b, block in enumerate(box["blocks"]):
                at = owner(steps[min(b, n_seq - 1)]) * depth + (half if b == n_seq else 0)
                whole = lax.dynamic_update_slice_in_dim(whole, block, at, 0)
            box["whole"] = [whole[i : i + deep] for i in range(0, model, deep)]
        count = model // deep
        return box["whole"], jnp.arange(count, dtype=jnp.int32), count, deep, False

    def begin():
        held, places, count, deep, _ = in_order()
        box["begun"] = call(
            functools.partial(begin_kernel, count - 1, deep, rows + tail, slots),
            jax.ShapeDtypeStruct((slots * (rows + tail), 3 * width), f32),
            [places, take(box["normed"]), *held[: count - 1]],
            scalars=1,
        )
        give(box["begun"])

    def first():
        held, places, count, deep, split = in_order()
        *box["fields"], maps, planes = call(
            functools.partial(
                first_kernel, (seqs, span, width, slots, count, deep, 2 if split else 1, tail)
            ),
            [
                fields,
                two,
                two,
                jax.ShapeDtypeStruct((3, seqs, width), f32),
                jax.ShapeDtypeStruct((4, seqs, width), f32),
            ],
            [
                places,
                place,
                box["normed"],
                box["start"],
                take(box["ends"]),
                *vectors,
                box["picked"],
                box["begun"],
                *held[count - 1 :],
                *[box["g", k] for k in range(slots)],
            ],
            scalars=2,
        )
        box["linked"] = lax.ppermute(planes, "seq", [(i + 1, i) for i in range(n_seq - 1)])
        box["known"], box["maps"] = first_maps(maps), maps
        join(1)

    def join(bit):
        mine = box["maps"] if bit == 1 else take(jnp.stack(box["known"][0]))
        other = swapped(mine, "seq", bit)
        give(other)
        box["known"] = joined_maps(box["known"], other, index["first"][seq_bits.index(bit)])

    def join_rest():
        bit = 2
        while bit < n_seq:
            join(bit)
            bit *= 2

    def second():
        _, earlier, later = box["known"]
        later = jnp.stack(later)
        out = call(
            functools.partial(second_kernel, (seqs, span, width, slots, tail)),
            [
                jax.ShapeDtypeStruct((slots * (rows + tail), 3 * width), bf16),
                *[jax.ShapeDtypeStruct((2, per, span, width), bf16)] * slots,
                jax.ShapeDtypeStruct((seqs, width), f32),
                jax.ShapeDtypeStruct((8, width), f32),
                jax.ShapeDtypeStruct((seqs, width), f32),
                jax.ShapeDtypeStruct((seqs, width), f32),
            ],
            [
                place,
                take(box["ends"]),
                *vectors[:2],
                jnp.stack(earlier),
                later,
                box["start"],
                *box["fields"],
            ],
            scratch=[space] * 5,
            scalars=1,
        )
        box["grads"], box["moving"] = out[0], out[1 : slots + 1]
        box["final"], box["sums"] = out[slots + 1], out[slots + 2]
        box["grads"] = call(
            functools.partial(mend_kernel, (per, span, width, rows + tail)),
            jax.ShapeDtypeStruct((slots * (rows + tail), 3 * width), bf16),
            [out[0], *out[slots + 3 :], later, box["linked"]],
            aliases={0: 0},
        )
        rounds.before = []
        box["farthest"] = partials((far,), bf16, 2)
        box["grads"] = lax.optimization_barrier((box["grads"], box["farthest"]))[0]

    def moved(among):
        for k in among:
            box["moved", k] = box["moving"][k]
            if k:
                box["moved", k] = swapped(take(box["moving"][k]), "stream", k)
                give(box["moved", k])

    def token_grads():
        held, places, count, deep, split = in_order()
        out = call(
            functools.partial(
                token_kernel, (slots, count, deep, rows, width, split, tail), parts
            ),
            [
                jax.ShapeDtypeStruct((rows, model), f32),
                *[jax.ShapeDtypeStruct((rows, model), bf16)] * (slots - 1),
                jax.ShapeDtypeStruct((8, model), f32),
            ],
            [
                places,
                place,
                take(box["grads"]),
                box["sums"],
                *held,
                *[piece for slot in tokens_of for piece in slot],
                box["means"],
                box["scales"],
            ],
            scalars=2,
        )
        box["kept"] = {k: out[k] for k in range(slots)}
        box["summed"] = out[slots]
        give(out[0])

    def token_sends(bit):
        kept = box["kept"]
        for k in sorted(kept, reverse=True):
            if k & bit:
                got = swapped(take(kept.pop(k).astype(bf16)), "stream", bit)
                kept[k ^ bit] = kept[k ^ bit].astype(f32) + got.astype(f32)
                give(got)

    def token_part(i, count):
        if i == 0:
            box["sending"] = box["kept"].pop(2).astype(bf16)
            box["arrived"] = []
        low, high = rows * i // count // 16 * 16, rows * (i + 1) // count // 16 * 16
        box["arrived"].append(swapped(take(box["sending"][low:high]), "stream", 2))
        give(box["arrived"][i])
        if i + 1 == count:
            box["kept"][0] = box["kept"][0] + jnp.concatenate(box["arrived"], axis=0).astype(f32)

    def sums(axis, bit):
        if "states" not in box:
            mine = jnp.where(index["holds"], cut(box["final"], index["share"], share, 1), 0.0)
            box["states"] = {k: mine[k * per : (k + 1) * per] for k in range(slots)}
        states, summed = box["states"], box["summed"][:6]
        going = [k for k in sorted(states) if k & bit] if axis == "stream" else []
        if going:
            row = jnp.concatenate([states[k] for k in going], axis=1)
            row = jnp.pad(row, ((0, 0), (0, model - row.shape[1])))
            summed = jnp.concatenate([summed, row], axis=0)
        got = swapped(take(summed), axis, bit)
        give(got)
        box["summed"] = box["summed"][:6] + got[:6]
        for i, k in enumerate(going):
            states.pop(k)
            states[k ^ bit] = states[k ^ bit] + got[6:, i * share : (i + 1) * share]

    def assemble():
        box["outputs"], box["direct"] = found = call(
            functools.partial(assemble_kernel, slots, width),
            [jax.ShapeDtypeStruct((per, span, model), bf16)] * 2,
            [index["where"], *[take(box["moved", k]) for k in range(slots)]],
            scalars=1,
            pinned=False,
        )
        give(*found)
        give(*found)

    def finish():
        grad_normed = box["kept"][0]
        source = inputs.astype(f32).reshape(rows, model)
        scale = take(box["scales"])[:rows, :1]
        scaled = (source - box["means"][:rows, :1]) * scale
        grad_scaled = grad_normed * norm_gain
        grad_source = scale * (
            grad_scaled
            - jnp.mean(grad_scaled, axis=1, keepdims=True)
            - scaled * jnp.mean(grad_scaled * scaled, axis=1, keepdims=True)
        )
        box["input_grad"] = (grad_source.reshape(per, span, model) + box["direct"].astype(f32)).astype(bf16)
        give(box["input_grad"])

    part = functools.partial
    if dealing:
        early = [
            [part(far_tokens, 0)],
            [near_tokens, part(far_tokens, 1), part(passed_tokens, 0), messages],
            [part(passed_tokens, 1), out_grads, normalise],
        ]
    else:
        early = [[everyones_tokens], [messages], [out_grads, normalise]]
    early.append([from_others] + ([begin] if depth % 128 == 0 else []))
    deal()
    if dealing:
        ahead_tokens()
    rounds.turn()
    for step in range(1, far + 1):
        gather(step)
        for other in early[step - 1] if step <= len(early) else ():
            other()
        rounds.turn()
    if depth % 128:
        begin()
    first()
    rounds.turn()
    join_rest()
    rounds.turn()
    second()
    late = [
        [part(moved, range(slots)[:3])],
        [part(moved, range(slots)[3:]), token_grads],
        [part(token_sends, 1)]
        + [part(sums, "stream", bit) for bit in bits]
        + [part(sums, "seq", 1)],
        [part(sums, "seq", 2)],
    ]
    for step in range(2, far + 2):
        late_at = step - 2 if far > 4 or step < 3 else min(step - 3, 1)
        while len(late) <= late_at:
            late.append([])
        late[late_at].insert(0, part(sums_of, step))
    if dealing:
        late[2].append(part(token_part, 0, 2))
        late[3].insert(0, part(token_part, 1, 2))
    else:
        late[3] += [part(token_sends, bit) for bit in bits[1:]]
    late[2].append(assemble)
    late += [[] for _ in range(far - len(late))]
    late[far - 1].insert(1, last_columns)
    for step in range(1, far + 1):
        scatter(step)
        for other in late[step - 1] if step <= len(late) else ():
            other()
        rounds.turn()
    weight_grad = stored()
    finish()
    for bit in seq_bits[2:]:
        sums("seq", bit)

    input_grad = box["input_grad"]
    outputs, final_state, summed = box["outputs"], box["states"][0], box["summed"]

    return (
        outputs,
        final_state,
        input_grad,
        weight_grad,
        summed[0],
        summed[1],
        summed[2],
        summed[3],
        summed[4],
        summed[5],
    )


def solution(mesh):
    return jax.shard_map(
        local,
        mesh=mesh,
        in_specs=(
            P("stream", "seq", None),
            P("stream", None),
            P("stream"),
            P("seq", "stream"),
            P(),
            P(),
            P(),
            P(),
            P(),
            P(),
            P("stream", "seq", None),
        ),
        out_specs=(
            P("stream", "seq", None),
            P("stream", "seq"),
            P("stream", "seq", None),
            P("seq", "stream"),
            P(),
            P(),
            P(),
            P(),
            P(),
            P(),
        ),
        check_vma=False,
    )
```

```python
import functools

import jax
import jax.numpy as jnp
from jax import lax
from jax.experimental import pallas as pl
from jax.experimental.pallas import tpu as pltpu
from jax.sharding import PartitionSpec as P

epsilon = 1e-05
f32 = jnp.float32
bf16 = jnp.bfloat16
PAD = 8
STEP = 256
ROOM = 5 * 512 * 1024


def vmem_spec():
    return pl.BlockSpec(memory_space=pltpu.VMEM)


def smem_spec():
    return pl.BlockSpec(memory_space=pltpu.SMEM)


def call(kernel, out_shape, operands, scratch=(), scalars=0, pinned=True, aliases=None):
    held = jax.tree.map(lambda out: pltpu.VMEM(out.shape, out.dtype), out_shape)
    return pl.pallas_call(
        kernel,
        out_shape=held if pinned else out_shape,
        in_specs=[smem_spec()] * scalars + [vmem_spec()] * (len(operands) - scalars),
        out_specs=jax.tree.map(lambda _: vmem_spec(), out_shape),
        scratch_shapes=list(scratch),
        input_output_aliases=aliases or {},
        compiler_params=pltpu.CompilerParams(vmem_limit_bytes=lax.axis_size("stream") * ROOM),
        cost_estimate=pl.CostEstimate(flops=0, bytes_accessed=0, transcendentals=0),
    )(
        *operands[:scalars],
        *[pltpu.with_memory_space_constraint(x, pltpu.VMEM) for x in operands[scalars:]],
    )


def at_spot(spot, count):
    if count != 8:
        return spot
    return spot * 2 if isinstance(spot, int) and spot < 4 else (
        15 - spot * 2 if isinstance(spot, int) else jnp.where(spot < 4, spot * 2, 15 - spot * 2)
    )


def spot_of(index, count):
    if count != 8:
        return index
    return jnp.where(index % 2 == 0, index // 2, (15 - index) // 2)


def wrapped(value, count):
    value = jnp.where(value >= count, value - count, value)
    return jnp.where(value < 0, value + count, value)


def along_ring(value, steps):
    count = lax.axis_size("seq")
    order = [at_spot(i, count) for i in range(count)]
    return lax.ppermute(value, "seq", [(order[i], order[(i + steps) % count]) for i in range(count)])


def cut(array, start, size, axis):
    starts = [jnp.int32(0)] * array.ndim
    sizes = list(array.shape)
    starts[axis], sizes[axis] = start, size
    return lax.dynamic_slice(array, starts, sizes, allow_negative_indices=False)


def pasted(array, piece, start, axis):
    starts = [jnp.int32(0)] * array.ndim
    starts[axis] = start
    return lax.dynamic_update_slice(array, piece, starts, allow_negative_indices=False)


def swapped(value, axis, bit):
    return lax.ppermute(value, axis, [(i, i ^ bit) for i in range(lax.axis_size(axis))])


def norm_kernel(parts, rows, tail, units, place, *refs):
    flat = sum(len(slot) for slot in parts)
    pieces = refs[:flat]
    gain, bias, normed, means, scales, picked = refs[flat:]
    gain_row, bias_row = gain[...], bias[...]
    lanes = pl.ds(pl.multiple_of(place[2], units), units)
    at = 0
    for k, slot in enumerate(parts):
        for low, high in slot:
            x = pieces[at][...].astype(f32)
            mean = jnp.mean(x, axis=1, keepdims=True)
            centered = x - mean
            scale = lax.rsqrt(jnp.mean(centered * centered, axis=1, keepdims=True) + epsilon)
            base = k * (rows + tail)
            normed[base + low : base + high, :] = (centered * scale * gain_row + bias_row).astype(bf16)
            count = min(high, rows) - low
            here = slice(k * rows + low, k * rows + low + count)
            means[here, :] = jnp.broadcast_to(mean[:count], (count, 128))
            scales[here, :] = jnp.broadcast_to(scale[:count], (count, 128))
            picked[here, :] = pieces[at][:count, lanes]
            at += 1


def strided(ref, row, seqs, stride, low=0, count=None):
    count = ref.shape[0] if count is None else count
    tiles = [ref[low + lane, pl.ds(row, seqs, stride=stride), :] for lane in range(count)]
    return jnp.concatenate(tiles, axis=1)


def put_strided(ref, row, seqs, stride, value, low=0):
    for lane in range(value.shape[1] // 128):
        ref[low + lane, pl.ds(row, seqs, stride=stride), :] = value[:, lane * 128 : (lane + 1) * 128]


def put_rows(ref, row, count, value, low=0):
    for lane in range(value.shape[1] // 128):
        ref[low + lane, pl.ds(row, count), :] = value[:, lane * 128 : (lane + 1) * 128]


def get_rows(ref, row, count):
    return jnp.concatenate([ref[lane, pl.ds(row, count), :] for lane in range(ref.shape[0])], axis=1)


def message_kernel(slots, units, tail, where, grads, start, lengths, *outs):
    rows, per = grads.shape[0], start.shape[0]
    for k in range(slots):
        lanes = pl.ds(pl.multiple_of(where[k], units), units)
        outs[k][:rows, :] = grads[:, lanes]
        left = start[:, lanes]
        extra = []
        for _ in range(3):
            part = left.astype(bf16).astype(f32)
            extra.append(part)
            left = left - part
        counts = lengths[...]
        high = counts // 256
        extra += [
            jnp.broadcast_to(n.astype(f32)[:, :1], (per, units)) for n in (high, counts - high * 256)
        ]
        extra.append(jnp.zeros((tail - 5 * per, units), f32))
        outs[k][rows:, :] = jnp.concatenate(extra, axis=0).astype(bf16)


def merge_kernel(cuts, mine_up, mine_down, up, down, *outs):
    count, total = up.shape[0], mine_up.shape[0]
    first, last = slice(0, count), slice(total - count, total)
    for n, (low, high) in enumerate(cuts):
        lanes = slice(low, high)
        out_up, out_down = outs[2 * n], outs[2 * n + 1]
        out_up[first, :] = (mine_up[first, lanes] + up[:, lanes].astype(f32)).astype(bf16)
        out_down[last, :] = (mine_down[last, lanes] + down[:, lanes].astype(f32)).astype(bf16)
        if count < total:
            out_up[count:, :] = mine_up[count:, lanes].astype(bf16)
            out_down[: total - count, :] = mine_down[: total - count, lanes].astype(bf16)


def stored_kernel(width, place, mine, up, down, near, distant, out):
    own = mine[...] + up[...].astype(f32) + down[...].astype(f32)
    shift = place[0] * 2 * width
    out[:, pl.ds(pl.multiple_of(shift, width), width)] = own
    out[:, width : 2 * width] = near[...].astype(f32)
    out[:, pl.ds(pl.multiple_of(2 * width - shift, width), width)] = distant[...].astype(f32)


def assemble_kernel(slots, width, where, *refs):
    for k in range(slots):
        lanes = pl.ds(pl.multiple_of(where[k], width), width)
        for which in range(2):
            refs[slots + which][:, :, lanes] = refs[k][which]


def spread_rows(dims, low, width, g_in, picked, gs, xs):
    seqs, span, slots = dims
    per, lane = seqs // slots, low // 128
    for n in range(seqs):
        to, lanes = n * (span + PAD) + PAD, slice(low, low + width)
        at = n % per * span
        put_rows(gs, to, span, g_in[n // per][at : at + span, lanes].astype(f32), lane)
        put_rows(xs, to, span, picked[n * span : (n + 1) * span, lanes].astype(f32), lane)


def joined(refs):
    return refs[0][...] if len(refs) == 1 else jnp.concatenate([ref[...] for ref in refs], axis=0)


def begin_kernel(blocks, depth, rows, count, sources, normed, *refs):
    total = refs[blocks]
    for k in range(count):
        here = slice(k * rows, (k + 1) * rows)
        sum_ = None
        for b in range(blocks):
            at = pl.multiple_of(sources[b] * depth, depth)
            term = jnp.dot(normed[here, pl.ds(at, depth)], refs[b][...], preferred_element_type=f32)
            sum_ = term if sum_ is None else sum_ + term
        total[here, :] = sum_


def first_kernel(dims, sources, place, normed, start, lens, v0, v1, v2, v3, picked, begun, *refs):
    vecs = (v0, v1, v2, v3)
    seqs, span, width, slots, blocks, depth, late, tail = dims
    stride = span + PAD
    g_in = refs[late : late + slots]
    fields, known, scans, maps, planes = refs[late + slots :]
    cand, forg, rese = (fields.at[i] for i in range(3))
    gs, xs, products, sums = known.at[0], known.at[1], scans.at[0], scans.at[1]
    per = seqs // slots
    rows = per * span
    ext = rows + tail
    at = pl.multiple_of(sources[blocks - 1] * depth, depth)
    lead = joined(refs[:late])
    for k in range(slots):
        here = slice(k * ext, (k + 1) * ext)
        for piece in range(3):
            field = fields.at[place[3 + piece]]
            columns = slice(piece * width, (piece + 1) * width)
            total = begun[here, columns] + jnp.dot(
                normed[here, pl.ds(at, depth)], lead[:, columns], preferred_element_type=f32
            )
            total = total.astype(bf16).astype(f32)
            for j in range(per):
                to = (k * per + j) * stride + PAD
                before = jnp.broadcast_to(total[rows + j : rows + j + 1, :], (8, width))
                put_rows(field, to - 8, 8, before)
                put_rows(field, to, span, total[j * span : (j + 1) * span, :])
    before = jnp.where(place[1] == 0, start[...], strided(cand, PAD - 1, seqs, stride))
    put_strided(cand, PAD - 1, seqs, stride, before)
    ends = lens[...]
    base = place[0]
    step = min(width, STEP)
    ends = ends[:, :step]
    for low in range(0, width, step):
        units = slice(low, low + step)
        lane, lanes = low // 128, step // 128
        spread_rows((seqs, span, slots), low, step, g_in, picked, gs, xs)
        own = pl.ds(pl.multiple_of(place[2] + low, 128), step)
        peep_f, peep_r, bias_f, bias_r = (row[:, own] for row in vecs)

        def turn(t, carry):
            previous, decays, injects, handed = carry
            row = t + PAD
            c, f, r = (strided(ref, row, seqs, stride, lane, lanes) for ref in (cand, forg, rese))
            f = jax.nn.sigmoid(f + peep_f * previous + bias_f)
            r = jax.nn.sigmoid(r + peep_r * previous + bias_r)
            put_strided(forg, row, seqs, stride, f, lane)
            put_strided(rese, row, seqs, stride, r, lane)
            live = base + t < ends
            d = jnp.where(live, f, 1.0)
            inject = jnp.where(live, (1.0 - f) * c, 0.0)
            pulled = jnp.where(live, r * strided(gs, row, seqs, stride, lane, lanes), 0.0)
            decays, injects = decays * d, d * injects + inject
            put_strided(products, row, seqs, stride, decays, lane)
            put_strided(sums, row, seqs, stride, injects, lane)
            return c, decays, injects, handed + decays * pulled

        one, zero = jnp.ones((seqs, step), f32), jnp.zeros((seqs, step), f32)
        put_strided(products, PAD - 1, seqs, stride, one, lane)
        put_strided(sums, PAD - 1, seqs, stride, zero, lane)
        _, decays, injects, handed = lax.fori_loop(
            0, span, turn, (before[:, units], one, zero, zero), unroll=8
        )
        maps[0, :, units], maps[1, :, units], maps[2, :, units] = decays, injects, handed
        c, f, r, g, x = (
            strided(ref, PAD, seqs, stride, lane, lanes) for ref in (cand, forg, rese, gs, xs)
        )
        live = base < ends
        d = jnp.where(live, f, 1.0)
        inject = jnp.where(live, (1.0 - f) * c, 0.0)
        via_adjoint = jnp.where(live, (1.0 - f) * peep_f, 0.0)
        via_state = jnp.where(live, r * (1.0 - r) * g * peep_r, 0.0)
        planes[0, :, units], planes[1, :, units] = via_adjoint, via_adjoint * c
        planes[2, :, units], planes[3, :, units] = via_state * d, via_state * (inject - x)


def second_kernel(
    dims, place, lens, v0, v1, earlier, later, start, fields, known, scans, *refs
):
    vecs = (v0, v1)
    seqs, span, width, slots, tail = dims
    stride = span + PAD
    grads, moved = refs[0], refs[1 : slots + 1]
    final, sums, ending, ends_kept, outs, directs, gcs, fts, rts = refs[slots + 1 :]
    cand, forg, rese = (fields.at[i] for i in range(3))
    gs, xs, products, injected = known.at[0], known.at[1], scans.at[0], scans.at[1]
    per = seqs // slots
    base = place[0]
    step = min(width, STEP)
    ends = lens[:, :step]
    sums[...] = jnp.zeros_like(sums)
    for k in range(slots):
        to = k * (per * span + tail) + per * span
        grads[to : to + tail, :] = jnp.zeros((tail, 3 * width), bf16)
    for low in range(0, width, step):
        units = slice(low, low + step)
        lane, lanes = low // 128, step // 128
        own = pl.ds(pl.multiple_of(place[2] + low, 128), step)
        peep_f, peep_r = (row[:, own] for row in vecs)
        begin = earlier[0, :, units] * start[:, units] + earlier[1, :, units]
        after = later[2, :, units]

        def token(ref, row):
            return strided(ref, row, seqs, stride, lane, lanes)

        def token_of(ref, row):
            return strided(ref, row, seqs, stride)

        def state_at(row):
            return token(products, row) * begin + token(injected, row)

        end = state_at(span - 1 + PAD)
        final[:, units] = later[0, :, units] * end + later[1, :, units]
        ending[:, units] = end

        def backward(i, carry):
            reached, upcoming, state, c, pf, pr, bf, br = carry
            row = span - 1 - i + PAD
            f, r, x, g = (token(ref, row) for ref in (forg, rese, xs, gs))
            prior, previous = state_at(row - 1), token(cand, row - 1)
            live = base + (span - 1 - i) < ends
            zero = jnp.zeros_like(f)
            pulled = r * g
            adjoint = jnp.where(live, pulled, zero) + reached
            kept = jnp.where(live, (1.0 - f) * adjoint, zero)
            ft = f * kept * (prior - c)
            change = r * (state - x)
            rt = jnp.where(live, (1.0 - r) * g * change, zero)
            put_strided(gcs, row, seqs, stride, kept + upcoming)
            put_strided(fts, row, seqs, stride, ft)
            put_strided(rts, row, seqs, stride, rt)
            put_strided(outs, row, seqs, stride, jnp.where(live, r * state + (1.0 - r) * x, x))
            put_strided(directs, row, seqs, stride, jnp.where(live, (1.0 - r) * g, g))
            reached = jnp.where(live, f * adjoint, adjoint)
            return (
                reached,
                ft * peep_f + rt * peep_r,
                prior,
                previous,
                pf + ft * previous,
                pr + rt * previous,
                bf + ft,
                br + rt,
            )

        zero = jnp.zeros((seqs, step), f32)
        last = token(cand, span - 1 + PAD)
        done = lax.fori_loop(
            0, span, backward, (after, zero, end, last, zero, zero, zero, zero), unroll=8
        )
        ends_kept[:, units] = token_of(gcs, span - 1 + PAD)
        for i in range(4):
            sums[i : i + 1, units] = jnp.sum(done[4 + i], axis=0, keepdims=True)
        for n in range(seqs):
            at = n * stride + PAD
            k, j = n // per, n % per
            to = k * (per * span + tail) + j * span
            for gate, ref in enumerate((gcs, fts, rts)):
                here = slice(gate * width + low, gate * width + low + step)
                grads[to : to + span, here] = get_rows(ref, at, span).astype(bf16)
            moved[k][0, j, :, units] = get_rows(outs, at, span).astype(bf16)
            moved[k][1, j, :, units] = get_rows(directs, at, span).astype(bf16)


def mend_kernel(dims, grads, ending, kept, later, linked, out):
    per, span, width, ext = dims
    after = later[2]
    upcoming = ending[...] * (linked[0] * after + linked[2]) - linked[1] * after + linked[3]
    value = (kept[...] + upcoming).astype(bf16)
    last = lax.broadcasted_iota(jnp.int32, (16, width), 0) == 15
    for n in range(ending.shape[0]):
        at = n // per * ext + n % per * span + span - 16
        rows = slice(at, at + 16)
        row = jnp.broadcast_to(value[n : n + 1, :].astype(f32), (16, width))
        out[rows, :width] = jnp.where(last, row, grads[rows, :width].astype(f32)).astype(bf16)


def partial_kernel(distances, depth, width, owners, place, normed, grads, *outs):
    for i, distance in enumerate(distances):
        lanes = pl.ds(pl.multiple_of(owners[distance] * depth, min(depth, 128)), depth)
        columns = normed[:, lanes]
        for piece in range(3):
            gate = pl.ds(pl.multiple_of(place[3 + piece] * width, width), width)
            sum_ = lax.dot_general(
                columns, grads[:, gate], (((0,), (0,)), ((), ())), preferred_element_type=f32
            )
            here = slice(piece * width, (piece + 1) * width)
            split = len(outs) // len(distances)
            count = depth // split
            for n in range(split):
                outs[split * i + n][:, here] = sum_[n * count : (n + 1) * count].astype(outs[0].dtype)


def token_kernel(dims, parts, sources, place, grads, gate_sums, *refs):
    slots, blocks, depth, rows, width, split, tail = dims
    flat = sum(len(slot) for slot in parts)
    n_w = blocks + (1 if split else 0)
    pieces = refs[n_w : n_w + flat]
    means, scales, own = refs[n_w + flat : n_w + flat + 3]
    others = refs[n_w + flat + 3 : n_w + flat + slots + 2]
    sums = refs[n_w + flat + slots + 2]
    first_of = [sum(len(slot) for slot in parts[:k]) for k in range(slots)]

    def raw(k, lanes):
        found = [
            pieces[first_of[k] + i][: min(high, rows) - low, lanes]
            for i, (low, high) in enumerate(parts[k])
        ]
        return found[0] if len(found) == 1 else jnp.concatenate(found, axis=0)

    def block(b):
        return joined(refs[b : b + 2] if split and b == blocks - 1 else refs[b : b + 1])

    sums[...] = jnp.zeros_like(sums)
    sums[:4, pl.ds(pl.multiple_of(place[2], width), width)] = gate_sums[:4, :]
    for b in range(blocks):
        at = pl.multiple_of(sources[b] * depth, depth)
        lanes = pl.ds(at, depth)
        gain_sum, bias_sum = jnp.zeros((8, depth), f32), jnp.zeros((8, depth), f32)
        weights = block(b)
        for k in range(slots):
            here = pl.ds(k * rows, rows)
            total = None
            for piece in range(3):
                gate = pl.ds(pl.multiple_of(place[3 + piece] * width, width), width)
                term = lax.dot_general(
                    grads[k * (rows + tail) : k * (rows + tail) + rows, gate],
                    weights[:, piece * width : (piece + 1) * width],
                    (((1,), (1,)), ((), ())),
                    preferred_element_type=f32,
                )
                total = term if total is None else total + term
            copies = depth // 128
            mean = jnp.concatenate([means[here, :]] * copies, axis=1)
            scale = jnp.concatenate([scales[here, :]] * copies, axis=1)
            scaled = (raw(k, lanes).astype(f32) - mean) * scale
            gain_sum += jnp.sum((total * scaled).reshape(rows // 8, 8, depth), axis=0)
            bias_sum += jnp.sum(total.reshape(rows // 8, 8, depth), axis=0)
            if k == 0:
                own[:, lanes] = total
            else:
                others[k - 1][:, lanes] = total.astype(bf16)
        sums[4:5, lanes] = jnp.sum(gain_sum, axis=0, keepdims=True)
        sums[5:6, lanes] = jnp.sum(bias_sum, axis=0, keepdims=True)


def first_maps(maps):
    one, zero = jnp.ones_like(maps[0]), jnp.zeros_like(maps[0])
    return (maps[0], maps[1], maps[2]), (one, zero), (one, zero, zero)


def joined_maps(known, other, first):
    (decay, inject, handed), before, later = known
    theirs = (other[0], other[1], other[2])
    before_new = (theirs[0] * before[0], before[0] * theirs[1] + before[1])
    later_new = (
        later[0] * theirs[0],
        theirs[0] * later[1] + theirs[1],
        later[2] + later[0] * theirs[2],
    )
    before = tuple(jnp.where(first, a, b) for a, b in zip(before, before_new))
    later = tuple(jnp.where(first, b, a) for a, b in zip(later, later_new))
    inject_new = jnp.where(first, theirs[0] * inject + theirs[1], decay * theirs[1] + inject)
    handed_new = jnp.where(first, handed + decay * theirs[2], theirs[2] + theirs[0] * handed)
    return (decay * theirs[0], inject_new, handed_new), before, later


class Rounds:
    def __init__(self):
        self.before, self.given = [], []

    def take(self, value):
        if not self.before:
            return value
        return lax.optimization_barrier((value, self.before))[0]

    def give(self, *values):
        self.given += values

    def turn(self):
        self.before, self.given = self.given, []


def local(
    inputs,
    start_state,
    lengths,
    weights,
    peep_forget,
    peep_reset,
    bias_forget,
    bias_reset,
    norm_gain,
    norm_bias,
    out_grad,
):
    per, span, model = inputs.shape
    n_seq, slots = lax.axis_size("seq"), lax.axis_size("stream")
    at_seq, at_stream = lax.axis_index("seq"), lax.axis_index("stream")
    seqs = per * slots
    width = model // slots
    depth = model // n_seq
    rows = per * span
    tokens = seqs * span
    tail = 16
    half = depth // 2
    spot = spot_of(at_seq, n_seq)
    far = n_seq // 2
    steps = [0]
    for k in range(1, far):
        steps += [-k, k]
    steps.append(far)
    dealing = slots == 4

    def owner(distance):
        return at_spot(wrapped(spot + distance, n_seq), n_seq)

    def per_stream(table):
        found = table[0]
        for d in range(1, len(table)):
            found = jnp.where(at_stream == d, table[d], found)
        return found

    gates = ((0, 1, 2), (1, 0, 2), (1, 2, 0), (2, 1, 0)) if dealing else ((0, 1, 2),)
    gate_of = [per_stream([table[piece] for table in gates]) for piece in range(3)]
    bits = [1 << b for b in range(slots.bit_length() - 1)]
    seq_bits = [1 << b for b in range(n_seq.bit_length() - 1)]
    share = model // n_seq
    index = {
        "sources": jnp.stack([owner(distance) for distance in steps]).astype(jnp.int32),
        "place": jnp.stack([at_seq * span, at_seq, at_stream * width, *gate_of]).astype(jnp.int32),
        "owners": jnp.stack([owner(distance) for distance in range(n_seq)]).astype(jnp.int32),
        "where": jnp.stack([(at_stream ^ k) * width for k in range(slots)]).astype(jnp.int32),
        "lanes": [(at_stream ^ k) * width for k in range(slots)],
        "rows": [(at_stream ^ k) * per for k in range(slots)],
        "first": [(at_seq & bit) == 0 for bit in seq_bits],
        "even": at_stream % 2 == 0,
        "odd": (at_stream & 1).reshape(1).astype(jnp.int32),
        "share": at_seq * share % width,
        "holds": at_stream == at_seq * share // width,
    }
    index, inputs, weights, out_grad, start_state, lengths = lax.optimization_barrier(
        (index, inputs, weights, out_grad, start_state, lengths)
    )
    sources, place, even = index["sources"], index["place"], index["even"]

    vectors = [
        row.reshape(1, model) for row in (peep_forget, peep_reset, bias_forget, bias_reset)
    ]
    gain_row, bias_row = norm_gain.reshape(1, model), norm_bias.reshape(1, model)
    tall = seqs * (span + PAD)
    fields, two = (jax.ShapeDtypeStruct((n, width // 128, tall, 128), f32) for n in (3, 2))
    space = pltpu.VMEM((min(width, STEP) // 128, tall, 128), f32)

    rounds = Rounds()
    take, give = rounds.take, rounds.give
    box = {}

    def deal():
        if dealing:
            pieces = [weights[:, i * width : (i + 1) * width] for i in range(3)]
            own = jnp.where(even, pieces[0], pieces[2])
            near = swapped(pieces[1], "stream", 1)
            distant = swapped(jnp.where(even, pieces[2], pieces[0]), "stream", 2)
            box["dealt"] = jnp.concatenate([own, near, distant], axis=1)
            give(near, distant)
            return
        everything = lax.all_gather(weights, "stream", axis=1, tiled=True)
        found = [
            lax.dynamic_slice_in_dim(everything, gate * model + at_stream * width, width, 1)
            for gate in range(3)
        ]
        box["dealt"] = jnp.concatenate(found, axis=1)

    def last_columns():
        came = box["came"]
        rest = box["mine", far + 1][0][:, width:] + came[0].astype(f32) + came[1].astype(f32)
        box["rest"] = rest[:, :width], rest[:, width:]
        if dealing:
            near, distant = (part_of.astype(bf16) for part_of in box["rest"])
            box["distant"] = swapped(distant, "stream", 2)
            box["near"] = swapped(near, "stream", 1)
            rounds.before = [*rounds.before, distant, near]

    def stored():
        came = box["came"]
        own = box["mine", far + 1][0][:, :width] + came[2].astype(f32) + came[3].astype(f32)
        if dealing:
            return call(
                functools.partial(stored_kernel, width),
                jax.ShapeDtypeStruct((depth, 3 * width), f32),
                [index["odd"], box["mine", far + 1][0][:, :width], *came[2:], box["near"], box["distant"]],
                scalars=1,
                pinned=False,
            )
        else:
            flat = lax.all_gather(
                jnp.concatenate([own, *box["rest"]], axis=1).astype(bf16), "stream", axis=0
            ).astype(f32)
            flat = jnp.swapaxes(flat.reshape(slots, depth, 3, width), 0, 2)
            flat = jnp.swapaxes(flat, 1, 2).reshape(3 * slots, depth, width)
            found = [
                lax.dynamic_index_in_dim(flat, 3 * at_stream + i, 0, keepdims=False)
                for i in range(3)
            ]
        return jnp.concatenate(found, axis=1)

    def gather(step):
        if step == 1:
            box["up"] = box["down"] = take(box["dealt"])
            box["blocks"] = [box["dealt"]]
        if step == far:
            box["up"], box["down"] = box["up"][:half], box["down"][half:]
        box["up"] = along_ring(take(box["up"]), 1)
        box["down"] = along_ring(take(box["down"]), -1)
        box["blocks"] += [box["up"], box["down"]]
        give(box["up"], box["down"])

    def partials(distances, kind, split=1):
        grads = take(box["grads"])
        if depth % 128:
            found = []
            for distance in distances:
                at = owner(distance)
                sum_ = lax.dot_general(
                    lax.dynamic_slice_in_dim(box["normed"], at * depth, depth, 1),
                    grads,
                    (((0,), (0,)), ((), ())),
                    preferred_element_type=f32,
                ).astype(kind)
                found += [sum_[n * depth // split :][: depth // split] for n in range(split)]
            return found
        return call(
            functools.partial(
                partial_kernel, [distance % n_seq for distance in distances], depth, width
            ),
            [jax.ShapeDtypeStruct((depth // split, 3 * width), kind)] * (split * len(distances)),
            [index["owners"], place, box["normed"], grads],
            scalars=2,
        )

    def scatter(step):
        cuts_of = [(width, 3 * width), (0, width)] if step == far else [(0, 3 * width)]
        if step == 1:
            sent = box["farthest"]
        else:
            sent = call(
                functools.partial(merge_kernel, cuts_of),
                [jax.ShapeDtypeStruct((depth, b - a), bf16) for a, b in cuts_of for _ in range(2)],
                [*box["mine", step], box["up"], box["down"]],
            )
        came = [along_ring(take(value), 1 - 2 * (i % 2)) for i, value in enumerate(sent)]
        rounds.before = [*rounds.before, *sent]
        box["up"], box["down"] = came[:2]
        box["came"] = came
        give(*came)

    def sums_of(step):
        distance = far + 1 - step
        box["mine", step] = partials((distance, -distance) if distance else (0,), f32)
        give(*box["mine", step])

    whole_part = [(0, rows + tail)]
    cuts = [(0, rows // 2), (rows // 2, rows + tail)]
    parts = [whole_part, whole_part, cuts, cuts] if dealing else [whole_part] * slots
    tokens_of = [[None] * len(slot) for slot in parts]
    flat_inputs = inputs.reshape(rows, model)

    def ahead_tokens():
        box["ahead"] = lax.ppermute(
            take(inputs[:, -1, :]), "seq", [(i, i + 1) for i in range(n_seq - 1)]
        )
        give(box["ahead"])

    def own_tokens():
        tokens_of[0][0] = jnp.concatenate(
            [flat_inputs, box["ahead"], jnp.zeros((tail - per, model), bf16)], axis=0
        )

    def everyones_tokens():
        ahead_tokens()
        own_tokens()
        for bit in reversed(bits):
            for k in range(slots):
                if tokens_of[k][0] is not None and tokens_of[k ^ bit][0] is None:
                    tokens_of[k ^ bit][0] = swapped(tokens_of[k][0], "stream", bit)

    def near_tokens():
        own_tokens()
        tokens_of[1][0] = swapped(take(tokens_of[0][0]), "stream", 1)
        give(tokens_of[1][0])

    def far_tokens(i):
        low, high = cuts[i]
        source = flat_inputs[low:high] if high <= rows else tokens_of[0][0][low:high]
        tokens_of[2][i] = swapped(take(source), "stream", 2)
        give(tokens_of[2][i])

    def passed_tokens(i):
        tokens_of[3][i] = swapped(take(tokens_of[2][i]), "stream", 1)
        give(tokens_of[3][i])

    def messages():
        box["messages"] = call(
            functools.partial(message_kernel, slots, width, tail),
            [jax.ShapeDtypeStruct((rows + tail, width), bf16)] * slots,
            [
                index["where"],
                take(out_grad.reshape(rows, model)),
                start_state,
                jnp.broadcast_to(lengths[:, None], (per, 128)),
            ],
            scalars=1,
        )

    def out_grads(behind=()):
        for k in range(slots):
            box["g", k] = box["messages"][k]
            if k:
                message = take(box["g", k])
                if behind:
                    message = lax.optimization_barrier((message, behind[-1]))[0]
                box["g", k] = swapped(message, "stream", k)
                if not behind:
                    give(box["g", k])

    def normalise():
        flat = [piece for slot in tokens_of for piece in slot]
        box["normed"], box["means"], box["scales"], box["picked"] = call(
            functools.partial(norm_kernel, parts, rows, tail, width),
            [
                jax.ShapeDtypeStruct((slots * (rows + tail), model), bf16),
                jax.ShapeDtypeStruct((tokens, 128), f32),
                jax.ShapeDtypeStruct((tokens, 128), f32),
                jax.ShapeDtypeStruct((tokens, width), bf16),
            ],
            [place, *flat, take(gain_row), bias_row],
            scalars=1,
        )
        give(box["normed"])

    def from_others():
        give(*[box["g", k] for k in range(1, slots)])
        extra = [box["g", k][rows : rows + 5 * per].astype(f32) for k in range(slots)]
        extra = [x.reshape(5, per, width) for x in extra]
        box["start"] = jnp.concatenate([x[0] + x[1] + x[2] for x in extra], axis=0)
        ends = jnp.concatenate([x[3] * 256 + x[4] for x in extra], axis=0)
        box["ends"] = ends.astype(jnp.int32)

    def in_order():
        if depth % 128 == 0:
            return box["blocks"], sources, n_seq, depth, True
        deep = 2 * 128
        if "whole" not in box:
            whole = jnp.zeros((model, 3 * width), bf16)
            for b, block in enumerate(box["blocks"]):
                at = owner(steps[min(b, n_seq - 1)]) * depth + (half if b == n_seq else 0)
                whole = lax.dynamic_update_slice_in_dim(whole, block, at, 0)
            box["whole"] = [whole[i : i + deep] for i in range(0, model, deep)]
        count = model // deep
        return box["whole"], jnp.arange(count, dtype=jnp.int32), count, deep, False

    def begin():
        held, places, count, deep, _ = in_order()
        box["begun"] = call(
            functools.partial(begin_kernel, count - 1, deep, rows + tail, slots),
            jax.ShapeDtypeStruct((slots * (rows + tail), 3 * width), f32),
            [places, take(box["normed"]), *held[: count - 1]],
            scalars=1,
        )
        give(box["begun"])

    def first():
        held, places, count, deep, split = in_order()
        *box["fields"], maps, planes = call(
            functools.partial(
                first_kernel, (seqs, span, width, slots, count, deep, 2 if split else 1, tail)
            ),
            [
                fields,
                two,
                two,
                jax.ShapeDtypeStruct((3, seqs, width), f32),
                jax.ShapeDtypeStruct((4, seqs, width), f32),
            ],
            [
                places,
                place,
                box["normed"],
                box["start"],
                take(box["ends"]),
                *vectors,
                box["picked"],
                box["begun"],
                *held[count - 1 :],
                *[box["g", k] for k in range(slots)],
            ],
            scalars=2,
        )
        box["linked"] = lax.ppermute(planes, "seq", [(i + 1, i) for i in range(n_seq - 1)])
        box["known"], box["maps"] = first_maps(maps), maps
        join(1)

    def join(bit):
        mine = box["maps"] if bit == 1 else take(jnp.stack(box["known"][0]))
        other = swapped(mine, "seq", bit)
        give(other)
        box["known"] = joined_maps(box["known"], other, index["first"][seq_bits.index(bit)])

    def join_rest():
        bit = 2
        while bit < n_seq:
            join(bit)
            bit *= 2

    def second():
        _, earlier, later = box["known"]
        later = jnp.stack(later)
        out = call(
            functools.partial(second_kernel, (seqs, span, width, slots, tail)),
            [
                jax.ShapeDtypeStruct((slots * (rows + tail), 3 * width), bf16),
                *[jax.ShapeDtypeStruct((2, per, span, width), bf16)] * slots,
                jax.ShapeDtypeStruct((seqs, width), f32),
                jax.ShapeDtypeStruct((8, width), f32),
                jax.ShapeDtypeStruct((seqs, width), f32),
                jax.ShapeDtypeStruct((seqs, width), f32),
            ],
            [
                place,
                take(box["ends"]),
                *vectors[:2],
                jnp.stack(earlier),
                later,
                box["start"],
                *box["fields"],
            ],
            scratch=[space] * 5,
            scalars=1,
        )
        box["grads"], box["moving"] = out[0], out[1 : slots + 1]
        box["final"], box["sums"] = out[slots + 1], out[slots + 2]
        box["grads"] = call(
            functools.partial(mend_kernel, (per, span, width, rows + tail)),
            jax.ShapeDtypeStruct((slots * (rows + tail), 3 * width), bf16),
            [out[0], *out[slots + 3 :], later, box["linked"]],
            aliases={0: 0},
        )
        rounds.before = []
        box["farthest"] = partials((far,), bf16, 2)
        box["grads"] = lax.optimization_barrier((box["grads"], box["farthest"]))[0]

    def moved(among):
        for k in among:
            box["moved", k] = box["moving"][k]
            if k:
                box["moved", k] = swapped(take(box["moving"][k]), "stream", k)
                give(box["moved", k])

    def token_grads():
        held, places, count, deep, split = in_order()
        out = call(
            functools.partial(
                token_kernel, (slots, count, deep, rows, width, split, tail), parts
            ),
            [
                jax.ShapeDtypeStruct((rows, model), f32),
                *[jax.ShapeDtypeStruct((rows, model), bf16)] * (slots - 1),
                jax.ShapeDtypeStruct((8, model), f32),
            ],
            [
                places,
                place,
                take(box["grads"]),
                box["sums"],
                *held,
                *[piece for slot in tokens_of for piece in slot],
                box["means"],
                box["scales"],
            ],
            scalars=2,
        )
        box["kept"] = {k: out[k] for k in range(slots)}
        box["summed"] = out[slots]
        give(out[0])

    def token_sends(bit):
        kept = box["kept"]
        for k in sorted(kept, reverse=True):
            if k & bit:
                got = swapped(take(kept.pop(k).astype(bf16)), "stream", bit)
                kept[k ^ bit] = kept[k ^ bit].astype(f32) + got.astype(f32)
                give(got)

    def token_part(i, count):
        if i == 0:
            box["sending"] = box["kept"].pop(2).astype(bf16)
            box["arrived"] = []
        low, high = rows * i // count // 16 * 16, rows * (i + 1) // count // 16 * 16
        box["arrived"].append(swapped(take(box["sending"][low:high]), "stream", 2))
        give(box["arrived"][i])
        if i + 1 == count:
            box["kept"][0] = box["kept"][0] + jnp.concatenate(box["arrived"], axis=0).astype(f32)

    def sums(axis, bit):
        if "states" not in box:
            mine = jnp.where(index["holds"], cut(box["final"], index["share"], share, 1), 0.0)
            box["states"] = {k: mine[k * per : (k + 1) * per] for k in range(slots)}
        states, summed = box["states"], box["summed"][:6]
        going = [k for k in sorted(states) if k & bit] if axis == "stream" else []
        if going:
            row = jnp.concatenate([states[k] for k in going], axis=1)
            row = jnp.pad(row, ((0, 0), (0, model - row.shape[1])))
            summed = jnp.concatenate([summed, row], axis=0)
        got = swapped(take(summed), axis, bit)
        give(got)
        box["summed"] = box["summed"][:6] + got[:6]
        for i, k in enumerate(going):
            states.pop(k)
            states[k ^ bit] = states[k ^ bit] + got[6:, i * share : (i + 1) * share]

    def assemble():
        box["outputs"], box["direct"] = found = call(
            functools.partial(assemble_kernel, slots, width),
            [jax.ShapeDtypeStruct((per, span, model), bf16)] * 2,
            [index["where"], *[take(box["moved", k]) for k in range(slots)]],
            scalars=1,
            pinned=False,
        )
        give(*found)
        give(*found)

    def finish():
        grad_normed = box["kept"][0]
        source = inputs.astype(f32).reshape(rows, model)
        scale = take(box["scales"])[:rows, :1]
        scaled = (source - box["means"][:rows, :1]) * scale
        grad_scaled = grad_normed * norm_gain
        grad_source = scale * (
            grad_scaled
            - jnp.mean(grad_scaled, axis=1, keepdims=True)
            - scaled * jnp.mean(grad_scaled * scaled, axis=1, keepdims=True)
        )
        box["input_grad"] = (grad_source.reshape(per, span, model) + box["direct"].astype(f32)).astype(bf16)
        give(box["input_grad"])

    part = functools.partial
    if dealing:
        early = [
            [part(far_tokens, 0)],
            [near_tokens, part(far_tokens, 1), part(passed_tokens, 0), messages],
            [part(passed_tokens, 1), part(out_grads, tokens_of[3]), normalise],
        ]
    else:
        early = [[everyones_tokens], [messages], [out_grads, normalise]]
    early.append([from_others] + ([begin] if depth % 128 == 0 else []))
    deal()
    if dealing:
        ahead_tokens()
    rounds.turn()
    for step in range(1, far + 1):
        gather(step)
        for other in early[step - 1] if step <= len(early) else ():
            other()
        rounds.turn()
    if depth % 128:
        begin()
    first()
    rounds.turn()
    join_rest()
    rounds.turn()
    second()
    late = [
        [part(moved, range(slots)[:3])],
        [part(moved, range(slots)[3:]), token_grads],
        [part(token_sends, 1)]
        + [part(sums, "stream", bit) for bit in bits]
        + [part(sums, "seq", 1)],
        [part(sums, "seq", 2)],
    ]
    for step in range(2, far + 2):
        late_at = step - 2 if far > 4 or step < 3 else min(step - 3, 1)
        while len(late) <= late_at:
            late.append([])
        late[late_at].insert(0, part(sums_of, step))
    if dealing:
        late[2].append(part(token_part, 0, 2))
        late[3].insert(0, part(token_part, 1, 2))
    else:
        late[3] += [part(token_sends, bit) for bit in bits[1:]]
    late[2].append(assemble)
    late += [[] for _ in range(far - len(late))]
    late[far - 1].insert(1, last_columns)
    for step in range(1, far + 1):
        scatter(step)
        for other in late[step - 1] if step <= len(late) else ():
            other()
        rounds.turn()
    weight_grad = stored()
    finish()
    for bit in seq_bits[2:]:
        sums("seq", bit)

    input_grad = box["input_grad"]
    outputs, final_state, summed = box["outputs"], box["states"][0], box["summed"]

    return (
        outputs,
        final_state,
        input_grad,
        weight_grad,
        summed[0],
        summed[1],
        summed[2],
        summed[3],
        summed[4],
        summed[5],
    )


def solution(mesh):
    return jax.shard_map(
        local,
        mesh=mesh,
        in_specs=(
            P("stream", "seq", None),
            P("stream", None),
            P("stream"),
            P("seq", "stream"),
            P(),
            P(),
            P(),
            P(),
            P(),
            P(),
            P("stream", "seq", None),
        ),
        out_specs=(
            P("stream", "seq", None),
            P("stream", "seq"),
            P("stream", "seq", None),
            P("seq", "stream"),
            P(),
            P(),
            P(),
            P(),
            P(),
            P(),
        ),
        check_vma=False,
    )
```

```python
import functools

import jax
import jax.numpy as jnp
from jax import lax
from jax.experimental import pallas as pl
from jax.experimental.pallas import tpu as pltpu
from jax.sharding import PartitionSpec as P

epsilon = 1e-05
f32 = jnp.float32
bf16 = jnp.bfloat16
PAD = 8
STEP = 256
ROOM = 5 * 512 * 1024


def vmem_spec():
    return pl.BlockSpec(memory_space=pltpu.VMEM)


def smem_spec():
    return pl.BlockSpec(memory_space=pltpu.SMEM)


def call(kernel, out_shape, operands, scratch=(), scalars=0, pinned=True, aliases=None):
    held = jax.tree.map(lambda out: pltpu.VMEM(out.shape, out.dtype), out_shape)
    return pl.pallas_call(
        kernel,
        out_shape=held if pinned else out_shape,
        in_specs=[smem_spec()] * scalars + [vmem_spec()] * (len(operands) - scalars),
        out_specs=jax.tree.map(lambda _: vmem_spec(), out_shape),
        scratch_shapes=list(scratch),
        input_output_aliases=aliases or {},
        compiler_params=pltpu.CompilerParams(vmem_limit_bytes=lax.axis_size("stream") * ROOM),
        cost_estimate=pl.CostEstimate(flops=0, bytes_accessed=0, transcendentals=0),
    )(
        *operands[:scalars],
        *[pltpu.with_memory_space_constraint(x, pltpu.VMEM) for x in operands[scalars:]],
    )


def at_spot(spot, count):
    if count != 8:
        return spot
    return spot * 2 if isinstance(spot, int) and spot < 4 else (
        15 - spot * 2 if isinstance(spot, int) else jnp.where(spot < 4, spot * 2, 15 - spot * 2)
    )


def spot_of(index, count):
    if count != 8:
        return index
    return jnp.where(index % 2 == 0, index // 2, (15 - index) // 2)


def wrapped(value, count):
    value = jnp.where(value >= count, value - count, value)
    return jnp.where(value < 0, value + count, value)


def along_ring(value, steps):
    count = lax.axis_size("seq")
    order = [at_spot(i, count) for i in range(count)]
    return lax.ppermute(value, "seq", [(order[i], order[(i + steps) % count]) for i in range(count)])


def cut(array, start, size, axis):
    starts = [jnp.int32(0)] * array.ndim
    sizes = list(array.shape)
    starts[axis], sizes[axis] = start, size
    return lax.dynamic_slice(array, starts, sizes, allow_negative_indices=False)


def pasted(array, piece, start, axis):
    starts = [jnp.int32(0)] * array.ndim
    starts[axis] = start
    return lax.dynamic_update_slice(array, piece, starts, allow_negative_indices=False)


def swapped(value, axis, bit):
    return lax.ppermute(value, axis, [(i, i ^ bit) for i in range(lax.axis_size(axis))])


def norm_kernel(parts, rows, tail, units, place, *refs):
    flat = sum(len(slot) for slot in parts)
    pieces = refs[:flat]
    gain, bias, normed, means, scales, picked = refs[flat:]
    gain_row, bias_row = gain[...], bias[...]
    lanes = pl.ds(pl.multiple_of(place[2], units), units)
    at = 0
    for k, slot in enumerate(parts):
        for low, high in slot:
            x = pieces[at][...].astype(f32)
            mean = jnp.mean(x, axis=1, keepdims=True)
            centered = x - mean
            scale = lax.rsqrt(jnp.mean(centered * centered, axis=1, keepdims=True) + epsilon)
            base = k * (rows + tail)
            normed[base + low : base + high, :] = (centered * scale * gain_row + bias_row).astype(bf16)
            count = min(high, rows) - low
            here = slice(k * rows + low, k * rows + low + count)
            means[here, :] = jnp.broadcast_to(mean[:count], (count, 128))
            scales[here, :] = jnp.broadcast_to(scale[:count], (count, 128))
            picked[here, :] = pieces[at][:count, lanes]
            at += 1


def strided(ref, row, seqs, stride, low=0, count=None):
    count = ref.shape[0] if count is None else count
    tiles = [ref[low + lane, pl.ds(row, seqs, stride=stride), :] for lane in range(count)]
    return jnp.concatenate(tiles, axis=1)


def put_strided(ref, row, seqs, stride, value, low=0):
    for lane in range(value.shape[1] // 128):
        ref[low + lane, pl.ds(row, seqs, stride=stride), :] = value[:, lane * 128 : (lane + 1) * 128]


def put_rows(ref, row, count, value, low=0):
    for lane in range(value.shape[1] // 128):
        ref[low + lane, pl.ds(row, count), :] = value[:, lane * 128 : (lane + 1) * 128]


def get_rows(ref, row, count):
    return jnp.concatenate([ref[lane, pl.ds(row, count), :] for lane in range(ref.shape[0])], axis=1)


def message_kernel(slots, units, tail, where, grads, start, lengths, *outs):
    rows, per = grads.shape[0], start.shape[0]
    for k in range(slots):
        lanes = pl.ds(pl.multiple_of(where[k], units), units)
        outs[k][:rows, :] = grads[:, lanes]
        left = start[:, lanes]
        extra = []
        for _ in range(3):
            part = left.astype(bf16).astype(f32)
            extra.append(part)
            left = left - part
        counts = lengths[...]
        high = counts // 256
        extra += [
            jnp.broadcast_to(n.astype(f32)[:, :1], (per, units)) for n in (high, counts - high * 256)
        ]
        extra.append(jnp.zeros((tail - 5 * per, units), f32))
        outs[k][rows:, :] = jnp.concatenate(extra, axis=0).astype(bf16)


def merge_kernel(cuts, mine_up, mine_down, up, down, *outs):
    count, total = up.shape[0], mine_up.shape[0]
    first, last = slice(0, count), slice(total - count, total)
    for n, (low, high) in enumerate(cuts):
        lanes = slice(low, high)
        out_up, out_down = outs[2 * n], outs[2 * n + 1]
        out_up[first, :] = (mine_up[first, lanes] + up[:, lanes].astype(f32)).astype(bf16)
        out_down[last, :] = (mine_down[last, lanes] + down[:, lanes].astype(f32)).astype(bf16)
        if count < total:
            out_up[count:, :] = mine_up[count:, lanes].astype(bf16)
            out_down[: total - count, :] = mine_down[: total - count, lanes].astype(bf16)


def stored_kernel(width, place, mine, up, down, near, distant, out):
    own = mine[...] + up[...].astype(f32) + down[...].astype(f32)
    shift = place[0] * 2 * width
    out[:, pl.ds(pl.multiple_of(shift, width), width)] = own
    out[:, width : 2 * width] = near[...].astype(f32)
    out[:, pl.ds(pl.multiple_of(2 * width - shift, width), width)] = distant[...].astype(f32)


def assemble_kernel(slots, width, where, *refs):
    for k in range(slots):
        lanes = pl.ds(pl.multiple_of(where[k], width), width)
        for which in range(2):
            refs[slots + which][:, :, lanes] = refs[k][which]


def spread_rows(dims, low, width, g_in, picked, gs, xs):
    seqs, span, slots = dims
    per, lane = seqs // slots, low // 128
    for n in range(seqs):
        to, lanes = n * (span + PAD) + PAD, slice(low, low + width)
        at = n % per * span
        put_rows(gs, to, span, g_in[n // per][at : at + span, lanes].astype(f32), lane)
        put_rows(xs, to, span, picked[n * span : (n + 1) * span, lanes].astype(f32), lane)


def joined(refs):
    return refs[0][...] if len(refs) == 1 else jnp.concatenate([ref[...] for ref in refs], axis=0)


def begin_kernel(blocks, depth, rows, count, sources, normed, *refs):
    total = refs[blocks]
    for k in range(count):
        here = slice(k * rows, (k + 1) * rows)
        sum_ = None
        for b in range(blocks):
            at = pl.multiple_of(sources[b] * depth, depth)
            term = jnp.dot(normed[here, pl.ds(at, depth)], refs[b][...], preferred_element_type=f32)
            sum_ = term if sum_ is None else sum_ + term
        total[here, :] = sum_


def first_kernel(dims, sources, place, normed, start, lens, v0, v1, v2, v3, picked, begun, *refs):
    vecs = (v0, v1, v2, v3)
    seqs, span, width, slots, blocks, depth, late, tail = dims
    stride = span + PAD
    g_in = refs[late : late + slots]
    fields, known, scans, maps, planes = refs[late + slots :]
    cand, forg, rese = (fields.at[i] for i in range(3))
    gs, xs, products, sums = known.at[0], known.at[1], scans.at[0], scans.at[1]
    per = seqs // slots
    rows = per * span
    ext = rows + tail
    at = pl.multiple_of(sources[blocks - 1] * depth, depth)
    lead = joined(refs[:late])
    for k in range(slots):
        here = slice(k * ext, (k + 1) * ext)
        for piece in range(3):
            field = fields.at[place[3 + piece]]
            columns = slice(piece * width, (piece + 1) * width)
            total = begun[here, columns] + jnp.dot(
                normed[here, pl.ds(at, depth)], lead[:, columns], preferred_element_type=f32
            )
            total = total.astype(bf16).astype(f32)
            for j in range(per):
                to = (k * per + j) * stride + PAD
                before = jnp.broadcast_to(total[rows + j : rows + j + 1, :], (8, width))
                put_rows(field, to - 8, 8, before)
                put_rows(field, to, span, total[j * span : (j + 1) * span, :])
    before = jnp.where(place[1] == 0, start[...], strided(cand, PAD - 1, seqs, stride))
    put_strided(cand, PAD - 1, seqs, stride, before)
    ends = lens[...]
    base = place[0]
    step = min(width, STEP)
    ends = ends[:, :step]
    for low in range(0, width, step):
        units = slice(low, low + step)
        lane, lanes = low // 128, step // 128
        spread_rows((seqs, span, slots), low, step, g_in, picked, gs, xs)
        own = pl.ds(pl.multiple_of(place[2] + low, 128), step)
        peep_f, peep_r, bias_f, bias_r = (row[:, own] for row in vecs)

        def turn(t, carry):
            previous, decays, injects, handed = carry
            row = t + PAD
            c, f, r = (strided(ref, row, seqs, stride, lane, lanes) for ref in (cand, forg, rese))
            f = jax.nn.sigmoid(f + peep_f * previous + bias_f)
            r = jax.nn.sigmoid(r + peep_r * previous + bias_r)
            put_strided(forg, row, seqs, stride, f, lane)
            put_strided(rese, row, seqs, stride, r, lane)
            live = base + t < ends
            d = jnp.where(live, f, 1.0)
            inject = jnp.where(live, (1.0 - f) * c, 0.0)
            pulled = jnp.where(live, r * strided(gs, row, seqs, stride, lane, lanes), 0.0)
            decays, injects = decays * d, d * injects + inject
            put_strided(products, row, seqs, stride, decays, lane)
            put_strided(sums, row, seqs, stride, injects, lane)
            return c, decays, injects, handed + decays * pulled

        one, zero = jnp.ones((seqs, step), f32), jnp.zeros((seqs, step), f32)
        put_strided(products, PAD - 1, seqs, stride, one, lane)
        put_strided(sums, PAD - 1, seqs, stride, zero, lane)
        _, decays, injects, handed = lax.fori_loop(
            0, span, turn, (before[:, units], one, zero, zero), unroll=16
        )
        maps[0, :, units], maps[1, :, units], maps[2, :, units] = decays, injects, handed
        c, f, r, g, x = (
            strided(ref, PAD, seqs, stride, lane, lanes) for ref in (cand, forg, rese, gs, xs)
        )
        live = base < ends
        d = jnp.where(live, f, 1.0)
        inject = jnp.where(live, (1.0 - f) * c, 0.0)
        via_adjoint = jnp.where(live, (1.0 - f) * peep_f, 0.0)
        via_state = jnp.where(live, r * (1.0 - r) * g * peep_r, 0.0)
        planes[0, :, units], planes[1, :, units] = via_adjoint, via_adjoint * c
        planes[2, :, units], planes[3, :, units] = via_state * d, via_state * (inject - x)


def second_kernel(
    dims, place, lens, v0, v1, earlier, later, start, fields, known, scans, *refs
):
    vecs = (v0, v1)
    seqs, span, width, slots, tail = dims
    stride = span + PAD
    grads, moved = refs[0], refs[1 : slots + 1]
    final, sums, ending, ends_kept, outs, directs, gcs, fts, rts = refs[slots + 1 :]
    cand, forg, rese = (fields.at[i] for i in range(3))
    gs, xs, products, injected = known.at[0], known.at[1], scans.at[0], scans.at[1]
    per = seqs // slots
    base = place[0]
    step = min(width, STEP)
    ends = lens[:, :step]
    sums[...] = jnp.zeros_like(sums)
    for k in range(slots):
        to = k * (per * span + tail) + per * span
        grads[to : to + tail, :] = jnp.zeros((tail, 3 * width), bf16)
    for low in range(0, width, step):
        units = slice(low, low + step)
        lane, lanes = low // 128, step // 128
        own = pl.ds(pl.multiple_of(place[2] + low, 128), step)
        peep_f, peep_r = (row[:, own] for row in vecs)
        begin = earlier[0, :, units] * start[:, units] + earlier[1, :, units]
        after = later[2, :, units]

        def token(ref, row):
            return strided(ref, row, seqs, stride, lane, lanes)

        def token_of(ref, row):
            return strided(ref, row, seqs, stride)

        def state_at(row):
            return token(products, row) * begin + token(injected, row)

        end = state_at(span - 1 + PAD)
        final[:, units] = later[0, :, units] * end + later[1, :, units]
        ending[:, units] = end

        def backward(i, carry):
            reached, upcoming, state, c, pf, pr, bf, br = carry
            row = span - 1 - i + PAD
            f, r, x, g = (token(ref, row) for ref in (forg, rese, xs, gs))
            prior, previous = state_at(row - 1), token(cand, row - 1)
            live = base + (span - 1 - i) < ends
            zero = jnp.zeros_like(f)
            pulled = r * g
            adjoint = jnp.where(live, pulled, zero) + reached
            kept = jnp.where(live, (1.0 - f) * adjoint, zero)
            ft = f * kept * (prior - c)
            change = r * (state - x)
            rt = jnp.where(live, (1.0 - r) * g * change, zero)
            put_strided(gcs, row, seqs, stride, kept + upcoming)
            put_strided(fts, row, seqs, stride, ft)
            put_strided(rts, row, seqs, stride, rt)
            put_strided(outs, row, seqs, stride, jnp.where(live, r * state + (1.0 - r) * x, x))
            put_strided(directs, row, seqs, stride, jnp.where(live, (1.0 - r) * g, g))
            reached = jnp.where(live, f * adjoint, adjoint)
            return (
                reached,
                ft * peep_f + rt * peep_r,
                prior,
                previous,
                pf + ft * previous,
                pr + rt * previous,
                bf + ft,
                br + rt,
            )

        zero = jnp.zeros((seqs, step), f32)
        last = token(cand, span - 1 + PAD)
        done = lax.fori_loop(
            0, span, backward, (after, zero, end, last, zero, zero, zero, zero), unroll=8
        )
        ends_kept[:, units] = token_of(gcs, span - 1 + PAD)
        for i in range(4):
            sums[i : i + 1, units] = jnp.sum(done[4 + i], axis=0, keepdims=True)
        for n in range(seqs):
            at = n * stride + PAD
            k, j = n // per, n % per
            to = k * (per * span + tail) + j * span
            for gate, ref in enumerate((gcs, fts, rts)):
                here = slice(gate * width + low, gate * width + low + step)
                grads[to : to + span, here] = get_rows(ref, at, span).astype(bf16)
            moved[k][0, j, :, units] = get_rows(outs, at, span).astype(bf16)
            moved[k][1, j, :, units] = get_rows(directs, at, span).astype(bf16)


def mend_kernel(dims, grads, ending, kept, later, linked, out):
    per, span, width, ext = dims
    after = later[2]
    upcoming = ending[...] * (linked[0] * after + linked[2]) - linked[1] * after + linked[3]
    value = (kept[...] + upcoming).astype(bf16)
    last = lax.broadcasted_iota(jnp.int32, (16, width), 0) == 15
    for n in range(ending.shape[0]):
        at = n // per * ext + n % per * span + span - 16
        rows = slice(at, at + 16)
        row = jnp.broadcast_to(value[n : n + 1, :].astype(f32), (16, width))
        out[rows, :width] = jnp.where(last, row, grads[rows, :width].astype(f32)).astype(bf16)


def partial_kernel(distances, depth, width, owners, place, normed, grads, *outs):
    for i, distance in enumerate(distances):
        lanes = pl.ds(pl.multiple_of(owners[distance] * depth, min(depth, 128)), depth)
        columns = normed[:, lanes]
        for piece in range(3):
            gate = pl.ds(pl.multiple_of(place[3 + piece] * width, width), width)
            sum_ = lax.dot_general(
                columns, grads[:, gate], (((0,), (0,)), ((), ())), preferred_element_type=f32
            )
            here = slice(piece * width, (piece + 1) * width)
            split = len(outs) // len(distances)
            count = depth // split
            for n in range(split):
                outs[split * i + n][:, here] = sum_[n * count : (n + 1) * count].astype(outs[0].dtype)


def token_kernel(dims, parts, sources, place, grads, gate_sums, *refs):
    slots, blocks, depth, rows, width, split, tail = dims
    flat = sum(len(slot) for slot in parts)
    n_w = blocks + (1 if split else 0)
    pieces = refs[n_w : n_w + flat]
    means, scales, own = refs[n_w + flat : n_w + flat + 3]
    others = refs[n_w + flat + 3 : n_w + flat + slots + 2]
    sums = refs[n_w + flat + slots + 2]
    first_of = [sum(len(slot) for slot in parts[:k]) for k in range(slots)]

    def raw(k, lanes):
        found = [
            pieces[first_of[k] + i][: min(high, rows) - low, lanes]
            for i, (low, high) in enumerate(parts[k])
        ]
        return found[0] if len(found) == 1 else jnp.concatenate(found, axis=0)

    def block(b):
        return joined(refs[b : b + 2] if split and b == blocks - 1 else refs[b : b + 1])

    sums[...] = jnp.zeros_like(sums)
    sums[:4, pl.ds(pl.multiple_of(place[2], width), width)] = gate_sums[:4, :]
    for b in range(blocks):
        at = pl.multiple_of(sources[b] * depth, depth)
        lanes = pl.ds(at, depth)
        gain_sum, bias_sum = jnp.zeros((8, depth), f32), jnp.zeros((8, depth), f32)
        weights = block(b)
        for k in range(slots):
            here = pl.ds(k * rows, rows)
            total = None
            for piece in range(3):
                gate = pl.ds(pl.multiple_of(place[3 + piece] * width, width), width)
                term = lax.dot_general(
                    grads[k * (rows + tail) : k * (rows + tail) + rows, gate],
                    weights[:, piece * width : (piece + 1) * width],
                    (((1,), (1,)), ((), ())),
                    preferred_element_type=f32,
                )
                total = term if total is None else total + term
            copies = depth // 128
            mean = jnp.concatenate([means[here, :]] * copies, axis=1)
            scale = jnp.concatenate([scales[here, :]] * copies, axis=1)
            scaled = (raw(k, lanes).astype(f32) - mean) * scale
            gain_sum += jnp.sum((total * scaled).reshape(rows // 8, 8, depth), axis=0)
            bias_sum += jnp.sum(total.reshape(rows // 8, 8, depth), axis=0)
            if k == 0:
                own[:, lanes] = total
            else:
                others[k - 1][:, lanes] = total.astype(bf16)
        sums[4:5, lanes] = jnp.sum(gain_sum, axis=0, keepdims=True)
        sums[5:6, lanes] = jnp.sum(bias_sum, axis=0, keepdims=True)


def first_maps(maps):
    one, zero = jnp.ones_like(maps[0]), jnp.zeros_like(maps[0])
    return (maps[0], maps[1], maps[2]), (one, zero), (one, zero, zero)


def joined_maps(known, other, first):
    (decay, inject, handed), before, later = known
    theirs = (other[0], other[1], other[2])
    before_new = (theirs[0] * before[0], before[0] * theirs[1] + before[1])
    later_new = (
        later[0] * theirs[0],
        theirs[0] * later[1] + theirs[1],
        later[2] + later[0] * theirs[2],
    )
    before = tuple(jnp.where(first, a, b) for a, b in zip(before, before_new))
    later = tuple(jnp.where(first, b, a) for a, b in zip(later, later_new))
    inject_new = jnp.where(first, theirs[0] * inject + theirs[1], decay * theirs[1] + inject)
    handed_new = jnp.where(first, handed + decay * theirs[2], theirs[2] + theirs[0] * handed)
    return (decay * theirs[0], inject_new, handed_new), before, later


class Rounds:
    def __init__(self):
        self.before, self.given = [], []

    def take(self, value):
        if not self.before:
            return value
        return lax.optimization_barrier((value, self.before))[0]

    def give(self, *values):
        self.given += values

    def turn(self):
        self.before, self.given = self.given, []


def local(
    inputs,
    start_state,
    lengths,
    weights,
    peep_forget,
    peep_reset,
    bias_forget,
    bias_reset,
    norm_gain,
    norm_bias,
    out_grad,
):
    per, span, model = inputs.shape
    n_seq, slots = lax.axis_size("seq"), lax.axis_size("stream")
    at_seq, at_stream = lax.axis_index("seq"), lax.axis_index("stream")
    seqs = per * slots
    width = model // slots
    depth = model // n_seq
    rows = per * span
    tokens = seqs * span
    tail = 16
    half = depth // 2
    spot = spot_of(at_seq, n_seq)
    far = n_seq // 2
    steps = [0]
    for k in range(1, far):
        steps += [-k, k]
    steps.append(far)
    dealing = slots == 4

    def owner(distance):
        return at_spot(wrapped(spot + distance, n_seq), n_seq)

    def per_stream(table):
        found = table[0]
        for d in range(1, len(table)):
            found = jnp.where(at_stream == d, table[d], found)
        return found

    gates = ((0, 1, 2), (1, 0, 2), (1, 2, 0), (2, 1, 0)) if dealing else ((0, 1, 2),)
    gate_of = [per_stream([table[piece] for table in gates]) for piece in range(3)]
    bits = [1 << b for b in range(slots.bit_length() - 1)]
    seq_bits = [1 << b for b in range(n_seq.bit_length() - 1)]
    share = model // n_seq
    index = {
        "sources": jnp.stack([owner(distance) for distance in steps]).astype(jnp.int32),
        "place": jnp.stack([at_seq * span, at_seq, at_stream * width, *gate_of]).astype(jnp.int32),
        "owners": jnp.stack([owner(distance) for distance in range(n_seq)]).astype(jnp.int32),
        "where": jnp.stack([(at_stream ^ k) * width for k in range(slots)]).astype(jnp.int32),
        "lanes": [(at_stream ^ k) * width for k in range(slots)],
        "rows": [(at_stream ^ k) * per for k in range(slots)],
        "first": [(at_seq & bit) == 0 for bit in seq_bits],
        "even": at_stream % 2 == 0,
        "odd": (at_stream & 1).reshape(1).astype(jnp.int32),
        "share": at_seq * share % width,
        "holds": at_stream == at_seq * share // width,
    }
    index, inputs, weights, out_grad, start_state, lengths = lax.optimization_barrier(
        (index, inputs, weights, out_grad, start_state, lengths)
    )
    sources, place, even = index["sources"], index["place"], index["even"]

    vectors = [
        row.reshape(1, model) for row in (peep_forget, peep_reset, bias_forget, bias_reset)
    ]
    gain_row, bias_row = norm_gain.reshape(1, model), norm_bias.reshape(1, model)
    tall = seqs * (span + PAD)
    fields, two = (jax.ShapeDtypeStruct((n, width // 128, tall, 128), f32) for n in (3, 2))
    space = pltpu.VMEM((min(width, STEP) // 128, tall, 128), f32)

    rounds = Rounds()
    take, give = rounds.take, rounds.give
    box = {}

    def deal():
        if dealing:
            pieces = [weights[:, i * width : (i + 1) * width] for i in range(3)]
            own = jnp.where(even, pieces[0], pieces[2])
            near = swapped(pieces[1], "stream", 1)
            distant = swapped(jnp.where(even, pieces[2], pieces[0]), "stream", 2)
            box["dealt"] = jnp.concatenate([own, near, distant], axis=1)
            give(near, distant)
            return
        everything = lax.all_gather(weights, "stream", axis=1, tiled=True)
        found = [
            lax.dynamic_slice_in_dim(everything, gate * model + at_stream * width, width, 1)
            for gate in range(3)
        ]
        box["dealt"] = jnp.concatenate(found, axis=1)

    def last_columns():
        came = box["came"]
        rest = box["mine", far + 1][0][:, width:] + came[0].astype(f32) + came[1].astype(f32)
        box["rest"] = rest[:, :width], rest[:, width:]
        if dealing:
            near, distant = (part_of.astype(bf16) for part_of in box["rest"])
            box["distant"] = swapped(distant, "stream", 2)
            box["near"] = swapped(near, "stream", 1)
            rounds.before = [*rounds.before, distant, near]

    def stored():
        came = box["came"]
        own = box["mine", far + 1][0][:, :width] + came[2].astype(f32) + came[3].astype(f32)
        if dealing:
            return call(
                functools.partial(stored_kernel, width),
                jax.ShapeDtypeStruct((depth, 3 * width), f32),
                [index["odd"], box["mine", far + 1][0][:, :width], *came[2:], box["near"], box["distant"]],
                scalars=1,
                pinned=False,
            )
        else:
            flat = lax.all_gather(
                jnp.concatenate([own, *box["rest"]], axis=1).astype(bf16), "stream", axis=0
            ).astype(f32)
            flat = jnp.swapaxes(flat.reshape(slots, depth, 3, width), 0, 2)
            flat = jnp.swapaxes(flat, 1, 2).reshape(3 * slots, depth, width)
            found = [
                lax.dynamic_index_in_dim(flat, 3 * at_stream + i, 0, keepdims=False)
                for i in range(3)
            ]
        return jnp.concatenate(found, axis=1)

    def gather(step):
        if step == 1:
            box["up"] = box["down"] = take(box["dealt"])
            box["blocks"] = [box["dealt"]]
        if step == far:
            box["up"], box["down"] = box["up"][:half], box["down"][half:]
        box["up"] = along_ring(take(box["up"]), 1)
        box["down"] = along_ring(take(box["down"]), -1)
        box["blocks"] += [box["up"], box["down"]]
        give(box["up"], box["down"])

    def partials(distances, kind, split=1):
        grads = take(box["grads"])
        if depth % 128:
            found = []
            for distance in distances:
                at = owner(distance)
                sum_ = lax.dot_general(
                    lax.dynamic_slice_in_dim(box["normed"], at * depth, depth, 1),
                    grads,
                    (((0,), (0,)), ((), ())),
                    preferred_element_type=f32,
                ).astype(kind)
                found += [sum_[n * depth // split :][: depth // split] for n in range(split)]
            return found
        return call(
            functools.partial(
                partial_kernel, [distance % n_seq for distance in distances], depth, width
            ),
            [jax.ShapeDtypeStruct((depth // split, 3 * width), kind)] * (split * len(distances)),
            [index["owners"], place, box["normed"], grads],
            scalars=2,
        )

    def scatter(step):
        cuts_of = [(width, 3 * width), (0, width)] if step == far else [(0, 3 * width)]
        if step == 1:
            sent = box["farthest"]
        else:
            sent = call(
                functools.partial(merge_kernel, cuts_of),
                [jax.ShapeDtypeStruct((depth, b - a), bf16) for a, b in cuts_of for _ in range(2)],
                [*box["mine", step], box["up"], box["down"]],
            )
        came = [along_ring(take(value), 1 - 2 * (i % 2)) for i, value in enumerate(sent)]
        rounds.before = [*rounds.before, *sent]
        box["up"], box["down"] = came[:2]
        box["came"] = came
        give(*came)

    def sums_of(step):
        distance = far + 1 - step
        box["mine", step] = partials((distance, -distance) if distance else (0,), f32)
        give(*box["mine", step])

    whole_part = [(0, rows + tail)]
    cuts = [(0, rows // 2), (rows // 2, rows + tail)]
    parts = [whole_part, whole_part, cuts, cuts] if dealing else [whole_part] * slots
    tokens_of = [[None] * len(slot) for slot in parts]
    flat_inputs = inputs.reshape(rows, model)

    def ahead_tokens():
        box["ahead"] = lax.ppermute(
            take(inputs[:, -1, :]), "seq", [(i, i + 1) for i in range(n_seq - 1)]
        )
        give(box["ahead"])

    def own_tokens():
        tokens_of[0][0] = jnp.concatenate(
            [flat_inputs, box["ahead"], jnp.zeros((tail - per, model), bf16)], axis=0
        )

    def everyones_tokens():
        ahead_tokens()
        own_tokens()
        for bit in reversed(bits):
            for k in range(slots):
                if tokens_of[k][0] is not None and tokens_of[k ^ bit][0] is None:
                    tokens_of[k ^ bit][0] = swapped(tokens_of[k][0], "stream", bit)

    def near_tokens():
        own_tokens()
        tokens_of[1][0] = swapped(take(tokens_of[0][0]), "stream", 1)
        give(tokens_of[1][0])

    def far_tokens(i):
        low, high = cuts[i]
        source = flat_inputs[low:high] if high <= rows else tokens_of[0][0][low:high]
        tokens_of[2][i] = swapped(take(source), "stream", 2)
        give(tokens_of[2][i])

    def passed_tokens(i):
        tokens_of[3][i] = swapped(take(tokens_of[2][i]), "stream", 1)
        give(tokens_of[3][i])

    def messages():
        box["messages"] = call(
            functools.partial(message_kernel, slots, width, tail),
            [jax.ShapeDtypeStruct((rows + tail, width), bf16)] * slots,
            [
                index["where"],
                take(out_grad.reshape(rows, model)),
                start_state,
                jnp.broadcast_to(lengths[:, None], (per, 128)),
            ],
            scalars=1,
        )

    def out_grads(behind=()):
        for k in range(slots):
            box["g", k] = box["messages"][k]
            if k:
                message = take(box["g", k])
                if behind:
                    message = lax.optimization_barrier((message, behind[-1]))[0]
                box["g", k] = swapped(message, "stream", k)
                if not behind:
                    give(box["g", k])

    def normalise():
        flat = [piece for slot in tokens_of for piece in slot]
        box["normed"], box["means"], box["scales"], box["picked"] = call(
            functools.partial(norm_kernel, parts, rows, tail, width),
            [
                jax.ShapeDtypeStruct((slots * (rows + tail), model), bf16),
                jax.ShapeDtypeStruct((tokens, 128), f32),
                jax.ShapeDtypeStruct((tokens, 128), f32),
                jax.ShapeDtypeStruct((tokens, width), bf16),
            ],
            [place, *flat, take(gain_row), bias_row],
            scalars=1,
        )
        give(box["normed"])

    def from_others():
        give(*[box["g", k] for k in range(1, slots)])
        extra = [box["g", k][rows : rows + 5 * per].astype(f32) for k in range(slots)]
        extra = [x.reshape(5, per, width) for x in extra]
        box["start"] = jnp.concatenate([x[0] + x[1] + x[2] for x in extra], axis=0)
        ends = jnp.concatenate([x[3] * 256 + x[4] for x in extra], axis=0)
        box["ends"] = ends.astype(jnp.int32)

    def in_order():
        if depth % 128 == 0:
            return box["blocks"], sources, n_seq, depth, True
        deep = 2 * 128
        if "whole" not in box:
            whole = jnp.zeros((model, 3 * width), bf16)
            for b, block in enumerate(box["blocks"]):
                at = owner(steps[min(b, n_seq - 1)]) * depth + (half if b == n_seq else 0)
                whole = lax.dynamic_update_slice_in_dim(whole, block, at, 0)
            box["whole"] = [whole[i : i + deep] for i in range(0, model, deep)]
        count = model // deep
        return box["whole"], jnp.arange(count, dtype=jnp.int32), count, deep, False

    def begin():
        held, places, count, deep, _ = in_order()
        box["begun"] = call(
            functools.partial(begin_kernel, count - 1, deep, rows + tail, slots),
            jax.ShapeDtypeStruct((slots * (rows + tail), 3 * width), f32),
            [places, take(box["normed"]), *held[: count - 1]],
            scalars=1,
        )
        give(box["begun"])

    def first():
        held, places, count, deep, split = in_order()
        *box["fields"], maps, planes = call(
            functools.partial(
                first_kernel, (seqs, span, width, slots, count, deep, 2 if split else 1, tail)
            ),
            [
                fields,
                two,
                two,
                jax.ShapeDtypeStruct((3, seqs, width), f32),
                jax.ShapeDtypeStruct((4, seqs, width), f32),
            ],
            [
                places,
                place,
                box["normed"],
                box["start"],
                take(box["ends"]),
                *vectors,
                box["picked"],
                box["begun"],
                *held[count - 1 :],
                *[box["g", k] for k in range(slots)],
            ],
            scalars=2,
        )
        box["linked"] = lax.ppermute(planes, "seq", [(i + 1, i) for i in range(n_seq - 1)])
        box["known"], box["maps"] = first_maps(maps), maps
        join(1)

    def join(bit):
        mine = box["maps"] if bit == 1 else take(jnp.stack(box["known"][0]))
        other = swapped(mine, "seq", bit)
        give(other)
        box["known"] = joined_maps(box["known"], other, index["first"][seq_bits.index(bit)])

    def join_rest():
        bit = 2
        while bit < n_seq:
            join(bit)
            bit *= 2

    def second():
        _, earlier, later = box["known"]
        later = jnp.stack(later)
        out = call(
            functools.partial(second_kernel, (seqs, span, width, slots, tail)),
            [
                jax.ShapeDtypeStruct((slots * (rows + tail), 3 * width), bf16),
                *[jax.ShapeDtypeStruct((2, per, span, width), bf16)] * slots,
                jax.ShapeDtypeStruct((seqs, width), f32),
                jax.ShapeDtypeStruct((8, width), f32),
                jax.ShapeDtypeStruct((seqs, width), f32),
                jax.ShapeDtypeStruct((seqs, width), f32),
            ],
            [
                place,
                take(box["ends"]),
                *vectors[:2],
                jnp.stack(earlier),
                later,
                box["start"],
                *box["fields"],
            ],
            scratch=[space] * 5,
            scalars=1,
        )
        box["grads"], box["moving"] = out[0], out[1 : slots + 1]
        box["final"], box["sums"] = out[slots + 1], out[slots + 2]
        box["grads"] = call(
            functools.partial(mend_kernel, (per, span, width, rows + tail)),
            jax.ShapeDtypeStruct((slots * (rows + tail), 3 * width), bf16),
            [out[0], *out[slots + 3 :], later, box["linked"]],
            aliases={0: 0},
        )
        rounds.before = []
        box["farthest"] = partials((far,), bf16, 2)
        box["grads"] = lax.optimization_barrier((box["grads"], box["farthest"]))[0]

    def moved(among):
        for k in among:
            box["moved", k] = box["moving"][k]
            if k:
                box["moved", k] = swapped(take(box["moving"][k]), "stream", k)
                give(box["moved", k])

    def token_grads():
        held, places, count, deep, split = in_order()
        out = call(
            functools.partial(
                token_kernel, (slots, count, deep, rows, width, split, tail), parts
            ),
            [
                jax.ShapeDtypeStruct((rows, model), f32),
                *[jax.ShapeDtypeStruct((rows, model), bf16)] * (slots - 1),
                jax.ShapeDtypeStruct((8, model), f32),
            ],
            [
                places,
                place,
                take(box["grads"]),
                box["sums"],
                *held,
                *[piece for slot in tokens_of for piece in slot],
                box["means"],
                box["scales"],
            ],
            scalars=2,
        )
        box["kept"] = {k: out[k] for k in range(slots)}
        box["summed"] = out[slots]
        give(out[0])

    def token_sends(bit):
        kept = box["kept"]
        for k in sorted(kept, reverse=True):
            if k & bit:
                got = swapped(take(kept.pop(k).astype(bf16)), "stream", bit)
                kept[k ^ bit] = kept[k ^ bit].astype(f32) + got.astype(f32)
                give(got)

    def token_part(i, count):
        if i == 0:
            box["sending"] = box["kept"].pop(2).astype(bf16)
            box["arrived"] = []
        low, high = rows * i // count // 16 * 16, rows * (i + 1) // count // 16 * 16
        box["arrived"].append(swapped(take(box["sending"][low:high]), "stream", 2))
        give(box["arrived"][i])
        if i + 1 == count:
            box["kept"][0] = box["kept"][0] + jnp.concatenate(box["arrived"], axis=0).astype(f32)

    def sums(axis, bit):
        if "states" not in box:
            mine = jnp.where(index["holds"], cut(box["final"], index["share"], share, 1), 0.0)
            box["states"] = {k: mine[k * per : (k + 1) * per] for k in range(slots)}
        states, summed = box["states"], box["summed"][:6]
        going = [k for k in sorted(states) if k & bit] if axis == "stream" else []
        if going:
            row = jnp.concatenate([states[k] for k in going], axis=1)
            row = jnp.pad(row, ((0, 0), (0, model - row.shape[1])))
            summed = jnp.concatenate([summed, row], axis=0)
        got = swapped(take(summed), axis, bit)
        give(got)
        box["summed"] = box["summed"][:6] + got[:6]
        for i, k in enumerate(going):
            states.pop(k)
            states[k ^ bit] = states[k ^ bit] + got[6:, i * share : (i + 1) * share]

    def assemble():
        box["outputs"], box["direct"] = found = call(
            functools.partial(assemble_kernel, slots, width),
            [jax.ShapeDtypeStruct((per, span, model), bf16)] * 2,
            [index["where"], *[take(box["moved", k]) for k in range(slots)]],
            scalars=1,
            pinned=False,
        )
        give(*found)
        give(*found)

    def finish():
        grad_normed = box["kept"][0]
        source = inputs.astype(f32).reshape(rows, model)
        scale = take(box["scales"])[:rows, :1]
        scaled = (source - box["means"][:rows, :1]) * scale
        grad_scaled = grad_normed * norm_gain
        grad_source = scale * (
            grad_scaled
            - jnp.mean(grad_scaled, axis=1, keepdims=True)
            - scaled * jnp.mean(grad_scaled * scaled, axis=1, keepdims=True)
        )
        box["input_grad"] = (grad_source.reshape(per, span, model) + box["direct"].astype(f32)).astype(bf16)
        give(box["input_grad"])

    part = functools.partial
    if dealing:
        early = [
            [part(far_tokens, 0)],
            [near_tokens, part(far_tokens, 1), part(passed_tokens, 0), messages],
            [part(passed_tokens, 1), part(out_grads, tokens_of[3]), normalise],
        ]
    else:
        early = [[everyones_tokens], [messages], [out_grads, normalise]]
    early.append([from_others] + ([begin] if depth % 128 == 0 else []))
    deal()
    if dealing:
        ahead_tokens()
    rounds.turn()
    for step in range(1, far + 1):
        gather(step)
        for other in early[step - 1] if step <= len(early) else ():
            other()
        rounds.turn()
    if depth % 128:
        begin()
    first()
    rounds.turn()
    join_rest()
    rounds.turn()
    second()
    late = [
        [part(moved, range(slots)[:3])],
        [part(moved, range(slots)[3:]), token_grads],
        [part(token_sends, 1)]
        + [part(sums, "stream", bit) for bit in bits]
        + [part(sums, "seq", 1)],
        [part(sums, "seq", 2)],
    ]
    for step in range(2, far + 2):
        late_at = step - 2 if far > 4 or step < 3 else min(step - 3, 1)
        while len(late) <= late_at:
            late.append([])
        late[late_at].insert(0, part(sums_of, step))
    if dealing:
        late[2].append(part(token_part, 0, 2))
        late[3].insert(0, part(token_part, 1, 2))
    else:
        late[3] += [part(token_sends, bit) for bit in bits[1:]]
    late[2].append(assemble)
    late += [[] for _ in range(far - len(late))]
    late[far - 1].insert(1, last_columns)
    for step in range(1, far + 1):
        scatter(step)
        for other in late[step - 1] if step <= len(late) else ():
            other()
        rounds.turn()
    weight_grad = stored()
    finish()
    for bit in seq_bits[2:]:
        sums("seq", bit)

    input_grad = box["input_grad"]
    outputs, final_state, summed = box["outputs"], box["states"][0], box["summed"]

    return (
        outputs,
        final_state,
        input_grad,
        weight_grad,
        summed[0],
        summed[1],
        summed[2],
        summed[3],
        summed[4],
        summed[5],
    )


def solution(mesh):
    return jax.shard_map(
        local,
        mesh=mesh,
        in_specs=(
            P("stream", "seq", None),
            P("stream", None),
            P("stream"),
            P("seq", "stream"),
            P(),
            P(),
            P(),
            P(),
            P(),
            P(),
            P("stream", "seq", None),
        ),
        out_specs=(
            P("stream", "seq", None),
            P("stream", "seq"),
            P("stream", "seq", None),
            P("seq", "stream"),
            P(),
            P(),
            P(),
            P(),
            P(),
            P(),
        ),
        check_vma=False,
    )
```
